32 devices in a mesh: fsdp: 2 (over core), ctx: 4 (over z), dp: 4 (over y, x).
Axes of the slice: x: 2, y: 2, z: 4, core: 2. Of those that a mesh axis runs over, the one named last changes fastest.
Arguments:
- query_stream: bfloat16 [1, 512, 8192], P(None, 'ctx', ('fsdp', 'dp')), may hold values from -6 to 6
- key_stream: bfloat16 [1, 512, 8192], P(None, 'ctx', ('fsdp', 'dp')), may hold values from -6 to 6
- value_stream: bfloat16 [1, 512, 8192], P(None, 'ctx', ('fsdp', 'dp')), may hold values from -6 to 6
- document_starts: int32 [1, 512], replicated, may hold values 0 or 1
- medium_taps: bfloat16 [512, 128], P(None, 'fsdp'), may hold values from -0.5 to 0.5
- modal_rate: bfloat16 [512, 16], P('fsdp', 'dp'), may hold values from 3.886223e-05 to 0.032958984
- modal_residue: bfloat16 [512, 16], P('fsdp', 'dp'), may hold values from -4 to 4
- skip_gain: float32 [8192], P(('fsdp', 'dp')), may hold values from 0.5 to 1.5
Outputs:
- hyena_out: bfloat16 [1, 512, 8192], P(None, 'ctx', ('fsdp', 'dp'))
The draws below stay inside these ranges and needn't reach their ends.
All inputs are finite; a program needn't handle non-finite values.
Results may differ from the reference program's by a relative error of at most 0.0085.
Values may be sent and summed in bfloat16 or wider, within the bound.
No kernel may reach another device: no remote copies, remote signals or barrier semaphores. Data moves between devices by JAX's collectives and lax.ppermute only.
A program may use at most 64 MiB of HBM per device.

```python
import math
import jax
import jax.numpy as jnp
from jax import lax

D = 8192
TAPS = 128
ORDER = 16
GROUP_CH = 16
SEGMENTS = 1
SEQ = 512
GROUPS = 512


def touch_ends(entries, stream_key, low, top_value):
    extent = entries.shape
    place = [jax.random.randint(jax.random.fold_in(stream_key, axis), (), 0, extent[axis]) for axis in range(len(extent))]
    entries = entries.at[tuple(place)].set(low)
    longest = extent.index(max(extent))
    place[longest] = (place[longest] + 1) % extent[longest]
    return entries.at[tuple(place)].set(top_value)


def block_scale(rng, dims, shards, least, largest):
    factor_of, own = 1.0, jax.random.fold_in(rng, 6)
    for position, parts in shards:
        draws = jnp.exp(jax.random.uniform(jax.random.fold_in(own, position), (parts,), jnp.float32, least / len(shards), largest / len(shards)))
        factor_of = factor_of * jnp.repeat(draws, dims[position] // parts).reshape([-1 if axis == position else 1 for axis in range(len(dims))])
    return factor_of


def gaussian(rng, dims, width, bound, shards=(), held_as=jnp.bfloat16):
    drawn = width * jax.random.normal(rng, dims, jnp.float32)
    if shards:
        drawn = drawn * block_scale(rng, dims, shards, -0.22, 0.18)
    return jnp.clip(drawn, -bound, bound).astype(held_as)


def setup_inputs(seed: int = 0) -> dict:
    streams_of = jax.random.split(jax.random.key(seed), 9)
    query_stream = gaussian(streams_of[0], (SEGMENTS, SEQ, D), 1.0, 6.0, ((1, 4), (2, 8)))
    key_stream = gaussian(streams_of[1], (SEGMENTS, SEQ, D), 1.0, 6.0, ((1, 4), (2, 8)))
    value_stream = gaussian(streams_of[2], (SEGMENTS, SEQ, D), 1.0, 6.0, ((1, 4), (2, 8)))
    document_starts = touch_ends((jax.random.randint(streams_of[3], (SEGMENTS, SEQ), 0, SEQ // 4) < 1).astype(jnp.int32), jax.random.fold_in(streams_of[3], 1), 0, 1)
    medium_taps = gaussian(streams_of[4], (GROUPS, TAPS), TAPS ** -0.5, 0.5, ((1, 2),))
    modal_rate = jnp.clip(jnp.exp(math.log(0.032958984) - 6.742996 * jax.random.uniform(streams_of[5], (GROUPS, ORDER), jnp.float32) ** block_scale(streams_of[5], (GROUPS, ORDER), ((0, 2), (1, 4)), -0.2, 0.2)), 3.886222839355469e-05, 0.032958984).astype(jnp.bfloat16)
    modal_residue = gaussian(streams_of[6], (GROUPS, ORDER), 1.0, 4.0, ((0, 2), (1, 4)))
    skip_gain = jnp.clip(0.5 + 1.0 * jax.random.uniform(streams_of[7], (D,), jnp.float32) ** block_scale(streams_of[7], (D,), ((0, 8),), -0.2, 0.2), 0.5, 1.5)
    return dict(query_stream=query_stream, key_stream=key_stream, value_stream=value_stream, document_starts=document_starts, medium_taps=medium_taps, modal_rate=modal_rate, modal_residue=modal_residue, skip_gain=skip_gain)


highest = lax.Precision.HIGHEST

def toeplitz_taps(filters, block_len):
    groups = filters.shape[0]
    line = jnp.concatenate([jnp.zeros((groups, 1), filters.dtype), filters[:, ::-1], jnp.zeros((groups, block_len), filters.dtype)], axis=1)
    tiled = jnp.tile(line, (1, block_len))[:, :2 * block_len * block_len]
    return tiled.reshape(groups, block_len, 2 * block_len)

def medium_segment(product, doc_index, medium_taps):
    block_len = TAPS
    block_count = SEQ // block_len
    groups = medium_taps.shape[0]
    channels = product.shape[1] // groups
    matrix = toeplitz_taps(medium_taps.astype(jnp.float32), block_len)
    padded_data = jnp.concatenate([jnp.zeros((block_len, product.shape[1]), jnp.float32), product.astype(jnp.float32)], axis=0)
    padded_docs = jnp.concatenate([jnp.full((block_len,), -1, jnp.int32), doc_index], axis=0)

    def one_block(block_number):
        first_row = block_number * block_len
        window = lax.dynamic_slice_in_dim(padded_data, first_row, 2 * block_len, 0).reshape(2 * block_len, groups, channels)
        window_docs = lax.dynamic_slice_in_dim(padded_docs, first_row, 2 * block_len, 0)
        row_docs = lax.dynamic_slice_in_dim(padded_docs, first_row + block_len, block_len, 0)
        same_doc = row_docs[:, None] == window_docs[None, :]
        masked = jnp.where(same_doc[None], matrix, 0.0)
        result = jnp.einsum('gtj,jgc->tgc', masked, window, precision=highest)
        return result.reshape(block_len, groups * channels)
    outputs = lax.map(one_block, jnp.arange(block_count, dtype=jnp.int32))
    return outputs.reshape(SEQ, groups * channels).astype(jnp.bfloat16)

def modal_blocks(values, doc_index, starts, decay_rate, scaled, carry_state, block_len):
    row_count = values.shape[0]
    block_count = row_count // block_len
    groups = values.shape[1]
    channels = values.shape[2]
    lag_steps = jnp.arange(block_len + 1, dtype=jnp.float32)
    powers = jnp.exp(-decay_rate[:, :, None] * lag_steps)
    kernel = jnp.einsum('gn,gnk->gk', scaled, powers[:, :, :block_len], precision=highest)
    positions = jnp.arange(block_len, dtype=jnp.int32)
    offsets = positions[:, None] - positions[None, :]
    causal = offsets >= 0
    toeplitz = toeplitz_taps(kernel, block_len)[:, :, block_len:]
    carry_weight = scaled[:, None, :] * jnp.transpose(powers[:, :, 1:], (0, 2, 1))
    end_weight = powers[:, :, :block_len][:, :, ::-1]
    full_decay = jnp.transpose(powers[:, :, block_len])

    def advance(state_now, inputs):
        block_values, block_docs, block_starts = inputs
        before = block_docs[0] - block_starts[0]
        continues = block_docs == before
        same_doc = causal & (block_docs[:, None] == block_docs[None, :])
        local_part = jnp.einsum('gts,sgc->tgc', jnp.where(same_doc[None], toeplitz, 0.0), block_values, precision=highest)
        carried = jnp.einsum('gtn,ngc->tgc', jnp.where(continues[None, :, None], carry_weight, 0.0), state_now, precision=highest)
        keep_mask = block_docs == block_docs[block_len - 1]
        emitted = jnp.einsum('gns,sgc->ngc', jnp.where(keep_mask[None, None, :], end_weight, 0.0), block_values, precision=highest)
        factor = jnp.where(continues[block_len - 1], full_decay, 0.0)
        return (factor[:, :, None] * state_now + emitted, local_part + carried)
    final_state, outputs = lax.scan(advance, carry_state, (values.reshape(block_count, block_len, groups, channels), doc_index.reshape(block_count, block_len), starts.reshape(block_count, block_len)))
    return (outputs.reshape(row_count, groups, channels), final_state)

def reference(query_stream, key_stream, value_stream, document_starts, medium_taps, modal_rate, modal_residue, skip_gain):
    decay_rate = modal_rate.astype(jnp.float32)
    mode_count = decay_rate.shape[1]
    scaled = modal_residue.astype(jnp.float32) * jnp.sqrt((1.0 - jnp.exp(-2.0 * decay_rate)) / mode_count)
    results = []
    for segment in range(SEGMENTS):
        product = (key_stream[segment].astype(jnp.float32) * value_stream[segment].astype(jnp.float32)).astype(jnp.bfloat16)
        starts = document_starts[segment].astype(jnp.int32)
        doc_index = jnp.cumsum(starts).astype(jnp.int32)
        medium = medium_segment(product, doc_index, medium_taps)
        gated_values = (query_stream[segment].astype(jnp.float32) * medium.astype(jnp.float32)).astype(jnp.bfloat16)
        values = gated_values.astype(jnp.float32).reshape(SEQ, GROUPS, GROUP_CH)
        zero_state = jnp.zeros((mode_count, GROUPS, GROUP_CH), jnp.float32)
        long_part, final_state = modal_blocks(values, doc_index, starts, decay_rate, scaled, zero_state, TAPS)
        combined = long_part.reshape(SEQ, D) + skip_gain[None, :] * gated_values.astype(jnp.float32)
        results.append(combined.astype(jnp.bfloat16))
    return jnp.stack(results)
```

```python
import functools

import jax
import jax.numpy as jnp
from jax import lax
from jax.experimental import pallas as pl
from jax.experimental.pallas import tpu as pltpu
from jax.sharding import PartitionSpec as P

GROUP_CH = 16
LANES = 128
VMEM_BYTES = 32 * 1024 * 1024


def iota(shape, dim):
    return lax.broadcasted_iota(jnp.int32, shape, dim)


def dot(a, b, contract=((1,), (0,))):
    return lax.dot_general(a, b, (contract, ((), ())), preferred_element_type=jnp.float32)


def prepare_kernel(key_ref, value_ref, rate_ref, residue_ref, product_ref, modal_ref):
    product_ref[...] = (
        key_ref[...].astype(jnp.float32) * value_ref[...].astype(jnp.float32)
    ).astype(jnp.bfloat16)
    rate = rate_ref[...].astype(jnp.float32)
    residue = residue_ref[...].astype(jnp.float32)
    gap = jnp.zeros((8 - rate.shape[0], rate.shape[1]), jnp.float32)
    modal_ref[...] = jnp.concatenate([rate, gap, residue, gap], axis=0).astype(jnp.bfloat16)


def build_kernel(
    dp_size,
    ctx_size,
    place_ref,
    taps_ref,
    other_taps_ref,
    modal_ref,
    *rest,
):
    modal_parts = rest[: dp_size - 1]
    starts_ref, medium_ref, long_ref, end_ref, carry_ref, through_ref, before_ref, rows_ref = rest[
        dp_size - 1 :
    ]
    fsdp_place, ctx_place, dp_place = place_ref[0], place_ref[1], place_ref[2]
    groups, block = medium_ref.shape[0], medium_ref.shape[1]
    width = through_ref.shape[1]
    modes = width // groups
    half = taps_ref.shape[0]

    own = starts_ref[:, pl.ds(pl.multiple_of(ctx_place * block, block), block)].astype(jnp.float32)
    prior_place = jnp.maximum(ctx_place - 1, 0)
    prior = starts_ref[:, pl.ds(pl.multiple_of(prior_place * block, block), block)].astype(
        jnp.float32
    )
    row, col = iota((block, block), 0), iota((block, block), 1)
    doc_col = jnp.sum(
        jnp.where(col <= row, jnp.broadcast_to(own, (block, block)), 0.0), axis=1, keepdims=True
    )
    both = jnp.concatenate(
        [jnp.broadcast_to(own, (8, block)), jnp.broadcast_to(prior, (8, block))], axis=0
    ).astype(jnp.bfloat16)
    doc_row = dot(both, (row <= col).astype(jnp.bfloat16))[0:1]
    after_row = dot(both, (row > col).astype(jnp.bfloat16))[8:9]
    total = jnp.sum(own, axis=1, keepdims=True)
    prior_total = jnp.sum(prior, axis=1, keepdims=True)
    current_mask = (row >= col) & (doc_col == doc_row)
    previous_mask = (col > row) & (doc_col == 0.0) & (after_row == 0.0) & (ctx_place > 0)
    continues = doc_col == 0.0
    keeps = doc_col == total

    pieces = jnp.concatenate([modal_ref[...]] + [part[...] for part in modal_parts], axis=0)
    per_part = modes // dp_size
    lines = pieces.shape[0]
    line, mode = iota((2 * modes, lines), 1), iota((2 * modes, lines), 0)
    within = line % 16
    held = jnp.where(mode < modes, within, within - 8)
    owner = jnp.bitwise_xor(dp_place, line // 16)
    wanted = owner * per_part + held == jnp.where(mode < modes, mode, mode - modes)
    select = ((held >= 0) & (held < per_part) & wanted).astype(jnp.bfloat16)
    ordered = dot(select, pieces).astype(jnp.bfloat16)
    spread = (
        iota((pieces.shape[1], width), 0)
        == dp_place * groups + iota((pieces.shape[1], width), 1) // modes
    ).astype(jnp.bfloat16)
    by_channel = dot(ordered, spread)
    rate = by_channel[:modes]
    scaled = by_channel[modes:] * jnp.sqrt((1.0 - jnp.exp(-2.0 * rate)) / modes)
    through = jnp.exp(-rate * block)
    through_ref[...] = through * (total == 0.0).astype(jnp.float32)
    before_ref[...] = jnp.where(
        ctx_place == ctx_size - 1, through * (prior_total == 0.0).astype(jnp.float32), 1.0
    )
    on_line = iota((modes, width), 0) == iota((modes, width), 1) % modes
    rate_line = jnp.sum(jnp.where(on_line, rate, 0.0), axis=0, keepdims=True)
    scaled_line = jnp.sum(jnp.where(on_line, scaled, 0.0), axis=0, keepdims=True)

    token = iota((block, width), 0).astype(jnp.float32)
    carry_ref[...] = jnp.where(
        continues, scaled_line * jnp.exp(-rate_line * (token + 1.0)), 0.0
    ).astype(jnp.bfloat16)
    end_weight = jnp.where(keeps, jnp.exp(-rate_line * (block - 1.0 - token)), 0.0)
    for slab in range(width // LANES):
        lanes = slice(slab * LANES, (slab + 1) * LANES)
        end_ref[lanes, :] = jnp.transpose(end_weight[:, lanes]).astype(jnp.bfloat16)

    lag = ((block - iota((block, width), 0)) % block).astype(jnp.float32)
    response = scaled_line * jnp.exp(-rate_line * lag)
    high = response.astype(jnp.bfloat16)
    low = (response - high.astype(jnp.float32)).astype(jnp.bfloat16)
    member = (iota((groups, width), 0) == iota((groups, width), 1) // modes).astype(jnp.bfloat16)
    rows_ref[groups:, :] = dot(member, high, ((1,), (1,))) + dot(member, low, ((1,), (1,)))
    first = fsdp_place * dp_size * groups + dp_place * groups
    tap, lane = iota((half, block), 0), iota((half, block), 1)
    lag_of_lane = (block - lane) % block
    own_place = (tap + fsdp_place * half == lag_of_lane).astype(jnp.bfloat16)
    other_place = (tap + (1 - fsdp_place) * half == lag_of_lane).astype(jnp.bfloat16)
    own_rows = (
        iota((taps_ref.shape[1], groups), 0) == first + iota((taps_ref.shape[1], groups), 1)
    ).astype(jnp.bfloat16)
    own_taps = dot(taps_ref[...], own_rows).astype(jnp.bfloat16)
    other_taps = dot(other_taps_ref[...], own_rows).astype(jnp.bfloat16)
    rows_ref[:groups, :] = dot(own_taps, own_place, ((0,), (0,))) + dot(
        other_taps, other_place, ((0,), (0,))
    )

    def lay(group, _):
        medium_row = rows_ref[pl.ds(group, 1), :]
        turned = pltpu.roll(
            jnp.broadcast_to(medium_row, (block, block)), 0, 1, stride=1, stride_axis=0
        )
        medium_ref[group, :, :block] = jnp.where(previous_mask, turned, 0.0).astype(jnp.bfloat16)
        medium_ref[group, :, block:] = jnp.where(current_mask, turned, 0.0).astype(jnp.bfloat16)
        long_row = rows_ref[pl.ds(groups + group, 1), :]
        turned = pltpu.roll(
            jnp.broadcast_to(long_row, (block, block)), 0, 1, stride=1, stride_axis=0
        )
        long_ref[group] = jnp.where(current_mask, turned, 0.0).astype(jnp.bfloat16)
        return 0

    lax.fori_loop(0, groups, lay, 0, unroll=4)


def grouped(matrices, values):
    count, out, rows = matrices.shape
    product = dot(matrices.reshape(count * out, rows), values)
    lane = iota((out, LANES), 1) // GROUP_CH
    result = product[:out]
    for k in range(1, count):
        result = jnp.where(lane == k, product[k * out : (k + 1) * out], result)
    return result


def gate_kernel(halo_ref, product_ref, query_ref, medium_ref, end_ref, gated_ref, state_ref):
    width = product_ref.shape[1]
    modes = state_ref.shape[0]
    per_slab = LANES // GROUP_CH
    diagonal = iota((LANES, LANES), 0) // modes == iota((LANES, LANES), 1) // GROUP_CH
    for slab in range(width // LANES):
        lanes = slice(slab * LANES, (slab + 1) * LANES)
        window = jnp.concatenate([halo_ref[:, lanes], product_ref[:, lanes]], axis=0)
        medium = grouped(medium_ref[slab * per_slab : (slab + 1) * per_slab], window)
        gated = (
            query_ref[:, lanes].astype(jnp.float32)
            * medium.astype(jnp.bfloat16).astype(jnp.float32)
        ).astype(jnp.bfloat16)
        gated_ref[:, lanes] = gated
        spread = jnp.where(diagonal, dot(end_ref[lanes, :], gated), 0.0)
        state_ref[:, lanes] = jnp.sum(spread.reshape(per_slab, modes, LANES), axis=0).astype(
            state_ref.dtype
        )


def local_kernel(gated_ref, long_ref, gain_ref, part_ref):
    width = gated_ref.shape[1]
    per_slab = LANES // GROUP_CH
    for slab in range(width // LANES):
        lanes = slice(slab * LANES, (slab + 1) * LANES)
        gated = gated_ref[:, lanes]
        part_ref[:, lanes] = grouped(
            long_ref[slab * per_slab : (slab + 1) * per_slab], gated
        ) + gain_ref[:, lanes] * gated.astype(jnp.float32)


def finish_kernel(part_ref, carry_ref, near_ref, far_ref, before_ref, out_ref):
    width = part_ref.shape[1]
    modes = near_ref.shape[0]
    per_slab = LANES // GROUP_CH
    diagonal = iota((LANES, LANES), 0) // modes == iota((LANES, LANES), 1) // GROUP_CH
    entering = near_ref[...].astype(jnp.float32) + before_ref[...] * far_ref[...].astype(
        jnp.float32
    )
    for slab in range(width // LANES):
        lanes = slice(slab * LANES, (slab + 1) * LANES)
        state = jnp.concatenate([entering[:, lanes]] * per_slab, axis=0)
        spread = jnp.where(diagonal, state, 0.0).astype(jnp.bfloat16)
        out_ref[:, lanes] = (part_ref[:, lanes] + dot(carry_ref[:, lanes], spread)).astype(
            out_ref.dtype
        )


def call(kernel, outs, *args, scalars=0, scratch=()):
    specs = [pl.BlockSpec(memory_space=pltpu.SMEM)] * scalars + [
        pl.BlockSpec(memory_space=pltpu.VMEM)
    ] * (len(args) - scalars)
    return pl.pallas_call(
        kernel,
        out_shape=[jax.ShapeDtypeStruct(shape, dtype) for shape, dtype in outs],
        in_specs=specs,
        out_specs=[pl.BlockSpec(memory_space=pltpu.VMEM)] * len(outs),
        scratch_shapes=list(scratch),
        compiler_params=pltpu.CompilerParams(vmem_limit_bytes=VMEM_BYTES),
    )(*args)


def shifted(array, axis, distance):
    size = lax.axis_size(axis)
    return lax.ppermute(array, axis, [(i, i + distance) for i in range(size - distance)])


def entering_states(state, through, before):
    size = lax.axis_size("ctx")
    if size == 4:
        near = lax.ppermute(state, "ctx", [(0, 1), (2, 3)])
        both = (state.astype(jnp.float32) + through * near.astype(jnp.float32)).astype(state.dtype)
        far = lax.ppermute(both, "ctx", [(1, 2)]) + lax.ppermute(both, "ctx", [(1, 3)])
        return near, far
    total, factor, distance = state.astype(jnp.float32), through, 1
    while distance < size:
        total = total + factor * shifted(total, "ctx", distance)
        factor = factor * shifted(factor, "ctx", distance)
        distance *= 2
    near = shifted(total, "ctx", 1)
    return near, jnp.zeros_like(near)


def body(
    query_stream,
    key_stream,
    value_stream,
    document_starts,
    medium_taps,
    modal_rate,
    modal_residue,
    skip_gain,
):
    tokens, width = query_stream.shape[1:]
    groups = width // GROUP_CH
    fsdp_size, dp_size = lax.axis_size("fsdp"), lax.axis_size("dp")
    ctx_size = lax.axis_size("ctx")
    modes = modal_rate.shape[1] * dp_size
    assert fsdp_size == 2 and tokens == medium_taps.shape[1] * fsdp_size
    assert modes == GROUP_CH and modal_rate.shape[1] <= 8
    place = jnp.stack([lax.axis_index("fsdp"), lax.axis_index("ctx"), lax.axis_index("dp")])
    taps = medium_taps.T
    half = jnp.bfloat16
    product, modal = call(
        prepare_kernel,
        [((tokens, width), half), ((16, modal_rate.shape[0]), half)],
        key_stream[0],
        value_stream[0],
        modal_rate.T,
        modal_residue.T,
    )
    halo = shifted(product, "ctx", 1)
    other_taps = lax.ppermute(taps, "fsdp", [(0, 1), (1, 0)])
    modal_parts = [
        lax.ppermute(modal, "dp", [(i, i ^ k) for i in range(dp_size)]) for k in range(1, dp_size)
    ]
    medium, long, end, carry, through, before = call(
        functools.partial(build_kernel, dp_size, ctx_size),
        [
            ((groups, tokens, 2 * tokens), half),
            ((groups, tokens, tokens), half),
            ((width, tokens), half),
            ((tokens, width), half),
            ((modes, width), jnp.float32),
            ((modes, width), jnp.float32),
        ],
        place,
        taps,
        other_taps,
        modal,
        *modal_parts,
        document_starts,
        scalars=1,
        scratch=[pltpu.VMEM((2 * groups, tokens), jnp.float32)],
    )
    gated, state = call(
        gate_kernel,
        [((tokens, width), half), ((modes, width), half)],
        halo,
        product,
        query_stream[0],
        medium,
        end,
    )
    near, far = entering_states(state, through, before)
    (part,) = call(
        local_kernel, [((tokens, width), jnp.float32)], gated, long, skip_gain.reshape(1, width)
    )
    (out,) = call(finish_kernel, [((tokens, width), half)], part, carry, near, far, before)
    return out[None]


def solution(mesh):
    return jax.shard_map(
        body,
        mesh=mesh,
        in_specs=(
            P(None, "ctx", ("fsdp", "dp")),
            P(None, "ctx", ("fsdp", "dp")),
            P(None, "ctx", ("fsdp", "dp")),
            P(),
            P(None, "fsdp"),
            P("fsdp", "dp"),
            P("fsdp", "dp"),
            P(("fsdp", "dp")),
        ),
        out_specs=P(None, "ctx", ("fsdp", "dp")),
        check_vma=False,
    )
```

```python
import functools

import jax
import jax.numpy as jnp
from jax import lax
from jax.experimental import pallas as pl
from jax.experimental.pallas import tpu as pltpu
from jax.sharding import PartitionSpec as P

GROUP_CH = 16
LANES = 128
VMEM_BYTES = 32 * 1024 * 1024


def iota(shape, dim):
    return lax.broadcasted_iota(jnp.int32, shape, dim)


def dot(a, b, contract=((1,), (0,))):
    return lax.dot_general(a, b, (contract, ((), ())), preferred_element_type=jnp.float32)


def prepare_kernel(
    key_hbm,
    value_hbm,
    rate_hbm,
    residue_hbm,
    query_hbm,
    taps_hbm,
    starts_hbm,
    gain_hbm,
    product_ref,
    modal_ref,
    query_ref,
    taps_ref,
    starts_ref,
    gain_ref,
    key_ref,
    value_ref,
    rate_ref,
    residue_ref,
    arrived,
):
    pairs = (
        (key_hbm, key_ref),
        (value_hbm, value_ref),
        (rate_hbm, rate_ref),
        (residue_hbm, residue_ref),
        (query_hbm, query_ref),
        (taps_hbm, taps_ref),
        (starts_hbm, starts_ref),
        (gain_hbm, gain_ref),
    )
    copies = [
        pltpu.make_async_copy(source, target, arrived.at[i])
        for i, (source, target) in enumerate(pairs)
    ]
    for copy in copies:
        copy.start()
    for copy in copies[:4]:
        copy.wait()
    product_ref[...] = (
        key_ref[...].astype(jnp.float32) * value_ref[...].astype(jnp.float32)
    ).astype(jnp.bfloat16)
    rate = rate_ref[...].astype(jnp.float32)
    residue = residue_ref[...].astype(jnp.float32)
    gap = jnp.zeros((8 - rate.shape[0], rate.shape[1]), jnp.float32)
    modal_ref[...] = jnp.concatenate([rate, gap, residue, gap], axis=0).astype(jnp.bfloat16)
    for copy in copies[4:]:
        copy.wait()


def block_starts(starts_ref, ctx_place, block):
    prior_place = jnp.maximum(ctx_place - 1, 0)
    return [
        starts_ref[:, pl.ds(pl.multiple_of(place * block, block), block)].astype(jnp.float32)
        for place in (ctx_place, prior_place)
    ]


def document_masks(own, prior, block):
    row, col = iota((block, block), 0), iota((block, block), 1)
    doc_col = jnp.sum(
        jnp.where(col <= row, jnp.broadcast_to(own, (block, block)), 0.0), axis=1, keepdims=True
    )
    both = jnp.concatenate(
        [jnp.broadcast_to(own, (8, block)), jnp.broadcast_to(prior, (8, block))], axis=0
    ).astype(jnp.bfloat16)
    doc_row = dot(both, (row <= col).astype(jnp.bfloat16))[0:1]
    after_row = dot(both, (row > col).astype(jnp.bfloat16))[8:9]
    current = (row >= col) & (doc_col == doc_row)
    previous = (col > row) & (doc_col == 0.0) & (after_row == 0.0)
    return doc_col, current, previous


def circulant(row, block):
    return pltpu.roll(
        jnp.broadcast_to(row, (block, block)), 0, 1, stride=1, stride_axis=0
    ).astype(jnp.bfloat16)


def medium_kernel(
    dp_size, place_ref, taps_ref, other_taps_ref, starts_ref, medium_ref, rows_ref
):
    fsdp_place, ctx_place, dp_place = place_ref[0], place_ref[1], place_ref[2]
    groups, block = medium_ref.shape[0], medium_ref.shape[1]
    half = taps_ref.shape[0]
    own, prior = block_starts(starts_ref, ctx_place, block)
    _, current, previous = document_masks(own, prior, block)
    current = current.astype(jnp.bfloat16)
    previous = (previous & (ctx_place > 0)).astype(jnp.bfloat16)
    first = fsdp_place * dp_size * groups + dp_place * groups
    tap, lane = iota((half, block), 0), iota((half, block), 1)
    lag_of_lane = (block - lane) % block
    own_place = (tap + fsdp_place * half == lag_of_lane).astype(jnp.bfloat16)
    other_place = (tap + (1 - fsdp_place) * half == lag_of_lane).astype(jnp.bfloat16)
    own_rows = (
        iota((taps_ref.shape[1], groups), 0) == first + iota((taps_ref.shape[1], groups), 1)
    ).astype(jnp.bfloat16)
    own_taps = dot(taps_ref[...], own_rows).astype(jnp.bfloat16)
    other_taps = dot(other_taps_ref[...], own_rows).astype(jnp.bfloat16)
    rows_ref[...] = dot(own_taps, own_place, ((0,), (0,))) + dot(
        other_taps, other_place, ((0,), (0,))
    )
    for group in range(groups):
        turned = circulant(rows_ref[group : group + 1, :], block)
        medium_ref[group, :, :block] = turned * previous
        medium_ref[group, :, block:] = turned * current


def modal_kernel(dp_size, ctx_size, place_ref, modal_ref, *rest):
    modal_parts = rest[: dp_size - 1]
    starts_ref, long_ref, end_ref, carry_ref, *factor_refs, rows_ref = rest[dp_size - 1 :]
    through_ref, before_ref = factor_refs
    ctx_place, dp_place = place_ref[1], place_ref[2]
    groups, block = long_ref.shape[0], long_ref.shape[1]
    width = through_ref.shape[1]
    modes = width // groups
    own, prior = block_starts(starts_ref, ctx_place, block)
    doc_col, current, _ = document_masks(own, prior, block)
    current = current.astype(jnp.bfloat16)
    total = jnp.sum(own, axis=1, keepdims=True)
    prior_total = jnp.sum(prior, axis=1, keepdims=True)
    continues = doc_col == 0.0
    keeps = doc_col == total

    pieces = jnp.concatenate([modal_ref[...]] + [part[...] for part in modal_parts], axis=0)
    per_part = modes // dp_size
    lines = pieces.shape[0]
    line, mode = iota((2 * modes, lines), 1), iota((2 * modes, lines), 0)
    within = line % 16
    held = jnp.where(mode < modes, within, within - 8)
    owner = jnp.bitwise_xor(dp_place, line // 16)
    wanted = owner * per_part + held == jnp.where(mode < modes, mode, mode - modes)
    select = ((held >= 0) & (held < per_part) & wanted).astype(jnp.bfloat16)
    ordered = dot(select, pieces).astype(jnp.bfloat16)
    spread = (
        iota((pieces.shape[1], width), 0)
        == dp_place * groups + iota((pieces.shape[1], width), 1) // modes
    ).astype(jnp.bfloat16)
    by_channel = dot(ordered, spread)
    rate = by_channel[:modes]
    scaled = by_channel[modes:] * jnp.sqrt((1.0 - jnp.exp(-2.0 * rate)) / modes)
    through = jnp.exp(-rate * block)
    through_ref[...] = through * (total == 0.0).astype(jnp.float32)
    before_ref[...] = jnp.where(
        ctx_place == ctx_size - 1, through * (prior_total == 0.0).astype(jnp.float32), 1.0
    )
    on_line = iota((modes, width), 0) == iota((modes, width), 1) % modes
    rate_line = jnp.sum(jnp.where(on_line, rate, 0.0), axis=0, keepdims=True)
    scaled_line = jnp.sum(jnp.where(on_line, scaled, 0.0), axis=0, keepdims=True)

    token = iota((block, width), 0).astype(jnp.float32)
    carry_ref[...] = jnp.where(
        continues, scaled_line * jnp.exp(-rate_line * (token + 1.0)), 0.0
    ).astype(jnp.bfloat16)
    end_ref[...] = jnp.where(keeps, jnp.exp(-rate_line * (block - 1.0 - token)), 0.0).astype(
        jnp.bfloat16
    )

    lag = ((block - iota((block, width), 0)) % block).astype(jnp.float32)
    response = scaled_line * jnp.exp(-rate_line * lag)
    high = response.astype(jnp.bfloat16)
    low = (response - high.astype(jnp.float32)).astype(jnp.bfloat16)
    member = (iota((groups, width), 0) == iota((groups, width), 1) // modes).astype(jnp.bfloat16)
    rows_ref[...] = dot(member, high, ((1,), (1,))) + dot(member, low, ((1,), (1,)))
    for group in range(groups):
        long_ref[group] = circulant(rows_ref[group : group + 1, :], block) * current


def grouped(matrices, values):
    count, out, rows = matrices.shape
    product = dot(matrices.reshape(count * out, rows), values)
    lane = iota((out, LANES), 1) // GROUP_CH
    result = product[:out]
    for k in range(1, count):
        result = jnp.where(lane == k, product[k * out : (k + 1) * out], result)
    return result


def gate_kernel(halo_ref, product_ref, query_ref, medium_ref, end_ref, gated_ref, state_ref):
    width = product_ref.shape[1]
    modes = state_ref.shape[0]
    per_slab = LANES // GROUP_CH
    diagonal = iota((LANES, LANES), 0) // modes == iota((LANES, LANES), 1) // GROUP_CH
    slabs = [slice(at, at + LANES) for at in range(0, width, LANES)]
    for slab, lanes in enumerate(slabs):
        window = jnp.concatenate([halo_ref[:, lanes], product_ref[:, lanes]], axis=0)
        medium = grouped(medium_ref[slab * per_slab : (slab + 1) * per_slab], window)
        gated_ref[:, lanes] = (
            query_ref[:, lanes].astype(jnp.float32)
            * medium.astype(jnp.bfloat16).astype(jnp.float32)
        ).astype(jnp.bfloat16)
    for lanes in slabs:
        spread = jnp.where(
            diagonal, dot(end_ref[:, lanes], gated_ref[:, lanes], ((0,), (0,))), 0.0
        )
        state_ref[:, lanes] = jnp.sum(spread.reshape(per_slab, modes, LANES), axis=0).astype(
            state_ref.dtype
        )


def local_kernel(gated_ref, long_ref, gain_ref, part_ref):
    width = gated_ref.shape[1]
    per_slab = LANES // GROUP_CH
    for slab in range(width // LANES):
        lanes = slice(slab * LANES, (slab + 1) * LANES)
        gated = gated_ref[:, lanes]
        part_ref[:, lanes] = grouped(
            long_ref[slab * per_slab : (slab + 1) * per_slab], gated
        ) + gain_ref[:, lanes] * gated.astype(jnp.float32)


def finish_kernel(part_ref, carry_ref, near_ref, far_ref, before_ref, out_ref):
    width = part_ref.shape[1]
    modes = near_ref.shape[0]
    per_slab = LANES // GROUP_CH
    diagonal = iota((LANES, LANES), 0) // modes == iota((LANES, LANES), 1) // GROUP_CH
    entering = near_ref[...].astype(jnp.float32) + before_ref[...] * far_ref[...].astype(
        jnp.float32
    )
    for slab in range(width // LANES):
        lanes = slice(slab * LANES, (slab + 1) * LANES)
        state = jnp.concatenate([entering[:, lanes]] * per_slab, axis=0)
        spread = jnp.where(diagonal, state, 0.0).astype(jnp.bfloat16)
        out_ref[:, lanes] = (part_ref[:, lanes] + dot(carry_ref[:, lanes], spread)).astype(
            out_ref.dtype
        )


def call(kernel, outs, *args, spaces=None, scratch=()):
    spaces = spaces or [pltpu.VMEM] * len(args)
    return pl.pallas_call(
        kernel,
        out_shape=[jax.ShapeDtypeStruct(shape, dtype) for shape, dtype in outs],
        in_specs=[pl.BlockSpec(memory_space=space) for space in spaces],
        out_specs=[pl.BlockSpec(memory_space=pltpu.VMEM)] * len(outs),
        scratch_shapes=list(scratch),
        compiler_params=pltpu.CompilerParams(vmem_limit_bytes=VMEM_BYTES),
    )(*args)


def shifted(array, axis, distance):
    size = lax.axis_size(axis)
    return lax.ppermute(array, axis, [(i, i + distance) for i in range(size - distance)])


def entering_states(state, through, before):
    size = lax.axis_size("ctx")
    if size == 4:
        near = lax.ppermute(state, "ctx", [(0, 1), (2, 3)])
        both = (state.astype(jnp.float32) + through * near.astype(jnp.float32)).astype(state.dtype)
        far = lax.ppermute(both, "ctx", [(1, 2)]) + lax.ppermute(both, "ctx", [(1, 3)])
        return near, far
    total, factor, distance = state.astype(jnp.float32), through, 1
    while distance < size:
        total = total + factor * shifted(total, "ctx", distance)
        factor = factor * shifted(factor, "ctx", distance)
        distance *= 2
    near = shifted(total, "ctx", 1)
    return near, jnp.zeros_like(near)


def body(
    query_stream,
    key_stream,
    value_stream,
    document_starts,
    medium_taps,
    modal_rate,
    modal_residue,
    skip_gain,
):
    tokens, width = query_stream.shape[1:]
    groups = width // GROUP_CH
    fsdp_size, dp_size = lax.axis_size("fsdp"), lax.axis_size("dp")
    ctx_size = lax.axis_size("ctx")
    modes = modal_rate.shape[1] * dp_size
    assert fsdp_size == 2 and tokens == medium_taps.shape[1] * fsdp_size
    assert modes == GROUP_CH and modal_rate.shape[1] <= 8
    place = jnp.stack([lax.axis_index("fsdp"), lax.axis_index("ctx"), lax.axis_index("dp")])
    taps = medium_taps.T
    half = jnp.bfloat16
    rows = modal_rate.shape[0]
    inputs = [
        key_stream[0],
        value_stream[0],
        modal_rate.T,
        modal_residue.T,
        query_stream[0],
        taps,
        document_starts,
        skip_gain.reshape(1, width),
    ]
    product, modal, query, own_taps, starts, gain = call(
        prepare_kernel,
        [((tokens, width), half), ((16, rows), half)] + [(a.shape, a.dtype) for a in inputs[4:]],
        *[pltpu.with_memory_space_constraint(a, pltpu.HBM) for a in inputs],
        spaces=[pltpu.HBM] * len(inputs),
        scratch=[pltpu.VMEM(a.shape, a.dtype) for a in inputs[:4]]
        + [pltpu.SemaphoreType.DMA((len(inputs),))],
    )
    halo = shifted(product, "ctx", 1)
    other_taps = lax.ppermute(taps, "fsdp", [(0, 1), (1, 0)])
    modal_parts = [
        lax.ppermute(modal, "dp", [(i, i ^ k) for i in range(dp_size)]) for k in range(1, dp_size)
    ]
    (medium,) = call(
        functools.partial(medium_kernel, dp_size),
        [((groups, tokens, 2 * tokens), half)],
        place,
        own_taps,
        other_taps,
        starts,
        spaces=[pltpu.SMEM] + [pltpu.VMEM] * 3,
        scratch=[pltpu.VMEM((groups, tokens), jnp.float32)],
    )
    long, end, carry, through, before = call(
        functools.partial(modal_kernel, dp_size, ctx_size),
        [
            ((groups, tokens, tokens), half),
            ((tokens, width), half),
            ((tokens, width), half),
            ((modes, width), jnp.float32),
            ((modes, width), jnp.float32),
        ],
        place,
        modal,
        *modal_parts,
        starts,
        spaces=[pltpu.SMEM] + [pltpu.VMEM] * (dp_size + 1),
        scratch=[pltpu.VMEM((groups, tokens), jnp.float32)],
    )
    gated, state = call(
        gate_kernel,
        [((tokens, width), half), ((modes, width), half)],
        halo,
        product,
        query,
        medium,
        end,
    )
    near, far = entering_states(state, through, before)
    (part,) = call(
        local_kernel, [((tokens, width), jnp.float32)], gated, long, gain
    )
    (out,) = call(finish_kernel, [((tokens, width), half)], part, carry, near, far, before)
    return out[None]


def solution(mesh):
    return jax.shard_map(
        body,
        mesh=mesh,
        in_specs=(
            P(None, "ctx", ("fsdp", "dp")),
            P(None, "ctx", ("fsdp", "dp")),
            P(None, "ctx", ("fsdp", "dp")),
            P(),
            P(None, "fsdp"),
            P("fsdp", "dp"),
            P("fsdp", "dp"),
            P(("fsdp", "dp")),
        ),
        out_specs=P(None, "ctx", ("fsdp", "dp")),
        check_vma=False,
    )
```

```python
import functools

import jax
import jax.numpy as jnp
from jax import lax
from jax.experimental import pallas as pl
from jax.experimental.pallas import tpu as pltpu
from jax.sharding import PartitionSpec as P

GROUP_CH = 16
LANES = 128
VMEM_BYTES = 32 * 1024 * 1024


def iota(shape, dim):
    return lax.broadcasted_iota(jnp.int32, shape, dim)


def dot(a, b, contract=((1,), (0,))):
    return lax.dot_general(a, b, (contract, ((), ())), preferred_element_type=jnp.float32)


def prepare_kernel(
    key_hbm,
    value_hbm,
    rate_hbm,
    residue_hbm,
    query_hbm,
    taps_hbm,
    starts_hbm,
    gain_hbm,
    product_ref,
    modal_ref,
    query_ref,
    taps_ref,
    starts_ref,
    gain_ref,
    key_ref,
    value_ref,
    rate_ref,
    residue_ref,
    arrived,
):
    pairs = (
        (key_hbm, key_ref),
        (value_hbm, value_ref),
        (rate_hbm, rate_ref),
        (residue_hbm, residue_ref),
        (query_hbm, query_ref),
        (taps_hbm, taps_ref),
        (starts_hbm, starts_ref),
        (gain_hbm, gain_ref),
    )
    copies = [
        pltpu.make_async_copy(source, target, arrived.at[i])
        for i, (source, target) in enumerate(pairs)
    ]
    for copy in copies:
        copy.start()
    for copy in copies[:4]:
        copy.wait()
    product_ref[...] = (
        key_ref[...].astype(jnp.float32) * value_ref[...].astype(jnp.float32)
    ).astype(jnp.bfloat16)
    rate = rate_ref[...].astype(jnp.float32)
    residue = residue_ref[...].astype(jnp.float32)
    gap = jnp.zeros((8 - rate.shape[0], rate.shape[1]), jnp.float32)
    modal_ref[...] = jnp.concatenate([rate, gap, residue, gap], axis=0).astype(jnp.bfloat16)
    for copy in copies[4:]:
        copy.wait()


def block_starts(starts_ref, ctx_place, block):
    prior_place = jnp.maximum(ctx_place - 1, 0)
    return [
        starts_ref[:, pl.ds(pl.multiple_of(place * block, block), block)].astype(jnp.float32)
        for place in (ctx_place, prior_place)
    ]


def document_masks(own, prior, block):
    row, col = iota((block, block), 0), iota((block, block), 1)
    both = jnp.concatenate(
        [jnp.broadcast_to(own, (8, block)), jnp.broadcast_to(prior, (8, block))], axis=0
    ).astype(jnp.bfloat16)
    upto = (row <= col).astype(jnp.bfloat16)
    doc_row = dot(both, upto)[0:1]
    after_row = dot(both, (row > col).astype(jnp.bfloat16))[8:9]
    doc_col = dot(
        upto, jnp.broadcast_to(own, (block, block)).astype(jnp.bfloat16), ((0,), (1,))
    )
    current = (row >= col) & (doc_col == doc_row)
    previous = (col > row) & (doc_col == 0.0) & (after_row == 0.0)
    return doc_col, current, previous


def circulant(row, block):
    return pltpu.roll(
        jnp.broadcast_to(row, (block, block)), 0, 1, stride=1, stride_axis=0
    ).astype(jnp.bfloat16)


def medium_kernel(
    taps_ref,
    other_taps_ref,
    starts_ref,
    previous_ref,
    current_ref,
    same_ref,
    doc_ref,
    rows_ref,
):
    fsdp_place, ctx_place, dp_place = (lax.axis_index(axis) for axis in ("fsdp", "ctx", "dp"))
    groups, block = previous_ref.shape[0], previous_ref.shape[1]
    half = taps_ref.shape[0]
    first = (fsdp_place * lax.axis_size("dp") + dp_place) * groups
    base = pl.multiple_of(first // LANES * LANES, LANES)
    tap, lane = iota((half, block), 0), iota((half, block), 1)
    lag_of_lane = (block - lane) % block
    own_place = (tap + fsdp_place * half == lag_of_lane).astype(jnp.bfloat16)
    other_place = (tap + (1 - fsdp_place) * half == lag_of_lane).astype(jnp.bfloat16)
    rows_ref[...] = dot(taps_ref[:, pl.ds(base, LANES)], own_place, ((0,), (0,))) + dot(
        other_taps_ref[:, pl.ds(base, LANES)], other_place, ((0,), (0,))
    )
    own, prior = block_starts(starts_ref, ctx_place, block)
    doc_col, current, previous = document_masks(own, prior, block)
    current = current.astype(jnp.bfloat16)
    previous = (previous & (ctx_place > 0)).astype(jnp.bfloat16)
    same_ref[...] = current
    doc_ref[...] = doc_col
    for group in range(groups):
        turned = circulant(rows_ref[pl.ds(first - base + group, 1), :], block)
        previous_ref[group] = turned * previous
        current_ref[group] = turned * current


def slabs_of(width):
    return [slice(at, at + LANES) for at in range(0, width, LANES)]


def gated_by(query, medium):
    return (
        query.astype(jnp.float32) * medium.astype(jnp.bfloat16).astype(jnp.float32)
    ).astype(jnp.bfloat16)


def end_states(end_ref, gated_ref, state_ref):
    modes, width = state_ref.shape
    per_slab = LANES // GROUP_CH
    diagonal = iota((LANES, LANES), 0) // modes == iota((LANES, LANES), 1) // GROUP_CH
    for lanes in slabs_of(width):
        spread = jnp.where(
            diagonal, dot(end_ref[:, lanes], gated_ref[:, lanes], ((0,), (0,))), 0.0
        )
        state_ref[:, lanes] = jnp.sum(spread.reshape(per_slab, modes, LANES), axis=0).astype(
            state_ref.dtype
        )


def own_kernel(product_ref, query_ref, current_ref, medium_ref, gated_ref):
    per_slab = LANES // GROUP_CH
    for slab, lanes in enumerate(slabs_of(product_ref.shape[1])):
        medium = grouped(
            current_ref[slab * per_slab : (slab + 1) * per_slab], product_ref[:, lanes]
        )
        medium_ref[:, lanes] = medium
        gated_ref[:, lanes] = gated_by(query_ref[:, lanes], medium)


def modal_kernel(
    modal_ref,
    modal_rest_ref,
    starts_ref,
    doc_ref,
    gated_ref,
    end_ref,
    rate_ref,
    scaled_ref,
    through_ref,
    first_ref,
    far_ref,
    state_ref,
):
    ctx_place, dp_place = lax.axis_index("ctx"), lax.axis_index("dp")
    block, width = end_ref.shape
    modes = through_ref.shape[0]
    groups = width // modes
    per_part = modes // lax.axis_size("dp")
    first = dp_place * groups
    base = pl.multiple_of(first // LANES * LANES, LANES)
    pieces = jnp.concatenate(
        [modal_ref[:, pl.ds(base, LANES)], modal_rest_ref[:, pl.ds(base, LANES)]], axis=0
    )
    lines = pieces.shape[0]
    line, mode = iota((2 * modes, lines), 1), iota((2 * modes, lines), 0)
    within = line % 16
    held = jnp.where(mode < modes, within, within - 8)
    owner = jnp.bitwise_xor(dp_place, line // 16)
    wanted = owner * per_part + held == jnp.where(mode < modes, mode, mode - modes)
    select = ((held >= 0) & (held < per_part) & wanted).astype(jnp.bfloat16)
    ordered = dot(select, pieces).astype(jnp.bfloat16)
    spread = (
        iota((LANES, width), 0) == first - base + iota((LANES, width), 1) // modes
    ).astype(jnp.bfloat16)
    by_channel = dot(ordered, spread)
    rate = by_channel[:modes]
    on_line = iota((modes, width), 0) == iota((modes, width), 1) % modes
    rate_line = jnp.sum(jnp.where(on_line, rate, 0.0), axis=0, keepdims=True)
    token = iota((block, LANES), 0).astype(jnp.float32)
    keeps = doc_ref[...] == doc_ref[block - 1 : block, :]
    for lanes in slabs_of(width):
        weight = jnp.exp(-rate_line[:, lanes] * (block - 1.0 - token))
        end_ref[:, lanes] = jnp.where(keeps, weight, 0.0).astype(jnp.bfloat16)
    end_states(end_ref, gated_ref, state_ref)
    scaled = by_channel[modes:] * jnp.sqrt((1.0 - jnp.exp(-2.0 * rate)) / modes)
    rate_ref[...] = rate_line
    scaled_ref[...] = jnp.sum(jnp.where(on_line, scaled, 0.0), axis=0, keepdims=True)
    decay = jnp.exp(-rate * block)
    own, prior = block_starts(starts_ref, ctx_place, block)
    none_own = jnp.sum(own, axis=1, keepdims=True) == 0.0
    none_prior = jnp.sum(prior, axis=1, keepdims=True) == 0.0
    through_ref[...] = jnp.where(none_own, decay, 0.0)
    first_ref[...] = jnp.where(none_own & (ctx_place == 1), decay, 0.0)
    far_ref[...] = jnp.where(none_prior, decay, 0.0)


def long_kernel(rate_ref, scaled_ref, current_ref, doc_ref, long_ref, carry_ref, rows_ref):
    groups, block = long_ref.shape[0], long_ref.shape[1]
    width = carry_ref.shape[1]
    modes = width // groups
    lag = ((block - iota((block, width), 0)) % block).astype(jnp.float32)
    response = scaled_ref[...] * jnp.exp(-rate_ref[...] * lag)
    high = response.astype(jnp.bfloat16)
    low = (response - high.astype(jnp.float32)).astype(jnp.bfloat16)
    member = (iota((groups, width), 0) == iota((groups, width), 1) // modes).astype(jnp.bfloat16)
    rows_ref[...] = dot(member, high, ((1,), (1,))) + dot(member, low, ((1,), (1,)))
    token = iota((block, LANES), 0).astype(jnp.float32)
    continues = doc_ref[...] == 0.0
    for at in range(0, width, LANES):
        lanes = slice(at, at + LANES)
        weight = scaled_ref[:, lanes] * jnp.exp(-rate_ref[:, lanes] * (token + 1.0))
        carry_ref[:, lanes] = jnp.where(continues, weight, 0.0).astype(jnp.bfloat16)
    current = current_ref[...]
    for group in range(groups):
        long_ref[group] = circulant(rows_ref[group : group + 1, :], block) * current


def grouped(matrices, values):
    count, out, rows = matrices.shape
    product = dot(matrices.reshape(count * out, rows), values)
    lane = iota((out, LANES), 1) // GROUP_CH
    result = product[:out]
    for k in range(1, count):
        result = jnp.where(lane == k, product[k * out : (k + 1) * out], result)
    return result


def gate_kernel(
    halo_ref, query_ref, previous_ref, medium_ref, end_ref, _, gated_ref, state_ref
):
    per_slab = LANES // GROUP_CH
    for slab, lanes in enumerate(slabs_of(halo_ref.shape[1])):
        medium = medium_ref[:, lanes] + grouped(
            previous_ref[slab * per_slab : (slab + 1) * per_slab], halo_ref[:, lanes]
        )
        gated_ref[:, lanes] = gated_by(query_ref[:, lanes], medium)
    end_states(end_ref, gated_ref, state_ref)


def local_kernel(gated_ref, long_ref, gain_ref, part_ref):
    width = gated_ref.shape[1]
    per_slab = LANES // GROUP_CH
    for slab in range(width // LANES):
        lanes = slice(slab * LANES, (slab + 1) * LANES)
        gated = gated_ref[:, lanes]
        part_ref[:, lanes] = grouped(
            long_ref[slab * per_slab : (slab + 1) * per_slab], gated
        ) + gain_ref[:, lanes] * gated.astype(jnp.float32)


def finish_kernel(
    four, part_ref, carry_ref, first_ref, near_ref, far_ref, through_ref, out_ref
):
    width = part_ref.shape[1]
    modes = near_ref.shape[0]
    per_slab = LANES // GROUP_CH
    diagonal = iota((LANES, LANES), 0) // modes == iota((LANES, LANES), 1) // GROUP_CH
    entering = near_ref[...].astype(jnp.float32)
    if four:
        place = lax.axis_index("ctx")
        entering += jnp.where(place == 3, through_ref[...] * far_ref[...].astype(jnp.float32), 0.0)
        entering += jnp.where(place == 1, first_ref[...].astype(jnp.float32), 0.0)
    for slab in range(width // LANES):
        lanes = slice(slab * LANES, (slab + 1) * LANES)
        state = jnp.concatenate([entering[:, lanes]] * per_slab, axis=0)
        spread = jnp.where(diagonal, state, 0.0).astype(jnp.bfloat16)
        out_ref[:, lanes] = (part_ref[:, lanes] + dot(carry_ref[:, lanes], spread)).astype(
            out_ref.dtype
        )


def call(kernel, outs, *args, spaces=None, scratch=(), micros=0.3):
    spaces = spaces or [pltpu.VMEM] * len(args)
    return pl.pallas_call(
        kernel,
        out_shape=[jax.ShapeDtypeStruct(shape, dtype) for shape, dtype in outs],
        in_specs=[pl.BlockSpec(memory_space=space) for space in spaces],
        out_specs=[pl.BlockSpec(memory_space=pltpu.VMEM)] * len(outs),
        scratch_shapes=list(scratch),
        cost_estimate=pl.CostEstimate(
            flops=int(micros * 1e9), bytes_accessed=0, transcendentals=0
        ),
        compiler_params=pltpu.CompilerParams(vmem_limit_bytes=VMEM_BYTES),
    )(*args)


def shifted(array, axis, distance):
    size = lax.axis_size(axis)
    return lax.ppermute(array, axis, [(i, i + distance) for i in range(size - distance)])


def exchanged(array, axis, bit):
    return lax.ppermute(array, axis, [(i, i ^ bit) for i in range(lax.axis_size(axis))])


def entering_states(state, through):
    size = lax.axis_size("ctx")
    total, factor, distance = state.astype(jnp.float32), through, 1
    while distance < size:
        total = total + factor * shifted(total, "ctx", distance)
        factor = factor * shifted(factor, "ctx", distance)
        distance *= 2
    return shifted(total, "ctx", 1)


def body(
    query_stream,
    key_stream,
    value_stream,
    document_starts,
    medium_taps,
    modal_rate,
    modal_residue,
    skip_gain,
):
    tokens, width = query_stream.shape[1:]
    groups = width // GROUP_CH
    fsdp_size, dp_size = lax.axis_size("fsdp"), lax.axis_size("dp")
    ctx_size = lax.axis_size("ctx")
    modes = modal_rate.shape[1] * dp_size
    assert fsdp_size == 2 and tokens == medium_taps.shape[1] * fsdp_size
    assert modes == GROUP_CH and modal_rate.shape[1] <= 8
    taps = medium_taps.T
    half = jnp.bfloat16
    rows = modal_rate.shape[0]
    inputs = [
        key_stream[0],
        value_stream[0],
        modal_rate.T,
        modal_residue.T,
        query_stream[0],
        taps,
        document_starts,
        skip_gain.reshape(1, width),
    ]
    product, modal, query, own_taps, starts, gain = call(
        prepare_kernel,
        [((tokens, width), half), ((16, rows), half)] + [(a.shape, a.dtype) for a in inputs[4:]],
        *[pltpu.with_memory_space_constraint(a, pltpu.HBM) for a in inputs],
        spaces=[pltpu.HBM] * len(inputs),
        scratch=[pltpu.VMEM(a.shape, a.dtype) for a in inputs[:4]]
        + [pltpu.SemaphoreType.DMA((len(inputs),))],
    )
    halo = lax.ppermute(product, "ctx", [(i, (i + 1) % ctx_size) for i in range(ctx_size)])
    other_taps = exchanged(taps, "fsdp", 1)
    bit = 1
    while 2 * bit < dp_size:
        modal = jnp.concatenate([modal, exchanged(modal, "dp", bit)], axis=0)
        bit *= 2
    modal_rest = exchanged(modal, "dp", bit)
    square = ((groups, tokens, tokens), half)
    previous, current, same, documents = call(
        medium_kernel,
        [square, square, ((tokens, tokens), half), ((tokens, tokens), jnp.float32)],
        own_taps,
        other_taps,
        starts,
        scratch=[pltpu.VMEM((LANES, tokens), jnp.float32)],
    )
    medium, gated_own = call(
        own_kernel,
        [((tokens, width), jnp.float32), ((tokens, width), half)],
        product,
        query,
        current,
    )
    line, states = ((1, width), jnp.float32), ((modes, width), jnp.float32)
    end, rate, scaled, through, first_through, far_through, state_own = call(
        modal_kernel,
        [((tokens, width), half), line, line, states, states, states, ((modes, width), half)],
        modal,
        modal_rest,
        starts,
        documents,
        gated_own,
    )
    four = ctx_size == 4
    first = exchanged(state_own, "ctx", 1) if four else state_own
    long, carry = call(
        long_kernel,
        [square, ((tokens, width), half)],
        rate,
        scaled,
        same,
        documents,
        scratch=[pltpu.VMEM((groups, tokens), jnp.float32)],
    )
    gated, state = call(
        gate_kernel,
        [((tokens, width), half), ((modes, width), half)],
        halo,
        query,
        previous,
        medium,
        end,
        carry,
    )
    if four:
        both = state.astype(jnp.float32) + first_through * first.astype(jnp.float32)
        both = both.astype(half)
        far = exchanged(both, "ctx", 2)
        near = lax.ppermute(both, "ctx", [(1, 2), (2, 3)])
    else:
        near = far = entering_states(state, through)
    (part,) = call(local_kernel, [((tokens, width), jnp.float32)], gated, long, gain)
    (out,) = call(
        functools.partial(finish_kernel, four),
        [((tokens, width), half)],
        part,
        carry,
        first,
        near,
        far,
        far_through,
    )
    return out[None]


def solution(mesh):
    return jax.shard_map(
        body,
        mesh=mesh,
        in_specs=(
            P(None, "ctx", ("fsdp", "dp")),
            P(None, "ctx", ("fsdp", "dp")),
            P(None, "ctx", ("fsdp", "dp")),
            P(),
            P(None, "fsdp"),
            P("fsdp", "dp"),
            P("fsdp", "dp"),
            P(("fsdp", "dp")),
        ),
        out_specs=P(None, "ctx", ("fsdp", "dp")),
        check_vma=False,
    )
```

```python
import functools

import jax
import jax.numpy as jnp
from jax import lax
from jax.experimental import pallas as pl
from jax.experimental.pallas import tpu as pltpu
from jax.sharding import PartitionSpec as P

GROUP_CH = 16
LANES = 128
VMEM_BYTES = 32 * 1024 * 1024


def iota(shape, dim):
    return lax.broadcasted_iota(jnp.int32, shape, dim)


def dot(a, b, contract=((1,), (0,))):
    return lax.dot_general(a, b, (contract, ((), ())), preferred_element_type=jnp.float32)


def prepare_kernel(
    key_hbm,
    value_hbm,
    rate_hbm,
    residue_hbm,
    query_hbm,
    taps_hbm,
    starts_hbm,
    gain_hbm,
    product_ref,
    modal_ref,
    spread_ref,
    select_ref,
    query_ref,
    taps_ref,
    starts_ref,
    gain_ref,
    key_ref,
    value_ref,
    rate_ref,
    residue_ref,
    arrived,
):
    pairs = (
        (key_hbm, key_ref),
        (value_hbm, value_ref),
        (rate_hbm, rate_ref),
        (residue_hbm, residue_ref),
        (query_hbm, query_ref),
        (taps_hbm, taps_ref),
        (starts_hbm, starts_ref),
        (gain_hbm, gain_ref),
    )
    copies = [
        pltpu.make_async_copy(source, target, arrived.at[i])
        for i, (source, target) in enumerate(pairs)
    ]
    for copy in copies:
        copy.start()
    dp_place = lax.axis_index("dp")
    modes, width = select_ref.shape[0] // 2, spread_ref.shape[1]
    per_part = rate_ref.shape[0]
    lines = select_ref.shape[1]
    line, mode = iota((2 * modes, lines), 1), iota((2 * modes, lines), 0)
    within = line % 16
    held = jnp.where(mode < modes, within, within - 8)
    owner = jnp.bitwise_xor(dp_place, line // 16)
    wanted = owner * per_part + held == jnp.where(mode < modes, mode, mode - modes)
    select_ref[...] = ((held >= 0) & (held < per_part) & wanted).astype(jnp.bfloat16)
    first = dp_place * (width // modes) % LANES
    spread_ref[...] = (
        iota((LANES, width), 0) == first + iota((LANES, width), 1) // modes
    ).astype(jnp.bfloat16)
    for copy in copies[:4]:
        copy.wait()
    product_ref[...] = (
        key_ref[...].astype(jnp.float32) * value_ref[...].astype(jnp.float32)
    ).astype(jnp.bfloat16)
    rate = rate_ref[...].astype(jnp.float32)
    residue = residue_ref[...].astype(jnp.float32)
    gap = jnp.zeros((8 - rate.shape[0], rate.shape[1]), jnp.float32)
    modal_ref[...] = jnp.concatenate([rate, gap, residue, gap], axis=0).astype(jnp.bfloat16)
    for copy in copies[4:]:
        copy.wait()


def block_starts(starts_ref, ctx_place, block):
    prior_place = jnp.maximum(ctx_place - 1, 0)
    return [
        starts_ref[:, pl.ds(pl.multiple_of(place * block, block), block)].astype(jnp.float32)
        for place in (ctx_place, prior_place)
    ]


def document_masks(own, prior, block):
    row, col = iota((block, block), 0), iota((block, block), 1)
    both = jnp.concatenate(
        [jnp.broadcast_to(own, (8, block)), jnp.broadcast_to(prior, (8, block))], axis=0
    ).astype(jnp.bfloat16)
    upto = (row <= col).astype(jnp.bfloat16)
    doc_row = dot(both, upto)[0:1]
    after_row = dot(both, (row > col).astype(jnp.bfloat16))[8:9]
    doc_col = dot(
        upto, jnp.broadcast_to(own, (block, block)).astype(jnp.bfloat16), ((0,), (1,))
    )
    current = (row >= col) & (doc_col == doc_row)
    previous = (col > row) & (doc_col == 0.0) & (after_row == 0.0)
    return doc_col, current, previous


def circulant(row, block):
    return pltpu.roll(
        jnp.broadcast_to(row, (block // 2, block)), 0, 1, stride=1, stride_axis=0
    ).astype(jnp.bfloat16)


def folded(mask, block):
    half = block // 2
    lower = pltpu.roll(mask[half:], half, 1)
    return [mask[:half].astype(jnp.bfloat16), lower.astype(jnp.bfloat16)]


def medium_kernel(
    taps_ref,
    other_taps_ref,
    starts_ref,
    previous_ref,
    current_ref,
    same_ref,
    doc_ref,
    rows_ref,
):
    fsdp_place, ctx_place, dp_place = (lax.axis_index(axis) for axis in ("fsdp", "ctx", "dp"))
    groups, block = previous_ref.shape[0], previous_ref.shape[1]
    half = taps_ref.shape[0]
    first = (fsdp_place * lax.axis_size("dp") + dp_place) * groups
    base = pl.multiple_of(first // LANES * LANES, LANES)
    tap, lane = iota((half, block), 0), iota((half, block), 1)
    lag_of_lane = (block - lane) % block
    own_place = (tap + fsdp_place * half == lag_of_lane).astype(jnp.bfloat16)
    other_place = (tap + (1 - fsdp_place) * half == lag_of_lane).astype(jnp.bfloat16)
    rows_ref[...] = dot(taps_ref[:, pl.ds(base, LANES)], own_place, ((0,), (0,))) + dot(
        other_taps_ref[:, pl.ds(base, LANES)], other_place, ((0,), (0,))
    )
    own, prior = block_starts(starts_ref, ctx_place, block)
    doc_col, current, previous = document_masks(own, prior, block)
    current = folded(current.astype(jnp.float32), block)
    previous = folded((previous & (ctx_place > 0)).astype(jnp.float32), block)
    halves = [slice(0, block // 2), slice(block // 2, block)]
    doc_ref[...] = doc_col
    for part, rows in enumerate(halves):
        same_ref[rows, :] = current[part]
    for group in range(groups):
        turned = circulant(rows_ref[pl.ds(first - base + group, 1), :], block)
        for part, rows in enumerate(halves):
            previous_ref[group, rows, :] = turned * previous[part]
            current_ref[group, rows, :] = turned * current[part]


def slabs_of(width):
    return [slice(at, at + LANES) for at in range(0, width, LANES)]


def gated_by(query, medium):
    return (
        query.astype(jnp.float32) * medium.astype(jnp.bfloat16).astype(jnp.float32)
    ).astype(jnp.bfloat16)


def end_states(end_ref, gated_ref, state_ref):
    modes, width = state_ref.shape
    per_slab = LANES // GROUP_CH
    diagonal = iota((LANES, LANES), 0) // modes == iota((LANES, LANES), 1) // GROUP_CH
    for lanes in slabs_of(width):
        spread = jnp.where(
            diagonal, dot(end_ref[:, lanes], gated_ref[:, lanes], ((0,), (0,))), 0.0
        )
        state_ref[:, lanes] = jnp.sum(spread.reshape(per_slab, modes, LANES), axis=0).astype(
            state_ref.dtype
        )


def own_kernel(product_ref, query_ref, current_ref, medium_ref, gated_ref):
    per_slab = LANES // GROUP_CH
    for slab, lanes in enumerate(slabs_of(product_ref.shape[1])):
        medium = grouped(
            current_ref[slab * per_slab : (slab + 1) * per_slab], product_ref[:, lanes]
        )
        medium_ref[:, lanes] = medium
        gated_ref[:, lanes] = gated_by(query_ref[:, lanes], medium)


def on_line(modes, width):
    return iota((modes, width), 0) == iota((modes, width), 1) % modes


def modal_kernel(
    modal_ref,
    modal_rest_ref,
    select_ref,
    spread_ref,
    doc_ref,
    gated_ref,
    end_ref,
    channels_ref,
    state_ref,
):
    block, width = end_ref.shape
    modes = state_ref.shape[0]
    first = lax.axis_index("dp") * (width // modes)
    base = pl.multiple_of(first // LANES * LANES, LANES)
    pieces = jnp.concatenate(
        [modal_ref[:, pl.ds(base, LANES)], modal_rest_ref[:, pl.ds(base, LANES)]], axis=0
    )
    ordered = dot(select_ref[...], pieces)
    by_channel = dot(ordered.astype(jnp.bfloat16), spread_ref[...])
    channels_ref[...] = by_channel
    rate_line = jnp.sum(
        jnp.where(on_line(modes, width), by_channel[:modes], 0.0), axis=0, keepdims=True
    )
    left = (block - 1 - iota((block, LANES), 0)).astype(jnp.float32)
    keeps = doc_ref[...] == doc_ref[block - 1 : block, :]
    for lanes in slabs_of(width):
        weight = jnp.exp(-rate_line[:, lanes] * left)
        end_ref[:, lanes] = jnp.where(keeps, weight, 0.0).astype(jnp.bfloat16)
    end_states(end_ref, gated_ref, state_ref)


def long_kernel(
    channels_ref,
    starts_ref,
    same_ref,
    doc_ref,
    long_ref,
    carry_ref,
    through_ref,
    first_ref,
    far_ref,
    rows_ref,
):
    groups, block = long_ref.shape[0], long_ref.shape[1]
    modes, width = through_ref.shape
    ctx_place = lax.axis_index("ctx")
    rate = channels_ref[:modes]
    scaled = channels_ref[modes:] * jnp.sqrt((1.0 - jnp.exp(-2.0 * rate)) / modes)
    chosen = on_line(modes, width)
    rate_line = jnp.sum(jnp.where(chosen, rate, 0.0), axis=0, keepdims=True)
    scaled_line = jnp.sum(jnp.where(chosen, scaled, 0.0), axis=0, keepdims=True)
    lag = ((block - iota((block, LANES), 0)) % block).astype(jnp.float32)
    response = jnp.zeros((groups, block), jnp.float32)
    for lanes in slabs_of(width):
        terms = scaled_line[:, lanes] * jnp.exp(-rate_line[:, lanes] * lag)
        high = terms.astype(jnp.bfloat16)
        low = (terms - high.astype(jnp.float32)).astype(jnp.bfloat16)
        member = (
            iota((groups, LANES), 0) == (lanes.start + iota((groups, LANES), 1)) // modes
        ).astype(jnp.bfloat16)
        response += dot(member, high, ((1,), (1,))) + dot(member, low, ((1,), (1,)))
    rows_ref[...] = response
    since = (iota((block, LANES), 0) + 1).astype(jnp.float32)
    continues = doc_ref[...] == 0.0
    for lanes in slabs_of(width):
        weight = scaled_line[:, lanes] * jnp.exp(-rate_line[:, lanes] * since)
        carry_ref[:, lanes] = jnp.where(continues, weight, 0.0).astype(jnp.bfloat16)
    halves = [slice(0, block // 2), slice(block // 2, block)]
    same = [same_ref[rows, :] for rows in halves]
    for group in range(groups):
        turned = circulant(rows_ref[group : group + 1, :], block)
        for part, rows in enumerate(halves):
            long_ref[group, rows, :] = turned * same[part]
    decay = jnp.exp(-rate * block)
    own, prior = block_starts(starts_ref, ctx_place, block)
    none_own = jnp.sum(own, axis=1, keepdims=True) == 0.0
    none_prior = jnp.sum(prior, axis=1, keepdims=True) == 0.0
    through_ref[...] = jnp.where(none_own, decay, 0.0)
    first_ref[...] = jnp.where(none_own & (ctx_place == 1), decay, 0.0)
    far_ref[...] = jnp.where(none_prior, decay, 0.0)


def grouped(matrices, values):
    count, rows, _ = matrices.shape
    half = rows // 2
    lane = iota((half, LANES), 1) // GROUP_CH
    results = []
    for part in range(2):
        turned = values if part == 0 else jnp.concatenate([values[half:], values[:half]], axis=0)
        chosen = matrices[:, part * half : (part + 1) * half].reshape(count * half, rows)
        product = dot(chosen, turned)
        result = product[:half]
        for k in range(1, count):
            result = jnp.where(lane == k, product[k * half : (k + 1) * half], result)
        results.append(result)
    return jnp.concatenate(results, axis=0)


def gate_kernel(
    halo_ref, query_ref, previous_ref, medium_ref, end_ref, _, gated_ref, state_ref
):
    per_slab = LANES // GROUP_CH
    for slab, lanes in enumerate(slabs_of(halo_ref.shape[1])):
        medium = medium_ref[:, lanes] + grouped(
            previous_ref[slab * per_slab : (slab + 1) * per_slab], halo_ref[:, lanes]
        )
        gated_ref[:, lanes] = gated_by(query_ref[:, lanes], medium)
    end_states(end_ref, gated_ref, state_ref)


def local_kernel(gated_ref, long_ref, gain_ref, part_ref):
    width = gated_ref.shape[1]
    per_slab = LANES // GROUP_CH
    for slab in range(width // LANES):
        lanes = slice(slab * LANES, (slab + 1) * LANES)
        gated = gated_ref[:, lanes]
        part_ref[:, lanes] = grouped(
            long_ref[slab * per_slab : (slab + 1) * per_slab], gated
        ) + gain_ref[:, lanes] * gated.astype(jnp.float32)


def finish_kernel(
    four, part_ref, carry_ref, first_ref, far_ref, near_ref, through_ref, out_ref
):
    width = part_ref.shape[1]
    modes = near_ref.shape[0]
    per_slab = LANES // GROUP_CH
    diagonal = iota((LANES, LANES), 0) // modes == iota((LANES, LANES), 1) // GROUP_CH
    entering = near_ref[...].astype(jnp.float32)
    if four:
        place = lax.axis_index("ctx")
        entering = jnp.where(place >= 2, entering, 0.0)
        entering += jnp.where(place == 3, through_ref[...] * far_ref[...].astype(jnp.float32), 0.0)
        entering += jnp.where(place == 1, first_ref[...].astype(jnp.float32), 0.0)
    for slab in range(width // LANES):
        lanes = slice(slab * LANES, (slab + 1) * LANES)
        state = jnp.concatenate([entering[:, lanes]] * per_slab, axis=0)
        spread = jnp.where(diagonal, state, 0.0).astype(jnp.bfloat16)
        out_ref[:, lanes] = (part_ref[:, lanes] + dot(carry_ref[:, lanes], spread)).astype(
            out_ref.dtype
        )


def call(kernel, outs, *args, spaces=None, scratch=(), micros=0.3):
    spaces = spaces or [pltpu.VMEM] * len(args)
    return pl.pallas_call(
        kernel,
        out_shape=[jax.ShapeDtypeStruct(shape, dtype) for shape, dtype in outs],
        in_specs=[pl.BlockSpec(memory_space=space) for space in spaces],
        out_specs=[pl.BlockSpec(memory_space=pltpu.VMEM)] * len(outs),
        scratch_shapes=list(scratch),
        cost_estimate=pl.CostEstimate(
            flops=int(micros * 1e9), bytes_accessed=0, transcendentals=0
        ),
        compiler_params=pltpu.CompilerParams(vmem_limit_bytes=VMEM_BYTES),
    )(*args)


def shifted(array, axis, distance):
    size = lax.axis_size(axis)
    return lax.ppermute(array, axis, [(i, i + distance) for i in range(size - distance)])


def exchanged(array, axis, bit):
    return lax.ppermute(array, axis, [(i, i ^ bit) for i in range(lax.axis_size(axis))])


def cycled(array, cycle):
    fsdp_size, ctx_size = lax.axis_size("fsdp"), lax.axis_size("ctx")
    after = dict(zip(cycle, cycle[1:] + cycle[:1]))
    moves = []
    for core in range(fsdp_size):
        for place in range(ctx_size):
            other = (core, after[place]) if place in after else (core ^ 1, place)
            moves.append((core * ctx_size + place, other[0] * ctx_size + other[1]))
    return lax.ppermute(array, ("fsdp", "ctx"), moves)


def entering_states(state, through):
    size = lax.axis_size("ctx")
    total, factor, distance = state.astype(jnp.float32), through, 1
    while distance < size:
        total = total + factor * shifted(total, "ctx", distance)
        factor = factor * shifted(factor, "ctx", distance)
        distance *= 2
    return shifted(total, "ctx", 1)


def body(
    query_stream,
    key_stream,
    value_stream,
    document_starts,
    medium_taps,
    modal_rate,
    modal_residue,
    skip_gain,
):
    tokens, width = query_stream.shape[1:]
    groups = width // GROUP_CH
    fsdp_size, dp_size = lax.axis_size("fsdp"), lax.axis_size("dp")
    ctx_size = lax.axis_size("ctx")
    modes = modal_rate.shape[1] * dp_size
    assert fsdp_size == 2 and tokens == medium_taps.shape[1] * fsdp_size
    assert modes == GROUP_CH and modal_rate.shape[1] <= 8
    taps = medium_taps.T
    half = jnp.bfloat16
    rows = modal_rate.shape[0]
    inputs = [
        key_stream[0],
        value_stream[0],
        modal_rate.T,
        modal_residue.T,
        query_stream[0],
        taps,
        document_starts,
        skip_gain.reshape(1, width),
    ]
    product, modal, spread, select, query, own_taps, starts, gain = call(
        prepare_kernel,
        [
            ((tokens, width), half),
            ((16, rows), half),
            ((LANES, width), half),
            ((2 * modes, 16 * dp_size), half),
        ]
        + [(a.shape, a.dtype) for a in inputs[4:]],
        *[pltpu.with_memory_space_constraint(a, pltpu.HBM) for a in inputs],
        spaces=[pltpu.HBM] * len(inputs),
        scratch=[pltpu.VMEM(a.shape, a.dtype) for a in inputs[:4]]
        + [pltpu.SemaphoreType.DMA((len(inputs),))],
    )
    halo = lax.ppermute(product, "ctx", [(i, (i + 1) % ctx_size) for i in range(ctx_size)])
    other_taps = exchanged(taps, "fsdp", 1)
    bit = 1
    while 2 * bit < dp_size:
        modal = jnp.concatenate([modal, exchanged(modal, "dp", bit)], axis=0)
        bit *= 2
    modal_rest = exchanged(modal, "dp", bit)
    square = ((groups, tokens, tokens), half)
    previous, current, same, documents = call(
        medium_kernel,
        [square, square, ((tokens, tokens), half), ((tokens, tokens), jnp.float32)],
        own_taps,
        other_taps,
        starts,
        scratch=[pltpu.VMEM((LANES, tokens), jnp.float32)],
    )
    medium, gated_own = call(
        own_kernel,
        [((tokens, width), jnp.float32), ((tokens, width), half)],
        product,
        query,
        current,
    )
    states = ((modes, width), jnp.float32)
    end, channels, state_own = call(
        modal_kernel,
        [
            ((tokens, width), half),
            ((2 * modes, width), jnp.float32),
            ((modes, width), half),
        ],
        modal,
        modal_rest,
        select,
        spread,
        documents,
        gated_own,
    )
    four = ctx_size == 4
    first = cycled(state_own, [0, 1]) if four else state_own
    long, carry, through, first_through, far_through = call(
        long_kernel,
        [square, ((tokens, width), half), states, states, states],
        channels,
        starts,
        same,
        documents,
        scratch=[
            pltpu.VMEM((groups, tokens), jnp.float32),
        ],
    )
    gated, state = call(
        gate_kernel,
        [((tokens, width), half), ((modes, width), half)],
        halo,
        query,
        previous,
        medium,
        end,
        carry,
    )
    if four:
        both = state.astype(jnp.float32) + first_through * first.astype(jnp.float32)
        both = both.astype(half)
        near = cycled(both, [1, 2, 3])
        far = cycled(both, [1, 3, 2])
    else:
        near = far = entering_states(state, through)
    (part,) = call(local_kernel, [((tokens, width), jnp.float32)], gated, long, gain)
    (out,) = call(
        functools.partial(finish_kernel, four),
        [((tokens, width), half)],
        part,
        carry,
        first,
        far,
        near,
        far_through,
    )
    return out[None]


def solution(mesh):
    return jax.shard_map(
        body,
        mesh=mesh,
        in_specs=(
            P(None, "ctx", ("fsdp", "dp")),
            P(None, "ctx", ("fsdp", "dp")),
            P(None, "ctx", ("fsdp", "dp")),
            P(),
            P(None, "fsdp"),
            P("fsdp", "dp"),
            P("fsdp", "dp"),
            P(("fsdp", "dp")),
        ),
        out_specs=P(None, "ctx", ("fsdp", "dp")),
        check_vma=False,
    )
```

```python
import functools

import jax
import jax.numpy as jnp
from jax import lax
from jax.experimental import pallas as pl
from jax.experimental.pallas import tpu as pltpu
from jax.sharding import PartitionSpec as P

GROUP_CH = 16
LANES = 128
VMEM_BYTES = 32 * 1024 * 1024


def iota(shape, dim):
    return lax.broadcasted_iota(jnp.int32, shape, dim)


def dot(a, b, contract=((1,), (0,))):
    return lax.dot_general(a, b, (contract, ((), ())), preferred_element_type=jnp.float32)


def prepare_kernel(
    key_hbm,
    value_hbm,
    rate_hbm,
    residue_hbm,
    query_hbm,
    taps_hbm,
    starts_hbm,
    gain_hbm,
    product_ref,
    modal_ref,
    spread_ref,
    select_ref,
    query_ref,
    taps_ref,
    starts_ref,
    gain_ref,
    key_ref,
    value_ref,
    rate_ref,
    residue_ref,
    arrived,
):
    pairs = (
        (key_hbm, key_ref),
        (value_hbm, value_ref),
        (rate_hbm, rate_ref),
        (residue_hbm, residue_ref),
        (query_hbm, query_ref),
        (taps_hbm, taps_ref),
        (starts_hbm, starts_ref),
        (gain_hbm, gain_ref),
    )
    copies = [
        pltpu.make_async_copy(source, target, arrived.at[i])
        for i, (source, target) in enumerate(pairs)
    ]
    for copy in copies:
        copy.start()
    dp_place = lax.axis_index("dp")
    modes, width = select_ref.shape[0] // 2, spread_ref.shape[1]
    per_part = rate_ref.shape[0]
    lines = select_ref.shape[1]
    line, mode = iota((2 * modes, lines), 1), iota((2 * modes, lines), 0)
    within = line % 16
    held = jnp.where(mode < modes, within, within - 8)
    owner = jnp.bitwise_xor(dp_place, line // 16)
    wanted = owner * per_part + held == jnp.where(mode < modes, mode, mode - modes)
    select_ref[...] = ((held >= 0) & (held < per_part) & wanted).astype(jnp.bfloat16)
    first = dp_place * (width // modes) % LANES
    spread_ref[...] = (
        iota((LANES, width), 0) == first + iota((LANES, width), 1) // modes
    ).astype(jnp.bfloat16)
    for copy in copies[:4]:
        copy.wait()
    product_ref[...] = (
        key_ref[...].astype(jnp.float32) * value_ref[...].astype(jnp.float32)
    ).astype(jnp.bfloat16)
    rate = rate_ref[...].astype(jnp.float32)
    residue = residue_ref[...].astype(jnp.float32)
    gap = jnp.zeros((8 - rate.shape[0], rate.shape[1]), jnp.float32)
    modal_ref[...] = jnp.concatenate([rate, gap, residue, gap], axis=0).astype(jnp.bfloat16)
    for copy in copies[4:]:
        copy.wait()


def block_starts(starts_ref, ctx_place, block):
    prior_place = jnp.maximum(ctx_place - 1, 0)
    return [
        starts_ref[:, pl.ds(pl.multiple_of(place * block, block), block)].astype(jnp.float32)
        for place in (ctx_place, prior_place)
    ]


def document_masks(own, prior, block):
    row, col = iota((block, block), 0), iota((block, block), 1)
    both = jnp.concatenate(
        [jnp.broadcast_to(own, (8, block)), jnp.broadcast_to(prior, (8, block))], axis=0
    ).astype(jnp.bfloat16)
    upto = (row <= col).astype(jnp.bfloat16)
    doc_row = dot(both, upto)[0:1]
    after_row = dot(both, (row > col).astype(jnp.bfloat16))[8:9]
    doc_col = dot(
        upto, jnp.broadcast_to(own, (block, block)).astype(jnp.bfloat16), ((0,), (1,))
    )
    current = (row >= col) & (doc_col == doc_row)
    previous = (col > row) & (doc_col == 0.0) & (after_row == 0.0)
    return doc_col, current, previous


def circulant(row, block):
    return pltpu.roll(
        jnp.broadcast_to(row, (block // 2, block)), 0, 1, stride=1, stride_axis=0
    ).astype(jnp.bfloat16)


def folded(mask, block):
    half = block // 2
    lower = pltpu.roll(mask[half:], half, 1)
    return [mask[:half].astype(jnp.bfloat16), lower.astype(jnp.bfloat16)]


def medium_kernel(
    taps_ref,
    other_taps_ref,
    starts_ref,
    previous_ref,
    current_ref,
    same_ref,
    doc_ref,
    rows_ref,
):
    fsdp_place, ctx_place, dp_place = (lax.axis_index(axis) for axis in ("fsdp", "ctx", "dp"))
    groups, block = previous_ref.shape[0], previous_ref.shape[1]
    half = taps_ref.shape[0]
    first = (fsdp_place * lax.axis_size("dp") + dp_place) * groups
    base = pl.multiple_of(first // LANES * LANES, LANES)
    tap, lane = iota((half, block), 0), iota((half, block), 1)
    lag_of_lane = (block - lane) % block
    own_place = (tap + fsdp_place * half == lag_of_lane).astype(jnp.bfloat16)
    other_place = (tap + (1 - fsdp_place) * half == lag_of_lane).astype(jnp.bfloat16)
    rows_ref[...] = dot(taps_ref[:, pl.ds(base, LANES)], own_place, ((0,), (0,))) + dot(
        other_taps_ref[:, pl.ds(base, LANES)], other_place, ((0,), (0,))
    )
    own, prior = block_starts(starts_ref, ctx_place, block)
    doc_col, current, previous = document_masks(own, prior, block)
    current = folded(current.astype(jnp.float32), block)
    previous = folded((previous & (ctx_place > 0)).astype(jnp.float32), block)
    halves = [slice(0, block // 2), slice(block // 2, block)]
    doc_ref[...] = doc_col
    for part, rows in enumerate(halves):
        same_ref[rows, :] = current[part]
    for group in range(groups):
        turned = circulant(rows_ref[pl.ds(first - base + group, 1), :], block)
        for part, rows in enumerate(halves):
            previous_ref[group, rows, :] = turned * previous[part]
            current_ref[group, rows, :] = turned * current[part]


def slabs_of(width):
    return [slice(at, at + LANES) for at in range(0, width, LANES)]


def gated_by(query, medium):
    return (
        query.astype(jnp.float32) * medium.astype(jnp.bfloat16).astype(jnp.float32)
    ).astype(jnp.bfloat16)


def end_states(end_ref, gated_ref, state_ref):
    modes, width = state_ref.shape
    per_slab = LANES // GROUP_CH
    diagonal = iota((LANES, LANES), 0) // modes == iota((LANES, LANES), 1) // GROUP_CH
    for lanes in slabs_of(width):
        spread = jnp.where(
            diagonal, dot(end_ref[:, lanes], gated_ref[:, lanes], ((0,), (0,))), 0.0
        )
        state_ref[:, lanes] = jnp.sum(spread.reshape(per_slab, modes, LANES), axis=0).astype(
            state_ref.dtype
        )


def own_kernel(product_ref, query_ref, current_ref, medium_ref, gated_ref):
    per_slab = LANES // GROUP_CH
    for slab, lanes in enumerate(slabs_of(product_ref.shape[1])):
        medium = grouped(
            current_ref[slab * per_slab : (slab + 1) * per_slab], product_ref[:, lanes]
        )
        medium_ref[:, lanes] = medium
        gated_ref[:, lanes] = gated_by(query_ref[:, lanes], medium)


def on_line(modes, width):
    return iota((modes, width), 0) == iota((modes, width), 1) % modes


def modal_kernel(
    modal_ref,
    modal_rest_ref,
    select_ref,
    spread_ref,
    doc_ref,
    gated_ref,
    end_ref,
    channels_ref,
    state_ref,
):
    block, width = end_ref.shape
    modes = state_ref.shape[0]
    first = lax.axis_index("dp") * (width // modes)
    base = pl.multiple_of(first // LANES * LANES, LANES)
    pieces = jnp.concatenate(
        [modal_ref[:, pl.ds(base, LANES)], modal_rest_ref[:, pl.ds(base, LANES)]], axis=0
    )
    ordered = dot(select_ref[...], pieces)
    by_channel = dot(ordered.astype(jnp.bfloat16), spread_ref[...])
    channels_ref[...] = by_channel
    rate_line = jnp.sum(
        jnp.where(on_line(modes, width), by_channel[:modes], 0.0), axis=0, keepdims=True
    )
    left = (block - 1 - iota((block, LANES), 0)).astype(jnp.float32)
    keeps = doc_ref[...] == doc_ref[block - 1 : block, :]
    for lanes in slabs_of(width):
        weight = jnp.exp(-rate_line[:, lanes] * left)
        end_ref[:, lanes] = jnp.where(keeps, weight, 0.0).astype(jnp.bfloat16)
    end_states(end_ref, gated_ref, state_ref)


def long_kernel(
    channels_ref,
    starts_ref,
    same_ref,
    doc_ref,
    long_ref,
    carry_ref,
    through_ref,
    first_ref,
    far_ref,
    rows_ref,
):
    groups, block = long_ref.shape[0], long_ref.shape[1]
    modes, width = through_ref.shape
    ctx_place = lax.axis_index("ctx")
    rate = channels_ref[:modes]
    scaled = channels_ref[modes:] * jnp.sqrt((1.0 - jnp.exp(-2.0 * rate)) / modes)
    chosen = on_line(modes, width)
    rate_line = jnp.sum(jnp.where(chosen, rate, 0.0), axis=0, keepdims=True)
    scaled_line = jnp.sum(jnp.where(chosen, scaled, 0.0), axis=0, keepdims=True)
    lag = ((block - iota((block, LANES), 0)) % block).astype(jnp.float32)
    response = jnp.zeros((groups, block), jnp.float32)
    for lanes in slabs_of(width):
        terms = scaled_line[:, lanes] * jnp.exp(-rate_line[:, lanes] * lag)
        high = terms.astype(jnp.bfloat16)
        low = (terms - high.astype(jnp.float32)).astype(jnp.bfloat16)
        member = (
            iota((groups, LANES), 0) == (lanes.start + iota((groups, LANES), 1)) // modes
        ).astype(jnp.bfloat16)
        response += dot(member, high, ((1,), (1,))) + dot(member, low, ((1,), (1,)))
    rows_ref[...] = response
    since = (iota((block, LANES), 0) + 1).astype(jnp.float32)
    continues = doc_ref[...] == 0.0
    for lanes in slabs_of(width):
        weight = scaled_line[:, lanes] * jnp.exp(-rate_line[:, lanes] * since)
        carry_ref[:, lanes] = jnp.where(continues, weight, 0.0).astype(jnp.bfloat16)
    halves = [slice(0, block // 2), slice(block // 2, block)]
    same = [same_ref[rows, :] for rows in halves]
    for group in range(groups):
        turned = circulant(rows_ref[group : group + 1, :], block)
        for part, rows in enumerate(halves):
            long_ref[group, rows, :] = turned * same[part]
    decay = jnp.exp(-rate * block)
    own, prior = block_starts(starts_ref, ctx_place, block)
    none_own = jnp.sum(own, axis=1, keepdims=True) == 0.0
    none_prior = jnp.sum(prior, axis=1, keepdims=True) == 0.0
    through_ref[...] = jnp.where(none_own, decay, 0.0)
    first_ref[...] = jnp.where(none_own & (ctx_place == 1), decay, 0.0)
    far_ref[...] = jnp.where(none_prior, decay, 0.0)


def grouped(matrices, values):
    count, rows, _ = matrices.shape
    half = rows // 2
    lane = iota((half, LANES), 1) // GROUP_CH
    results = []
    for part in range(2):
        turned = values if part == 0 else jnp.concatenate([values[half:], values[:half]], axis=0)
        chosen = matrices[:, part * half : (part + 1) * half].reshape(count * half, rows)
        product = dot(chosen, turned)
        result = product[:half]
        for k in range(1, count):
            result = jnp.where(lane == k, product[k * half : (k + 1) * half], result)
        results.append(result)
    return jnp.concatenate(results, axis=0)


def gate_kernel(
    halo_ref, query_ref, previous_ref, medium_ref, end_ref, _, gated_ref, state_ref
):
    per_slab = LANES // GROUP_CH
    for slab, lanes in enumerate(slabs_of(halo_ref.shape[1])):
        medium = medium_ref[:, lanes] + grouped(
            previous_ref[slab * per_slab : (slab + 1) * per_slab], halo_ref[:, lanes]
        )
        gated_ref[:, lanes] = gated_by(query_ref[:, lanes], medium)
    end_states(end_ref, gated_ref, state_ref)


def local_kernel(gated_ref, long_ref, gain_ref, part_ref):
    width = gated_ref.shape[1]
    per_slab = LANES // GROUP_CH
    for slab in range(width // LANES):
        lanes = slice(slab * LANES, (slab + 1) * LANES)
        gated = gated_ref[:, lanes]
        part_ref[:, lanes] = grouped(
            long_ref[slab * per_slab : (slab + 1) * per_slab], gated
        ) + gain_ref[:, lanes] * gated.astype(jnp.float32)


def finish_kernel(
    four, part_ref, carry_ref, first_ref, far_ref, near_ref, through_ref, out_ref
):
    width = part_ref.shape[1]
    modes = near_ref.shape[0]
    per_slab = LANES // GROUP_CH
    diagonal = iota((LANES, LANES), 0) // modes == iota((LANES, LANES), 1) // GROUP_CH
    entering = near_ref[...].astype(jnp.float32)
    if four:
        place = lax.axis_index("ctx")
        entering = jnp.where(place >= 2, entering, 0.0)
        entering += jnp.where(place == 3, through_ref[...] * far_ref[...].astype(jnp.float32), 0.0)
        entering += jnp.where(place == 1, first_ref[...].astype(jnp.float32), 0.0)
    for slab in range(width // LANES):
        lanes = slice(slab * LANES, (slab + 1) * LANES)
        state = jnp.concatenate([entering[:, lanes]] * per_slab, axis=0)
        spread = jnp.where(diagonal, state, 0.0).astype(jnp.bfloat16)
        out_ref[:, lanes] = (part_ref[:, lanes] + dot(carry_ref[:, lanes], spread)).astype(
            out_ref.dtype
        )


def call(kernel, outs, *args, spaces=None, scratch=(), micros=0.3):
    spaces = spaces or [pltpu.VMEM] * len(args)
    return pl.pallas_call(
        kernel,
        out_shape=[jax.ShapeDtypeStruct(shape, dtype) for shape, dtype in outs],
        in_specs=[pl.BlockSpec(memory_space=space) for space in spaces],
        out_specs=[pl.BlockSpec(memory_space=pltpu.VMEM)] * len(outs),
        scratch_shapes=list(scratch),
        cost_estimate=pl.CostEstimate(
            flops=int(micros * 1e9), bytes_accessed=0, transcendentals=0
        ),
        compiler_params=pltpu.CompilerParams(vmem_limit_bytes=VMEM_BYTES),
    )(*args)


def shifted(array, axis, distance):
    size = lax.axis_size(axis)
    return lax.ppermute(array, axis, [(i, i + distance) for i in range(size - distance)])


def exchanged(array, axis, bit):
    return lax.ppermute(array, axis, [(i, i ^ bit) for i in range(lax.axis_size(axis))])


def cycled(array, cycle, crossing=()):
    fsdp_size, ctx_size = lax.axis_size("fsdp"), lax.axis_size("ctx")
    after = dict(zip(cycle, cycle[1:] + cycle[:1]))
    moves = []
    for core in range(fsdp_size):
        for place in range(ctx_size):
            other = (core ^ (place in crossing), after[place]) if place in after else (core ^ 1, place)
            moves.append((core * ctx_size + place, other[0] * ctx_size + other[1]))
    return lax.ppermute(array, ("fsdp", "ctx"), moves)


def entering_states(state, through):
    size = lax.axis_size("ctx")
    total, factor, distance = state.astype(jnp.float32), through, 1
    while distance < size:
        total = total + factor * shifted(total, "ctx", distance)
        factor = factor * shifted(factor, "ctx", distance)
        distance *= 2
    return shifted(total, "ctx", 1)


def body(
    query_stream,
    key_stream,
    value_stream,
    document_starts,
    medium_taps,
    modal_rate,
    modal_residue,
    skip_gain,
):
    tokens, width = query_stream.shape[1:]
    groups = width // GROUP_CH
    fsdp_size, dp_size = lax.axis_size("fsdp"), lax.axis_size("dp")
    ctx_size = lax.axis_size("ctx")
    modes = modal_rate.shape[1] * dp_size
    assert fsdp_size == 2 and tokens == medium_taps.shape[1] * fsdp_size
    assert modes == GROUP_CH and modal_rate.shape[1] <= 8
    taps = medium_taps.T
    half = jnp.bfloat16
    rows = modal_rate.shape[0]
    inputs = [
        key_stream[0],
        value_stream[0],
        modal_rate.T,
        modal_residue.T,
        query_stream[0],
        taps,
        document_starts,
        skip_gain.reshape(1, width),
    ]
    product, modal, spread, select, query, own_taps, starts, gain = call(
        prepare_kernel,
        [
            ((tokens, width), half),
            ((16, rows), half),
            ((LANES, width), half),
            ((2 * modes, 16 * dp_size), half),
        ]
        + [(a.shape, a.dtype) for a in inputs[4:]],
        *[pltpu.with_memory_space_constraint(a, pltpu.HBM) for a in inputs],
        spaces=[pltpu.HBM] * len(inputs),
        scratch=[pltpu.VMEM(a.shape, a.dtype) for a in inputs[:4]]
        + [pltpu.SemaphoreType.DMA((len(inputs),))],
    )
    halo = lax.ppermute(product, "ctx", [(i, (i + 1) % ctx_size) for i in range(ctx_size)])
    other_taps = exchanged(taps, "fsdp", 1)
    bit = 1
    while 2 * bit < dp_size:
        modal = jnp.concatenate([modal, exchanged(modal, "dp", bit)], axis=0)
        bit *= 2
    modal_rest = exchanged(modal, "dp", bit)
    square = ((groups, tokens, tokens), half)
    previous, current, same, documents = call(
        medium_kernel,
        [square, square, ((tokens, tokens), half), ((tokens, tokens), jnp.float32)],
        own_taps,
        other_taps,
        starts,
        scratch=[pltpu.VMEM((LANES, tokens), jnp.float32)],
    )
    medium, gated_own = call(
        own_kernel,
        [((tokens, width), jnp.float32), ((tokens, width), half)],
        product,
        query,
        current,
    )
    states = ((modes, width), jnp.float32)
    end, channels, state_own = call(
        modal_kernel,
        [
            ((tokens, width), half),
            ((2 * modes, width), jnp.float32),
            ((modes, width), half),
        ],
        modal,
        modal_rest,
        select,
        spread,
        documents,
        gated_own,
    )
    four = ctx_size == 4
    first = cycled(state_own, [0, 1]) if four else state_own
    long, carry, through, first_through, far_through = call(
        long_kernel,
        [square, ((tokens, width), half), states, states, states],
        channels,
        starts,
        same,
        documents,
        scratch=[
            pltpu.VMEM((groups, tokens), jnp.float32),
        ],
    )
    gated, state = call(
        gate_kernel,
        [((tokens, width), half), ((modes, width), half)],
        halo,
        query,
        previous,
        medium,
        end,
        carry,
    )
    if four:
        both = state.astype(jnp.float32) + first_through * first.astype(jnp.float32)
        both = both.astype(half)
        near = cycled(both, [1, 2, 3], (3,))
        far = cycled(both, [1, 3, 2], (2,))
    else:
        near = far = entering_states(state, through)
    (part,) = call(local_kernel, [((tokens, width), jnp.float32)], gated, long, gain)
    (out,) = call(
        functools.partial(finish_kernel, four),
        [((tokens, width), half)],
        part,
        carry,
        first,
        far,
        near,
        far_through,
    )
    return out[None]


def solution(mesh):
    return jax.shard_map(
        body,
        mesh=mesh,
        in_specs=(
            P(None, "ctx", ("fsdp", "dp")),
            P(None, "ctx", ("fsdp", "dp")),
            P(None, "ctx", ("fsdp", "dp")),
            P(),
            P(None, "fsdp"),
            P("fsdp", "dp"),
            P("fsdp", "dp"),
            P(("fsdp", "dp")),
        ),
        out_specs=P(None, "ctx", ("fsdp", "dp")),
        check_vma=False,
    )
```

```python
import functools

import jax
import jax.numpy as jnp
from jax import lax
from jax.experimental import pallas as pl
from jax.experimental.pallas import tpu as pltpu
from jax.sharding import PartitionSpec as P

GROUP_CH = 16
LANES = 128
VMEM_BYTES = 32 * 1024 * 1024


def iota(shape, dim):
    return lax.broadcasted_iota(jnp.int32, shape, dim)


def dot(a, b, contract=((1,), (0,))):
    return lax.dot_general(a, b, (contract, ((), ())), preferred_element_type=jnp.float32)


def prepare_kernel(
    key_hbm,
    value_hbm,
    rate_hbm,
    residue_hbm,
    query_hbm,
    taps_hbm,
    starts_hbm,
    gain_hbm,
    product_ref,
    modal_ref,
    spread_ref,
    select_ref,
    rates_ref,
    query_ref,
    taps_ref,
    starts_ref,
    gain_ref,
    key_ref,
    value_ref,
    rate_ref,
    residue_ref,
    arrived,
):
    pairs = (
        (key_hbm, key_ref),
        (value_hbm, value_ref),
        (rate_hbm, rate_ref),
        (residue_hbm, residue_ref),
        (query_hbm, query_ref),
        (taps_hbm, taps_ref),
        (starts_hbm, starts_ref),
        (gain_hbm, gain_ref),
    )
    copies = [
        pltpu.make_async_copy(source, target, arrived.at[i])
        for i, (source, target) in enumerate(pairs)
    ]
    for copy in copies:
        copy.start()
    dp_place = lax.axis_index("dp")
    modes, width = select_ref.shape[0] // 2, spread_ref.shape[1]
    per_part = rate_ref.shape[0]
    lines = select_ref.shape[1]
    line, mode = iota((2 * modes, lines), 1), iota((2 * modes, lines), 0)
    within = line % 16
    held = jnp.where(mode < modes, within, within - 8)
    owner = jnp.bitwise_xor(dp_place, line // 16)
    wanted = owner * per_part + held == jnp.where(mode < modes, mode, mode - modes)
    select_ref[...] = ((held >= 0) & (held < per_part) & wanted).astype(jnp.bfloat16)
    line, mode = iota((lines, width), 0), iota((lines, width), 1) % modes
    within = line % 16
    owner = jnp.bitwise_xor(dp_place, line // 16)
    rates_ref[...] = ((within < per_part) & (owner * per_part + within == mode)).astype(
        jnp.float32
    )
    first = dp_place * (width // modes) % LANES
    spread_ref[...] = (
        iota((LANES, width), 0) == first + iota((LANES, width), 1) // modes
    ).astype(jnp.bfloat16)
    for copy in copies[:4]:
        copy.wait()
    product_ref[...] = (
        key_ref[...].astype(jnp.float32) * value_ref[...].astype(jnp.float32)
    ).astype(jnp.bfloat16)
    rate = rate_ref[...].astype(jnp.float32)
    residue = residue_ref[...].astype(jnp.float32)
    gap = jnp.zeros((8 - rate.shape[0], rate.shape[1]), jnp.float32)
    modal_ref[...] = jnp.concatenate([rate, gap, residue, gap], axis=0).astype(jnp.bfloat16)
    for copy in copies[4:]:
        copy.wait()


def block_starts(starts_ref, ctx_place, block):
    prior_place = jnp.maximum(ctx_place - 1, 0)
    return [
        starts_ref[:, pl.ds(pl.multiple_of(place * block, block), block)].astype(jnp.float32)
        for place in (ctx_place, prior_place)
    ]


def document_masks(own, prior, block):
    row, col = iota((block, block), 0), iota((block, block), 1)
    both = jnp.concatenate(
        [jnp.broadcast_to(own, (8, block)), jnp.broadcast_to(prior, (8, block))], axis=0
    ).astype(jnp.bfloat16)
    upto = (row <= col).astype(jnp.bfloat16)
    doc_row = dot(both, upto)[0:1]
    after_row = dot(both, (row > col).astype(jnp.bfloat16))[8:9]
    doc_col = dot(
        upto, jnp.broadcast_to(own, (block, block)).astype(jnp.bfloat16), ((0,), (1,))
    )
    current = (row >= col) & (doc_col == doc_row)
    previous = (col > row) & (doc_col == 0.0) & (after_row == 0.0)
    return doc_col, current, previous


def circulant(row, block):
    return pltpu.roll(
        jnp.broadcast_to(row, (block // 2, block)), 0, 1, stride=1, stride_axis=0
    ).astype(jnp.bfloat16)


def folded(mask, block):
    half = block // 2
    lower = pltpu.roll(mask[half:], half, 1)
    return [mask[:half].astype(jnp.bfloat16), lower.astype(jnp.bfloat16)]


def medium_kernel(
    taps_ref,
    other_taps_ref,
    starts_ref,
    previous_ref,
    current_ref,
    same_ref,
    doc_ref,
    rows_ref,
):
    fsdp_place, ctx_place, dp_place = (lax.axis_index(axis) for axis in ("fsdp", "ctx", "dp"))
    groups, block = previous_ref.shape[0], previous_ref.shape[1]
    half = taps_ref.shape[0]
    first = (fsdp_place * lax.axis_size("dp") + dp_place) * groups
    base = pl.multiple_of(first // LANES * LANES, LANES)
    tap, lane = iota((half, block), 0), iota((half, block), 1)
    lag_of_lane = (block - lane) % block
    own_place = (tap + fsdp_place * half == lag_of_lane).astype(jnp.bfloat16)
    other_place = (tap + (1 - fsdp_place) * half == lag_of_lane).astype(jnp.bfloat16)
    rows_ref[...] = dot(taps_ref[:, pl.ds(base, LANES)], own_place, ((0,), (0,))) + dot(
        other_taps_ref[:, pl.ds(base, LANES)], other_place, ((0,), (0,))
    )
    own, prior = block_starts(starts_ref, ctx_place, block)
    doc_col, current, previous = document_masks(own, prior, block)
    current = folded(current.astype(jnp.float32), block)
    previous = folded((previous & (ctx_place > 0)).astype(jnp.float32), block)
    halves = [slice(0, block // 2), slice(block // 2, block)]
    doc_ref[...] = doc_col
    for part, rows in enumerate(halves):
        same_ref[rows, :] = current[part]
    for group in range(groups):
        turned = circulant(rows_ref[pl.ds(first - base + group, 1), :], block)
        for part, rows in enumerate(halves):
            previous_ref[group, rows, :] = turned * previous[part]
            current_ref[group, rows, :] = turned * current[part]


def slabs_of(width):
    return [slice(at, at + LANES) for at in range(0, width, LANES)]


def gated_by(query, medium):
    return (
        query.astype(jnp.float32) * medium.astype(jnp.bfloat16).astype(jnp.float32)
    ).astype(jnp.bfloat16)


def end_states(end_ref, gated_ref, state_ref):
    modes, width = state_ref.shape
    per_slab = LANES // GROUP_CH
    diagonal = iota((LANES, LANES), 0) // modes == iota((LANES, LANES), 1) // GROUP_CH
    for lanes in slabs_of(width):
        spread = jnp.where(
            diagonal, dot(end_ref[:, lanes], gated_ref[:, lanes], ((0,), (0,))), 0.0
        )
        state_ref[:, lanes] = jnp.sum(spread.reshape(per_slab, modes, LANES), axis=0).astype(
            state_ref.dtype
        )


def own_kernel(product_ref, query_ref, current_ref, medium_ref, gated_ref):
    for slab, lanes in enumerate(slabs_of(product_ref.shape[1])):
        medium = grouped(stored_halves(current_ref, slab), product_ref[:, lanes])
        medium_ref[:, lanes] = medium
        gated_ref[:, lanes] = gated_by(query_ref[:, lanes], medium)


def on_line(modes, width):
    return iota((modes, width), 0) == iota((modes, width), 1) % modes


def modal_parts(modal_refs, spread_ref, groups):
    first = lax.axis_index("dp") * groups
    base = pl.multiple_of(first // LANES * LANES, LANES)
    pieces = jnp.concatenate([ref[:, pl.ds(base, LANES)] for ref in modal_refs], axis=0)
    return dot(pieces, spread_ref[...])


def end_weights(lines, rates_ref, doc_ref, end_ref):
    block, width = end_ref.shape
    rate_line = jnp.sum(lines * rates_ref[...], axis=0, keepdims=True)
    left = (block - 1 - iota((block, LANES), 0)).astype(jnp.float32)
    keeps = doc_ref[...] == doc_ref[block - 1 : block, :]
    for lanes in slabs_of(width):
        weight = jnp.exp(-rate_line[:, lanes] * left)
        end_ref[:, lanes] = jnp.where(keeps, weight, 0.0).astype(jnp.bfloat16)


def first_kernel(
    modal_ref, modal_rest_ref, spread_ref, rates_ref, doc_ref, gated_ref, state_ref, end_ref
):
    modes, width = state_ref.shape

    @pl.when(lax.axis_index("ctx") == 0)
    def _():
        lines = modal_parts([modal_ref, modal_rest_ref], spread_ref, width // modes)
        end_weights(lines, rates_ref, doc_ref, end_ref)
        end_states(end_ref, gated_ref, state_ref)

    @pl.when(lax.axis_index("ctx") != 0)
    def _():
        state_ref[...] = jnp.zeros_like(state_ref)


def modal_kernel(
    modal_ref,
    modal_rest_ref,
    select_ref,
    spread_ref,
    rates_ref,
    doc_ref,
    _,
    end_ref,
    channels_ref,
):
    modes, width = channels_ref.shape[0] // 2, channels_ref.shape[1]
    lines = modal_parts([modal_ref, modal_rest_ref], spread_ref, width // modes)
    end_weights(lines, rates_ref, doc_ref, end_ref)
    channels_ref[...] = dot(select_ref[...], lines.astype(jnp.bfloat16))


def modal_lines(channels_ref, modes, width):
    rate = channels_ref[:modes]
    scaled = channels_ref[modes:] * jnp.sqrt((1.0 - jnp.exp(-2.0 * rate)) / modes)
    chosen = on_line(modes, width)
    return [
        jnp.sum(jnp.where(chosen, part, 0.0), axis=0, keepdims=True) for part in (rate, scaled)
    ]


def response_kernel(channels_ref, starts_ref, rows_ref, through_ref, first_ref, far_ref):
    groups, block = rows_ref.shape
    modes, width = through_ref.shape
    ctx_place = lax.axis_index("ctx")
    rate_line, scaled_line = modal_lines(channels_ref, modes, width)
    lag = ((block - iota((block, LANES), 0)) % block).astype(jnp.float32)
    per_slab = LANES // modes
    gather = (iota((LANES, LANES), 0) // modes == iota((LANES, LANES), 1)).astype(jnp.bfloat16)
    for slab, lanes in enumerate(slabs_of(width)):
        terms = scaled_line[:, lanes] * jnp.exp(-rate_line[:, lanes] * lag)
        high = terms.astype(jnp.bfloat16)
        low = (terms - high.astype(jnp.float32)).astype(jnp.bfloat16)
        sums = jnp.transpose(dot(high, gather) + dot(low, gather))
        rows_ref[slab * per_slab : (slab + 1) * per_slab, :] = sums[:per_slab]
    decay = jnp.exp(-channels_ref[:modes] * block)
    own, prior = block_starts(starts_ref, ctx_place, block)
    none_own = jnp.sum(own, axis=1, keepdims=True) == 0.0
    none_prior = jnp.sum(prior, axis=1, keepdims=True) == 0.0
    through_ref[...] = jnp.where(none_own, decay, 0.0)
    first_ref[...] = jnp.where(none_own & (ctx_place == 1), decay, 0.0)
    far_ref[...] = jnp.where(none_prior, decay, 0.0)


def grouped(halves, values):
    rows = values.shape[0]
    half = rows // 2
    lane = iota((half, LANES), 1) // GROUP_CH
    results = []
    for part, chosen in enumerate(halves):
        turned = values if part == 0 else jnp.concatenate([values[half:], values[:half]], axis=0)
        product = dot(chosen, turned)
        result = product[:half]
        for k in range(1, chosen.shape[0] // half):
            result = jnp.where(lane == k, product[k * half : (k + 1) * half], result)
        results.append(result)
    return jnp.concatenate(results, axis=0)


def stored_halves(matrices_ref, slab):
    per_slab = LANES // GROUP_CH
    groups = slice(slab * per_slab, (slab + 1) * per_slab)
    half = matrices_ref.shape[1] // 2
    return [
        matrices_ref[groups, part * half : (part + 1) * half].reshape(per_slab * half, 2 * half)
        for part in range(2)
    ]


def gate_kernel(
    halo_ref, query_ref, previous_ref, medium_ref, end_ref, _, gated_ref, state_ref
):
    for slab, lanes in enumerate(slabs_of(halo_ref.shape[1])):
        medium = medium_ref[:, lanes] + grouped(
            stored_halves(previous_ref, slab), halo_ref[:, lanes]
        )
        gated_ref[:, lanes] = gated_by(query_ref[:, lanes], medium)
    end_states(end_ref, gated_ref, state_ref)


def local_kernel(gated_ref, rows_ref, same_ref, doc_ref, channels_ref, gain_ref, part_ref, carry_ref):
    block, width = part_ref.shape
    modes = channels_ref.shape[0] // 2
    per_slab = LANES // GROUP_CH
    half = block // 2
    same = [same_ref[:half, :], same_ref[half:, :]]
    rate_line, scaled_line = modal_lines(channels_ref, modes, width)
    since = (iota((block, LANES), 0) + 1).astype(jnp.float32)
    continues = doc_ref[...] == 0.0
    for slab, lanes in enumerate(slabs_of(width)):
        turned = [
            circulant(rows_ref[group : group + 1, :], block)
            for group in range(slab * per_slab, (slab + 1) * per_slab)
        ]
        halves = [jnp.concatenate([line * mask for line in turned], axis=0) for mask in same]
        gated = gated_ref[:, lanes]
        part_ref[:, lanes] = grouped(halves, gated) + gain_ref[:, lanes] * gated.astype(jnp.float32)
        weight = scaled_line[:, lanes] * jnp.exp(-rate_line[:, lanes] * since)
        carry_ref[:, lanes] = jnp.where(continues, weight, 0.0).astype(jnp.bfloat16)


def finish_kernel(
    four, part_ref, carry_ref, first_ref, near_ref, far_ref, through_ref, out_ref
):
    width = part_ref.shape[1]
    modes = near_ref.shape[0]
    per_slab = LANES // GROUP_CH
    diagonal = iota((LANES, LANES), 0) // modes == iota((LANES, LANES), 1) // GROUP_CH
    entering = near_ref[...].astype(jnp.float32)
    if four:
        place = lax.axis_index("ctx")
        entering = jnp.where(place >= 2, entering, 0.0)
        entering += jnp.where(place == 3, through_ref[...] * far_ref[...].astype(jnp.float32), 0.0)
        entering += jnp.where(place == 1, first_ref[...].astype(jnp.float32), 0.0)
    for slab in range(width // LANES):
        lanes = slice(slab * LANES, (slab + 1) * LANES)
        state = jnp.concatenate([entering[:, lanes]] * per_slab, axis=0)
        spread = jnp.where(diagonal, state, 0.0).astype(jnp.bfloat16)
        out_ref[:, lanes] = (part_ref[:, lanes] + dot(carry_ref[:, lanes], spread)).astype(
            out_ref.dtype
        )


def call(kernel, outs, *args, spaces=None, scratch=(), micros=0.3):
    spaces = spaces or [pltpu.VMEM] * len(args)
    return pl.pallas_call(
        kernel,
        out_shape=[jax.ShapeDtypeStruct(shape, dtype) for shape, dtype in outs],
        in_specs=[pl.BlockSpec(memory_space=space) for space in spaces],
        out_specs=[pl.BlockSpec(memory_space=pltpu.VMEM)] * len(outs),
        scratch_shapes=list(scratch),
        cost_estimate=pl.CostEstimate(
            flops=int(micros * 1e9), bytes_accessed=0, transcendentals=0
        ),
        compiler_params=pltpu.CompilerParams(vmem_limit_bytes=VMEM_BYTES),
    )(*args)


def shifted(array, axis, distance):
    size = lax.axis_size(axis)
    return lax.ppermute(array, axis, [(i, i + distance) for i in range(size - distance)])


def exchanged(array, axis, bit):
    return lax.ppermute(array, axis, [(i, i ^ bit) for i in range(lax.axis_size(axis))])


def cycled(array, cycle, crossing=()):
    fsdp_size, ctx_size = lax.axis_size("fsdp"), lax.axis_size("ctx")
    after = dict(zip(cycle, cycle[1:] + cycle[:1]))
    moves = []
    for core in range(fsdp_size):
        for place in range(ctx_size):
            other = (core ^ (place in crossing), after[place]) if place in after else (core ^ 1, place)
            moves.append((core * ctx_size + place, other[0] * ctx_size + other[1]))
    return lax.ppermute(array, ("fsdp", "ctx"), moves)


def entering_states(state, through):
    size = lax.axis_size("ctx")
    total, factor, distance = state.astype(jnp.float32), through, 1
    while distance < size:
        total = total + factor * shifted(total, "ctx", distance)
        factor = factor * shifted(factor, "ctx", distance)
        distance *= 2
    return shifted(total, "ctx", 1)


def body(
    query_stream,
    key_stream,
    value_stream,
    document_starts,
    medium_taps,
    modal_rate,
    modal_residue,
    skip_gain,
):
    tokens, width = query_stream.shape[1:]
    groups = width // GROUP_CH
    fsdp_size, dp_size = lax.axis_size("fsdp"), lax.axis_size("dp")
    ctx_size = lax.axis_size("ctx")
    modes = modal_rate.shape[1] * dp_size
    assert fsdp_size == 2 and tokens == medium_taps.shape[1] * fsdp_size
    assert modes == GROUP_CH and modal_rate.shape[1] <= 8
    taps = medium_taps.T
    half = jnp.bfloat16
    rows = modal_rate.shape[0]
    inputs = [
        key_stream[0],
        value_stream[0],
        modal_rate.T,
        modal_residue.T,
        query_stream[0],
        taps,
        document_starts,
        skip_gain.reshape(1, width),
    ]
    product, modal, spread, select, rates, query, own_taps, starts, gain = call(
        prepare_kernel,
        [
            ((tokens, width), half),
            ((16, rows), half),
            ((LANES, width), half),
            ((2 * modes, 16 * dp_size), half),
            ((16 * dp_size, width), jnp.float32),
        ]
        + [(a.shape, a.dtype) for a in inputs[4:]],
        *[pltpu.with_memory_space_constraint(a, pltpu.HBM) for a in inputs],
        spaces=[pltpu.HBM] * len(inputs),
        scratch=[pltpu.VMEM(a.shape, a.dtype) for a in inputs[:4]]
        + [pltpu.SemaphoreType.DMA((len(inputs),))],
    )
    halo = lax.ppermute(product, "ctx", [(i, (i + 1) % ctx_size) for i in range(ctx_size)])
    other_taps = exchanged(taps, "fsdp", 1)
    bit = 1
    while 2 * bit < dp_size:
        modal = jnp.concatenate([modal, exchanged(modal, "dp", bit)], axis=0)
        bit *= 2
    modal_rest = exchanged(modal, "dp", bit)
    square = ((groups, tokens, tokens), half)
    previous, current, same, documents = call(
        medium_kernel,
        [square, square, ((tokens, tokens), half), ((tokens, tokens), jnp.float32)],
        own_taps,
        other_taps,
        starts,
        scratch=[pltpu.VMEM((LANES, tokens), jnp.float32)],
    )
    medium, gated_own = call(
        own_kernel,
        [((tokens, width), jnp.float32), ((tokens, width), half)],
        product,
        query,
        current,
    )
    states = ((modes, width), jnp.float32)
    (state_own,) = call(
        first_kernel,
        [((modes, width), half)],
        modal,
        modal_rest,
        spread,
        rates,
        documents,
        gated_own,
        scratch=[pltpu.VMEM((tokens, width), half)],
    )
    end, channels = call(
        modal_kernel,
        [((tokens, width), half), ((2 * modes, width), jnp.float32)],
        modal,
        modal_rest,
        select,
        spread,
        rates,
        documents,
        state_own,
    )
    four = ctx_size == 4
    first = cycled(state_own, [0, 1]) if four else state_own
    response, through, first_through, far_through = call(
        response_kernel,
        [((groups, tokens), jnp.float32), states, states, states],
        channels,
        starts,
    )
    gated, state = call(
        gate_kernel,
        [((tokens, width), half), ((modes, width), half)],
        halo,
        query,
        previous,
        medium,
        end,
        response,
    )
    if four:
        both = state.astype(jnp.float32) + first_through * first.astype(jnp.float32)
        both = both.astype(half)
        near = cycled(both, [1, 2, 3], (3, ))
        far = cycled(both, [1, 3, 2], (3, ))
    else:
        near = far = entering_states(state, through)
    part, carry = call(
        local_kernel,
        [((tokens, width), jnp.float32), ((tokens, width), half)],
        gated,
        response,
        same,
        documents,
        channels,
        gain,
    )
    (out,) = call(
        functools.partial(finish_kernel, four),
        [((tokens, width), half)],
        part,
        carry,
        first,
        near,
        far,
        far_through,
    )
    return out[None]


def solution(mesh):
    return jax.shard_map(
        body,
        mesh=mesh,
        in_specs=(
            P(None, "ctx", ("fsdp", "dp")),
            P(None, "ctx", ("fsdp", "dp")),
            P(None, "ctx", ("fsdp", "dp")),
            P(),
            P(None, "fsdp"),
            P("fsdp", "dp"),
            P("fsdp", "dp"),
            P(("fsdp", "dp")),
        ),
        out_specs=P(None, "ctx", ("fsdp", "dp")),
        check_vma=False,
    )
```

```python
import functools

import jax
import jax.numpy as jnp
from jax import lax
from jax.experimental import pallas as pl
from jax.experimental.pallas import tpu as pltpu
from jax.sharding import PartitionSpec as P

GROUP_CH = 16
LANES = 128
VMEM_BYTES = 32 * 1024 * 1024


def iota(shape, dim):
    return lax.broadcasted_iota(jnp.int32, shape, dim)


def dot(a, b, contract=((1,), (0,))):
    return lax.dot_general(a, b, (contract, ((), ())), preferred_element_type=jnp.float32)


def prepare_kernel(
    key_hbm,
    value_hbm,
    rate_hbm,
    residue_hbm,
    query_hbm,
    taps_hbm,
    starts_hbm,
    gain_hbm,
    product_ref,
    modal_ref,
    spread_ref,
    select_ref,
    rates_ref,
    query_ref,
    taps_ref,
    starts_ref,
    gain_ref,
    key_ref,
    value_ref,
    rate_ref,
    residue_ref,
    arrived,
):
    pairs = (
        (key_hbm, key_ref),
        (value_hbm, value_ref),
        (rate_hbm, rate_ref),
        (residue_hbm, residue_ref),
        (query_hbm, query_ref),
        (taps_hbm, taps_ref),
        (starts_hbm, starts_ref),
        (gain_hbm, gain_ref),
    )
    copies = [
        pltpu.make_async_copy(source, target, arrived.at[i])
        for i, (source, target) in enumerate(pairs)
    ]
    for copy in copies:
        copy.start()
    dp_place = lax.axis_index("dp")
    modes, width = select_ref.shape[0] // 2, spread_ref.shape[1]
    per_part = rate_ref.shape[0]
    lines = select_ref.shape[1]
    pieces = lines // 16
    line, mode = iota((2 * modes, lines), 1), iota((2 * modes, lines), 0)
    within = line % 16
    held = jnp.where(mode < modes, within, within - 8)
    owner = jnp.bitwise_xor(dp_place, (pieces - line // 16) % pieces)
    wanted = owner * per_part + held == jnp.where(mode < modes, mode, mode - modes)
    select_ref[...] = ((held >= 0) & (held < per_part) & wanted).astype(jnp.bfloat16)
    line, mode = iota((lines, width), 0), iota((lines, width), 1) % modes
    within = line % 16
    owner = jnp.bitwise_xor(dp_place, (pieces - line // 16) % pieces)
    rates_ref[...] = ((within < per_part) & (owner * per_part + within == mode)).astype(
        jnp.float32
    )
    first = dp_place * (width // modes) % LANES
    spread_ref[...] = (
        iota((LANES, width), 0) == first + iota((LANES, width), 1) // modes
    ).astype(jnp.bfloat16)
    for copy in copies[:4]:
        copy.wait()
    product_ref[...] = (
        key_ref[...].astype(jnp.float32) * value_ref[...].astype(jnp.float32)
    ).astype(jnp.bfloat16)
    rate = rate_ref[...].astype(jnp.float32)
    residue = residue_ref[...].astype(jnp.float32)
    gap = jnp.zeros((8 - rate.shape[0], rate.shape[1]), jnp.float32)
    modal_ref[...] = jnp.concatenate([rate, gap, residue, gap], axis=0).astype(jnp.bfloat16)
    for copy in copies[4:]:
        copy.wait()


def block_starts(starts_ref, ctx_place, block):
    prior_place = jnp.maximum(ctx_place - 1, 0)
    return [
        starts_ref[:, pl.ds(pl.multiple_of(place * block, block), block)].astype(jnp.float32)
        for place in (ctx_place, prior_place)
    ]


def document_masks(own, prior, block):
    row, col = iota((block, block), 0), iota((block, block), 1)
    both = jnp.concatenate(
        [jnp.broadcast_to(own, (8, block)), jnp.broadcast_to(prior, (8, block))], axis=0
    ).astype(jnp.bfloat16)
    upto = (row <= col).astype(jnp.bfloat16)
    doc_row = dot(both, upto)[0:1]
    after_row = dot(both, (row > col).astype(jnp.bfloat16))[8:9]
    doc_col = dot(
        upto, jnp.broadcast_to(own, (block, block)).astype(jnp.bfloat16), ((0,), (1,))
    )
    current = (row >= col) & (doc_col == doc_row)
    previous = (col > row) & (doc_col == 0.0) & (after_row == 0.0)
    return doc_col, current, previous


def circulant(row, block):
    return pltpu.roll(
        jnp.broadcast_to(row, (block // 2, block)), 0, 1, stride=1, stride_axis=0
    ).astype(jnp.bfloat16)


def folded(mask, block):
    half = block // 2
    lower = pltpu.roll(mask[half:], half, 1)
    return [mask[:half].astype(jnp.bfloat16), lower.astype(jnp.bfloat16)]


def medium_kernel(
    taps_ref,
    other_taps_ref,
    starts_ref,
    previous_ref,
    current_ref,
    same_ref,
    doc_ref,
    rows_ref,
):
    fsdp_place, ctx_place, dp_place = (lax.axis_index(axis) for axis in ("fsdp", "ctx", "dp"))
    groups, block = previous_ref.shape[0], previous_ref.shape[1]
    half = taps_ref.shape[0]
    first = (fsdp_place * lax.axis_size("dp") + dp_place) * groups
    base = pl.multiple_of(first // LANES * LANES, LANES)
    tap, lane = iota((half, block), 0), iota((half, block), 1)
    lag_of_lane = (block - lane) % block
    own_place = (tap + fsdp_place * half == lag_of_lane).astype(jnp.bfloat16)
    other_place = (tap + (1 - fsdp_place) * half == lag_of_lane).astype(jnp.bfloat16)
    rows_ref[...] = dot(taps_ref[:, pl.ds(base, LANES)], own_place, ((0,), (0,))) + dot(
        other_taps_ref[:, pl.ds(base, LANES)], other_place, ((0,), (0,))
    )
    own, prior = block_starts(starts_ref, ctx_place, block)
    doc_col, current, previous = document_masks(own, prior, block)
    current = folded(current.astype(jnp.float32), block)
    previous = folded((previous & (ctx_place > 0)).astype(jnp.float32), block)
    halves = [slice(0, block // 2), slice(block // 2, block)]
    doc_ref[...] = doc_col
    for part, rows in enumerate(halves):
        same_ref[rows, :] = current[part]
    for group in range(groups):
        turned = circulant(rows_ref[pl.ds(first - base + group, 1), :], block)
        for part, rows in enumerate(halves):
            previous_ref[group, rows, :] = turned * previous[part]
            current_ref[group, rows, :] = turned * current[part]


def slabs_of(width):
    return [slice(at, at + LANES) for at in range(0, width, LANES)]


def gated_by(query, medium):
    return (
        query.astype(jnp.float32) * medium.astype(jnp.bfloat16).astype(jnp.float32)
    ).astype(jnp.bfloat16)


def end_states(end_ref, gated_ref, state_ref):
    modes, width = state_ref.shape
    per_slab = LANES // GROUP_CH
    diagonal = iota((LANES, LANES), 0) // modes == iota((LANES, LANES), 1) // GROUP_CH
    for lanes in slabs_of(width):
        spread = jnp.where(
            diagonal, dot(end_ref[:, lanes], gated_ref[:, lanes], ((0,), (0,))), 0.0
        )
        state_ref[:, lanes] = jnp.sum(spread.reshape(per_slab, modes, LANES), axis=0).astype(
            state_ref.dtype
        )


def own_kernel(product_ref, query_ref, current_ref, medium_ref, gated_ref):
    for slab, lanes in enumerate(slabs_of(product_ref.shape[1])):
        medium = grouped(stored_halves(current_ref, slab), product_ref[:, lanes])
        medium_ref[:, lanes] = medium
        gated_ref[:, lanes] = gated_by(query_ref[:, lanes], medium)


def on_line(modes, width):
    return iota((modes, width), 0) == iota((modes, width), 1) % modes


def modal_parts(modal_refs, spread_ref, groups):
    first = lax.axis_index("dp") * groups
    base = pl.multiple_of(first // LANES * LANES, LANES)
    pieces = jnp.concatenate([ref[:, pl.ds(base, LANES)] for ref in modal_refs], axis=0)
    return dot(pieces, spread_ref[...])


def end_weights(lines, rates_ref, doc_ref, end_ref):
    block, width = end_ref.shape
    rate_line = jnp.sum(lines * rates_ref[...], axis=0, keepdims=True)
    left = (block - 1 - iota((block, LANES), 0)).astype(jnp.float32)
    keeps = doc_ref[...] == doc_ref[block - 1 : block, :]
    for lanes in slabs_of(width):
        weight = jnp.exp(-rate_line[:, lanes] * left)
        end_ref[:, lanes] = jnp.where(keeps, weight, 0.0).astype(jnp.bfloat16)


def first_kernel(*refs):
    *modal_refs, spread_ref, rates_ref, doc_ref, gated_ref, state_ref, end_ref = refs
    modes, width = state_ref.shape

    @pl.when(lax.axis_index("ctx") == 0)
    def _():
        lines = modal_parts(modal_refs, spread_ref, width // modes)
        end_weights(lines, rates_ref, doc_ref, end_ref)
        end_states(end_ref, gated_ref, state_ref)

    @pl.when(lax.axis_index("ctx") != 0)
    def _():
        state_ref[...] = jnp.zeros_like(state_ref)


def modal_kernel(*refs):
    *modal_refs, select_ref, spread_ref, rates_ref, doc_ref, _, end_ref, channels_ref = refs
    modes, width = channels_ref.shape[0] // 2, channels_ref.shape[1]
    lines = modal_parts(modal_refs, spread_ref, width // modes)
    end_weights(lines, rates_ref, doc_ref, end_ref)
    channels_ref[...] = dot(select_ref[...], lines.astype(jnp.bfloat16))


def modal_lines(channels_ref, modes, width):
    rate = channels_ref[:modes]
    scaled = channels_ref[modes:] * jnp.sqrt((1.0 - jnp.exp(-2.0 * rate)) / modes)
    chosen = on_line(modes, width)
    return [
        jnp.sum(jnp.where(chosen, part, 0.0), axis=0, keepdims=True) for part in (rate, scaled)
    ]


def response_kernel(channels_ref, starts_ref, rows_ref, through_ref, first_ref, far_ref):
    groups, block = rows_ref.shape
    modes, width = through_ref.shape
    ctx_place = lax.axis_index("ctx")
    rate_line, scaled_line = modal_lines(channels_ref, modes, width)
    lag = ((block - iota((block, LANES), 0)) % block).astype(jnp.float32)
    per_slab = LANES // modes
    gather = (iota((LANES, LANES), 0) // modes == iota((LANES, LANES), 1)).astype(jnp.bfloat16)
    for slab, lanes in enumerate(slabs_of(width)):
        terms = scaled_line[:, lanes] * jnp.exp(-rate_line[:, lanes] * lag)
        high = terms.astype(jnp.bfloat16)
        low = (terms - high.astype(jnp.float32)).astype(jnp.bfloat16)
        sums = jnp.transpose(dot(high, gather) + dot(low, gather))
        rows_ref[slab * per_slab : (slab + 1) * per_slab, :] = sums[:per_slab]
    decay = jnp.exp(-channels_ref[:modes] * block)
    own, prior = block_starts(starts_ref, ctx_place, block)
    none_own = jnp.sum(own, axis=1, keepdims=True) == 0.0
    none_prior = jnp.sum(prior, axis=1, keepdims=True) == 0.0
    through_ref[...] = jnp.where(none_own, decay, 0.0)
    first_ref[...] = jnp.where(none_own & (ctx_place == 1), decay, 0.0)
    far_ref[...] = jnp.where(none_prior, decay, 0.0)


def grouped(halves, values):
    rows = values.shape[0]
    half = rows // 2
    lane = iota((half, LANES), 1) // GROUP_CH
    results = []
    for part, chosen in enumerate(halves):
        turned = values if part == 0 else jnp.concatenate([values[half:], values[:half]], axis=0)
        product = dot(chosen, turned)
        result = product[:half]
        for k in range(1, chosen.shape[0] // half):
            result = jnp.where(lane == k, product[k * half : (k + 1) * half], result)
        results.append(result)
    return jnp.concatenate(results, axis=0)


def stored_halves(matrices_ref, slab):
    per_slab = LANES // GROUP_CH
    groups = slice(slab * per_slab, (slab + 1) * per_slab)
    half = matrices_ref.shape[1] // 2
    return [
        matrices_ref[groups, part * half : (part + 1) * half].reshape(per_slab * half, 2 * half)
        for part in range(2)
    ]


def gate_kernel(
    halo_ref, query_ref, previous_ref, medium_ref, end_ref, _, gated_ref, state_ref
):
    for slab, lanes in enumerate(slabs_of(halo_ref.shape[1])):
        medium = medium_ref[:, lanes] + grouped(
            stored_halves(previous_ref, slab), halo_ref[:, lanes]
        )
        gated_ref[:, lanes] = gated_by(query_ref[:, lanes], medium)
    end_states(end_ref, gated_ref, state_ref)


def local_kernel(gated_ref, rows_ref, same_ref, doc_ref, channels_ref, gain_ref, part_ref, carry_ref):
    block, width = part_ref.shape
    modes = channels_ref.shape[0] // 2
    per_slab = LANES // GROUP_CH
    half = block // 2
    same = [same_ref[:half, :], same_ref[half:, :]]
    rate_line, scaled_line = modal_lines(channels_ref, modes, width)
    since = (iota((block, LANES), 0) + 1).astype(jnp.float32)
    continues = doc_ref[...] == 0.0
    for slab, lanes in enumerate(slabs_of(width)):
        turned = [
            circulant(rows_ref[group : group + 1, :], block)
            for group in range(slab * per_slab, (slab + 1) * per_slab)
        ]
        halves = [jnp.concatenate([line * mask for line in turned], axis=0) for mask in same]
        gated = gated_ref[:, lanes]
        part_ref[:, lanes] = grouped(halves, gated) + gain_ref[:, lanes] * gated.astype(jnp.float32)
        weight = scaled_line[:, lanes] * jnp.exp(-rate_line[:, lanes] * since)
        carry_ref[:, lanes] = jnp.where(continues, weight, 0.0).astype(jnp.bfloat16)


def finish_kernel(
    four, part_ref, carry_ref, first_ref, far_ref, middle_ref, near_ref, through_ref, out_ref
):
    width = part_ref.shape[1]
    modes = near_ref.shape[0]
    per_slab = LANES // GROUP_CH
    diagonal = iota((LANES, LANES), 0) // modes == iota((LANES, LANES), 1) // GROUP_CH
    entering = near_ref[...].astype(jnp.float32)
    if four:
        place = lax.axis_index("ctx")
        entering += through_ref[...] * far_ref[...].astype(jnp.float32)
        entering = jnp.where(place == 3, entering, 0.0)
        entering += jnp.where(place == 1, first_ref[...].astype(jnp.float32), 0.0)
        entering += jnp.where(place == 2, middle_ref[...].astype(jnp.float32), 0.0)
    for slab in range(width // LANES):
        lanes = slice(slab * LANES, (slab + 1) * LANES)
        state = jnp.concatenate([entering[:, lanes]] * per_slab, axis=0)
        spread = jnp.where(diagonal, state, 0.0).astype(jnp.bfloat16)
        out_ref[:, lanes] = (part_ref[:, lanes] + dot(carry_ref[:, lanes], spread)).astype(
            out_ref.dtype
        )


def call(kernel, outs, *args, spaces=None, scratch=(), micros=0.3):
    spaces = spaces or [pltpu.VMEM] * len(args)
    return pl.pallas_call(
        kernel,
        out_shape=[jax.ShapeDtypeStruct(shape, dtype) for shape, dtype in outs],
        in_specs=[pl.BlockSpec(memory_space=space) for space in spaces],
        out_specs=[pl.BlockSpec(memory_space=pltpu.VMEM)] * len(outs),
        scratch_shapes=list(scratch),
        cost_estimate=pl.CostEstimate(
            flops=int(micros * 1e9), bytes_accessed=0, transcendentals=0
        ),
        compiler_params=pltpu.CompilerParams(vmem_limit_bytes=VMEM_BYTES),
    )(*args)


def shifted(array, axis, distance):
    size = lax.axis_size(axis)
    return lax.ppermute(array, axis, [(i, i + distance) for i in range(size - distance)])


def exchanged(array, axis, bit):
    return lax.ppermute(array, axis, [(i, i ^ bit) for i in range(lax.axis_size(axis))])


def cycled(array, cycle, crossing=()):
    fsdp_size, ctx_size = lax.axis_size("fsdp"), lax.axis_size("ctx")
    after = dict(zip(cycle, cycle[1:] + cycle[:1]))
    moves = []
    for core in range(fsdp_size):
        for place in range(ctx_size):
            other = (core ^ (place in crossing), after[place]) if place in after else (core ^ 1, place)
            moves.append((core * ctx_size + place, other[0] * ctx_size + other[1]))
    return lax.ppermute(array, ("fsdp", "ctx"), moves)


def entering_states(state, through):
    size = lax.axis_size("ctx")
    total, factor, distance = state.astype(jnp.float32), through, 1
    while distance < size:
        total = total + factor * shifted(total, "ctx", distance)
        factor = factor * shifted(factor, "ctx", distance)
        distance *= 2
    return shifted(total, "ctx", 1)


def body(
    query_stream,
    key_stream,
    value_stream,
    document_starts,
    medium_taps,
    modal_rate,
    modal_residue,
    skip_gain,
):
    tokens, width = query_stream.shape[1:]
    groups = width // GROUP_CH
    fsdp_size, dp_size = lax.axis_size("fsdp"), lax.axis_size("dp")
    ctx_size = lax.axis_size("ctx")
    modes = modal_rate.shape[1] * dp_size
    assert fsdp_size == 2 and tokens == medium_taps.shape[1] * fsdp_size
    assert modes == GROUP_CH and modal_rate.shape[1] <= 8
    taps = medium_taps.T
    half = jnp.bfloat16
    rows = modal_rate.shape[0]
    inputs = [
        key_stream[0],
        value_stream[0],
        modal_rate.T,
        modal_residue.T,
        query_stream[0],
        taps,
        document_starts,
        skip_gain.reshape(1, width),
    ]
    product, modal, spread, select, rates, query, own_taps, starts, gain = call(
        prepare_kernel,
        [
            ((tokens, width), half),
            ((16, rows), half),
            ((LANES, width), half),
            ((2 * modes, 16 * dp_size), half),
            ((16 * dp_size, width), jnp.float32),
        ]
        + [(a.shape, a.dtype) for a in inputs[4:]],
        *[pltpu.with_memory_space_constraint(a, pltpu.HBM) for a in inputs],
        spaces=[pltpu.HBM] * len(inputs),
        scratch=[pltpu.VMEM(a.shape, a.dtype) for a in inputs[:4]]
        + [pltpu.SemaphoreType.DMA((len(inputs),))],
    )
    halo = lax.ppermute(product, "ctx", [(i, (i + 1) % ctx_size) for i in range(ctx_size)])
    other_taps = exchanged(taps, "fsdp", 1)
    modal = [modal] + [exchanged(modal, "dp", bit) for bit in reversed(range(1, dp_size))]
    square = ((groups, tokens, tokens), half)
    previous, current, same, documents = call(
        medium_kernel,
        [square, square, ((tokens, tokens), half), ((tokens, tokens), jnp.float32)],
        own_taps,
        other_taps,
        starts,
        scratch=[pltpu.VMEM((LANES, tokens), jnp.float32)],
    )
    medium, gated_own = call(
        own_kernel,
        [((tokens, width), jnp.float32), ((tokens, width), half)],
        product,
        query,
        current,
    )
    states = ((modes, width), jnp.float32)
    (state_own,) = call(
        first_kernel,
        [((modes, width), half)],
        *modal,
        spread,
        rates,
        documents,
        gated_own,
        scratch=[pltpu.VMEM((tokens, width), half)],
    )
    end, channels = call(
        modal_kernel,
        [((tokens, width), half), ((2 * modes, width), jnp.float32)],
        *modal,
        select,
        spread,
        rates,
        documents,
        state_own,
    )
    four = ctx_size == 4
    first = cycled(state_own, [0, 1]) if four else state_own
    response, through, first_through, far_through = call(
        response_kernel,
        [((groups, tokens), jnp.float32), states, states, states],
        channels,
        starts,
    )
    gated, state = call(
        gate_kernel,
        [((tokens, width), half), ((modes, width), half)],
        halo,
        query,
        previous,
        medium,
        end,
        response,
    )
    if four:
        both = state.astype(jnp.float32) + first_through * first.astype(jnp.float32)
        both = both.astype(half)
        near = cycled(state, [2, 3], ())
        middle = cycled(both, [1, 2], (2, ))
        far = cycled(both, [1, 3, 2], (2, ))
    else:
        near = middle = far = entering_states(state, through)
    part, carry = call(
        local_kernel,
        [((tokens, width), jnp.float32), ((tokens, width), half)],
        gated,
        response,
        same,
        documents,
        channels,
        gain,
    )
    (out,) = call(
        functools.partial(finish_kernel, four),
        [((tokens, width), half)],
        part,
        carry,
        first,
        far,
        middle,
        near,
        far_through,
    )
    return out[None]


def solution(mesh):
    return jax.shard_map(
        body,
        mesh=mesh,
        in_specs=(
            P(None, "ctx", ("fsdp", "dp")),
            P(None, "ctx", ("fsdp", "dp")),
            P(None, "ctx", ("fsdp", "dp")),
            P(),
            P(None, "fsdp"),
            P("fsdp", "dp"),
            P("fsdp", "dp"),
            P(("fsdp", "dp")),
        ),
        out_specs=P(None, "ctx", ("fsdp", "dp")),
        check_vma=False,
    )
```

```python
import functools

import jax
import jax.numpy as jnp
from jax import lax
from jax.experimental import pallas as pl
from jax.experimental.pallas import tpu as pltpu
from jax.sharding import PartitionSpec as P

GROUP_CH = 16
LANES = 128
VMEM_BYTES = 32 * 1024 * 1024


def iota(shape, dim):
    return lax.broadcasted_iota(jnp.int32, shape, dim)


def dot(a, b, contract=((1,), (0,))):
    return lax.dot_general(a, b, (contract, ((), ())), preferred_element_type=jnp.float32)


def prepare_kernel(
    key_hbm,
    value_hbm,
    rate_hbm,
    residue_hbm,
    query_hbm,
    taps_hbm,
    starts_hbm,
    gain_hbm,
    product_ref,
    modal_ref,
    spread_ref,
    select_ref,
    rates_ref,
    query_ref,
    taps_ref,
    starts_ref,
    gain_ref,
    key_ref,
    value_ref,
    rate_ref,
    residue_ref,
    arrived,
):
    pairs = (
        (key_hbm, key_ref),
        (value_hbm, value_ref),
        (rate_hbm, rate_ref),
        (residue_hbm, residue_ref),
        (query_hbm, query_ref),
        (taps_hbm, taps_ref),
        (starts_hbm, starts_ref),
        (gain_hbm, gain_ref),
    )
    copies = [
        pltpu.make_async_copy(source, target, arrived.at[i])
        for i, (source, target) in enumerate(pairs)
    ]
    for copy in copies:
        copy.start()
    dp_place = lax.axis_index("dp")
    modes, width = select_ref.shape[0] // 2, spread_ref.shape[1]
    per_part = rate_ref.shape[0]
    lines = select_ref.shape[1]
    pieces = lines // 16
    line, mode = iota((2 * modes, lines), 1), iota((2 * modes, lines), 0)
    within = line % 16
    held = jnp.where(mode < modes, within, within - 8)
    owner = jnp.bitwise_xor(dp_place, (pieces - line // 16) % pieces)
    wanted = owner * per_part + held == jnp.where(mode < modes, mode, mode - modes)
    select_ref[...] = ((held >= 0) & (held < per_part) & wanted).astype(jnp.bfloat16)
    line, mode = iota((lines, width), 0), iota((lines, width), 1) % modes
    within = line % 16
    owner = jnp.bitwise_xor(dp_place, (pieces - line // 16) % pieces)
    rates_ref[...] = ((within < per_part) & (owner * per_part + within == mode)).astype(
        jnp.float32
    )
    first = dp_place * (width // modes) % LANES
    spread_ref[...] = (
        iota((LANES, width), 0) == first + iota((LANES, width), 1) // modes
    ).astype(jnp.bfloat16)
    for copy in copies[:4]:
        copy.wait()
    product_ref[...] = (
        key_ref[...].astype(jnp.float32) * value_ref[...].astype(jnp.float32)
    ).astype(jnp.bfloat16)
    rate = rate_ref[...].astype(jnp.float32)
    residue = residue_ref[...].astype(jnp.float32)
    gap = jnp.zeros((8 - rate.shape[0], rate.shape[1]), jnp.float32)
    modal_ref[...] = jnp.concatenate([rate, gap, residue, gap], axis=0).astype(jnp.bfloat16)
    for copy in copies[4:]:
        copy.wait()


def block_starts(starts_ref, ctx_place, block):
    prior_place = jnp.maximum(ctx_place - 1, 0)
    return [
        starts_ref[:, pl.ds(pl.multiple_of(place * block, block), block)].astype(jnp.float32)
        for place in (ctx_place, prior_place)
    ]


def document_masks(own, prior, block):
    row, col = iota((block, block), 0), iota((block, block), 1)
    both = jnp.concatenate(
        [jnp.broadcast_to(own, (8, block)), jnp.broadcast_to(prior, (8, block))], axis=0
    ).astype(jnp.bfloat16)
    upto = (row <= col).astype(jnp.bfloat16)
    doc_row = dot(both, upto)[0:1]
    after_row = dot(both, (row > col).astype(jnp.bfloat16))[8:9]
    doc_col = dot(
        upto, jnp.broadcast_to(own, (block, block)).astype(jnp.bfloat16), ((0,), (1,))
    )
    current = (row >= col) & (doc_col == doc_row)
    previous = (col > row) & (doc_col == 0.0) & (after_row == 0.0)
    return doc_col, current, previous


def circulant(row, block):
    return pltpu.roll(
        jnp.broadcast_to(row, (block // 2, block)), 0, 1, stride=1, stride_axis=0
    ).astype(jnp.bfloat16)


def folded(mask, block):
    half = block // 2
    lower = pltpu.roll(mask[half:], half, 1)
    return [mask[:half].astype(jnp.bfloat16), lower.astype(jnp.bfloat16)]


def medium_kernel(
    taps_ref,
    other_taps_ref,
    starts_ref,
    previous_ref,
    current_ref,
    same_ref,
    doc_ref,
    clear_ref,
    rows_ref,
):
    fsdp_place, ctx_place, dp_place = (lax.axis_index(axis) for axis in ("fsdp", "ctx", "dp"))
    groups, block = previous_ref.shape[0], previous_ref.shape[1]
    half = taps_ref.shape[0]
    first = (fsdp_place * lax.axis_size("dp") + dp_place) * groups
    base = pl.multiple_of(first // LANES * LANES, LANES)
    tap, lane = iota((half, block), 0), iota((half, block), 1)
    lag_of_lane = (block - lane) % block
    own_place = (tap + fsdp_place * half == lag_of_lane).astype(jnp.bfloat16)
    other_place = (tap + (1 - fsdp_place) * half == lag_of_lane).astype(jnp.bfloat16)
    rows_ref[...] = dot(taps_ref[:, pl.ds(base, LANES)], own_place, ((0,), (0,))) + dot(
        other_taps_ref[:, pl.ds(base, LANES)], other_place, ((0,), (0,))
    )
    own, prior = block_starts(starts_ref, ctx_place, block)
    doc_col, current, previous = document_masks(own, prior, block)
    current = folded(current.astype(jnp.float32), block)
    previous = folded((previous & (ctx_place > 0)).astype(jnp.float32), block)
    halves = [slice(0, block // 2), slice(block // 2, block)]
    doc_ref[...] = doc_col
    for line, begun in enumerate((own, prior)):
        none = jnp.sum(begun, axis=1, keepdims=True) == 0.0
        clear_ref[line : line + 1, :] = jnp.where(none, jnp.ones((1, block), jnp.float32), 0.0)
    for part, rows in enumerate(halves):
        same_ref[rows, :] = current[part]
    for group in range(groups):
        turned = circulant(rows_ref[pl.ds(first - base + group, 1), :], block)
        for part, rows in enumerate(halves):
            previous_ref[group, rows, :] = turned * previous[part]
            current_ref[group, rows, :] = turned * current[part]


def slabs_of(width):
    return [slice(at, at + LANES) for at in range(0, width, LANES)]


def gated_by(query, medium):
    return (
        query.astype(jnp.float32) * medium.astype(jnp.bfloat16).astype(jnp.float32)
    ).astype(jnp.bfloat16)


def end_states(end_ref, gated_ref, state_ref):
    modes, width = state_ref.shape
    per_slab = LANES // GROUP_CH
    diagonal = iota((LANES, LANES), 0) // modes == iota((LANES, LANES), 1) // GROUP_CH
    for lanes in slabs_of(width):
        spread = jnp.where(
            diagonal, dot(end_ref[:, lanes], gated_ref[:, lanes], ((0,), (0,))), 0.0
        )
        state_ref[:, lanes] = jnp.sum(spread.reshape(per_slab, modes, LANES), axis=0).astype(
            state_ref.dtype
        )


def own_kernel(product_ref, query_ref, current_ref, medium_ref, gated_ref):
    for slab, lanes in enumerate(slabs_of(product_ref.shape[1])):
        medium = grouped(stored_halves(current_ref, slab), product_ref[:, lanes])
        medium_ref[:, lanes] = medium
        gated_ref[:, lanes] = gated_by(query_ref[:, lanes], medium)


def on_line(modes, width):
    return iota((modes, width), 0) == iota((modes, width), 1) % modes


def modal_parts(modal_refs, spread_ref, groups):
    first = lax.axis_index("dp") * groups
    base = pl.multiple_of(first // LANES * LANES, LANES)
    pieces = jnp.concatenate([ref[:, pl.ds(base, LANES)] for ref in modal_refs], axis=0)
    return dot(pieces, spread_ref[...])


def end_weights(lines, rates_ref, doc_ref, end_ref):
    block, width = end_ref.shape
    rate_line = jnp.sum(lines * rates_ref[...], axis=0, keepdims=True)
    left = (block - 1 - iota((block, LANES), 0)).astype(jnp.float32)
    keeps = doc_ref[...] == doc_ref[block - 1 : block, :]
    for lanes in slabs_of(width):
        weight = jnp.exp(-rate_line[:, lanes] * left)
        end_ref[:, lanes] = jnp.where(keeps, weight, 0.0).astype(jnp.bfloat16)


def first_kernel(*refs):
    *modal_refs, spread_ref, rates_ref, doc_ref, gated_ref, state_ref, end_ref = refs
    modes, width = state_ref.shape

    @pl.when(lax.axis_index("ctx") == 0)
    def _():
        lines = modal_parts(modal_refs, spread_ref, width // modes)
        end_weights(lines, rates_ref, doc_ref, end_ref)
        end_states(end_ref, gated_ref, state_ref)

    @pl.when(lax.axis_index("ctx") != 0)
    def _():
        state_ref[...] = jnp.zeros_like(state_ref)


def modal_kernel(four, *refs):
    *refs, end_ref, channels_ref, through_ref, far_ref = refs
    *modal_refs, select_ref, spread_ref, rates_ref, doc_ref, clear_ref, _ = refs
    modes, width = channels_ref.shape[0] // 2, channels_ref.shape[1]
    lines = modal_parts(modal_refs, spread_ref, width // modes)
    end_weights(lines, rates_ref, doc_ref, end_ref)
    by_channel = dot(select_ref[...], lines.astype(jnp.bfloat16))
    channels_ref[...] = by_channel
    wanted = (lax.axis_index("ctx") == 1).astype(jnp.float32) if four else 1.0
    for lanes in slabs_of(width):
        decay = jnp.exp(-by_channel[:modes, lanes] * end_ref.shape[0])
        through_ref[:, lanes] = decay * (clear_ref[0:1, :] * wanted)
        far_ref[:, lanes] = decay * clear_ref[1:2, :]


def modal_lines(channels_ref, modes, width):
    rate = channels_ref[:modes]
    scaled = channels_ref[modes:] * jnp.sqrt((1.0 - jnp.exp(-2.0 * rate)) / modes)
    chosen = on_line(modes, width)
    return [
        jnp.sum(jnp.where(chosen, part, 0.0), axis=0, keepdims=True) for part in (rate, scaled)
    ]


def response_kernel(channels_ref, _, rows_ref):
    groups, block = rows_ref.shape
    modes, width = channels_ref.shape[0] // 2, channels_ref.shape[1]
    rate_line, scaled_line = modal_lines(channels_ref, modes, width)
    lag = ((block - iota((block, LANES), 0)) % block).astype(jnp.float32)
    per_slab = LANES // modes
    gather = (iota((LANES, LANES), 0) // modes == iota((LANES, LANES), 1)).astype(jnp.bfloat16)
    for slab, lanes in enumerate(slabs_of(width)):
        terms = scaled_line[:, lanes] * jnp.exp(-rate_line[:, lanes] * lag)
        high = terms.astype(jnp.bfloat16)
        low = (terms - high.astype(jnp.float32)).astype(jnp.bfloat16)
        sums = jnp.transpose(dot(high, gather) + dot(low, gather))
        rows_ref[slab * per_slab : (slab + 1) * per_slab, :] = sums[:per_slab]


def grouped(halves, values):
    rows = values.shape[0]
    half = rows // 2
    lane = iota((half, LANES), 1) // GROUP_CH
    results = []
    for part, chosen in enumerate(halves):
        turned = values if part == 0 else jnp.concatenate([values[half:], values[:half]], axis=0)
        product = dot(chosen, turned)
        result = product[:half]
        for k in range(1, chosen.shape[0] // half):
            result = jnp.where(lane == k, product[k * half : (k + 1) * half], result)
        results.append(result)
    return jnp.concatenate(results, axis=0)


def stored_halves(matrices_ref, slab):
    per_slab = LANES // GROUP_CH
    groups = slice(slab * per_slab, (slab + 1) * per_slab)
    half = matrices_ref.shape[1] // 2
    return [
        matrices_ref[groups, part * half : (part + 1) * half].reshape(per_slab * half, 2 * half)
        for part in range(2)
    ]


def gate_kernel(
    halo_ref, query_ref, previous_ref, medium_ref, end_ref, _, gated_ref, state_ref
):
    for slab, lanes in enumerate(slabs_of(halo_ref.shape[1])):
        medium = medium_ref[:, lanes] + grouped(
            stored_halves(previous_ref, slab), halo_ref[:, lanes]
        )
        gated_ref[:, lanes] = gated_by(query_ref[:, lanes], medium)
    end_states(end_ref, gated_ref, state_ref)


def local_kernel(
    gated_ref, rows_ref, same_ref, doc_ref, channels_ref, gain_ref, part_ref, carry_ref
):
    block, width = part_ref.shape
    modes = channels_ref.shape[0] // 2
    per_slab = LANES // GROUP_CH
    half = block // 2
    same = [same_ref[:half, :], same_ref[half:, :]]
    rate_line, scaled_line = modal_lines(channels_ref, modes, width)
    since = (iota((block, LANES), 0) + 1).astype(jnp.float32)
    continues = doc_ref[...] == 0.0
    for slab, lanes in enumerate(slabs_of(width)):
        turned = [
            circulant(rows_ref[group : group + 1, :], block)
            for group in range(slab * per_slab, (slab + 1) * per_slab)
        ]
        halves = [jnp.concatenate([line * mask for line in turned], axis=0) for mask in same]
        gated = gated_ref[:, lanes]
        part_ref[:, lanes] = grouped(halves, gated) + gain_ref[:, lanes] * gated.astype(jnp.float32)
        weight = scaled_line[:, lanes] * jnp.exp(-rate_line[:, lanes] * since)
        carry_ref[:, lanes] = jnp.where(continues, weight, 0.0).astype(jnp.bfloat16)


def finish_kernel(
    four, part_ref, carry_ref, first_ref, far_ref, middle_ref, near_ref, through_ref, out_ref
):
    width = part_ref.shape[1]
    modes = near_ref.shape[0]
    per_slab = LANES // GROUP_CH
    diagonal = iota((LANES, LANES), 0) // modes == iota((LANES, LANES), 1) // GROUP_CH
    entering = near_ref[...].astype(jnp.float32)
    if four:
        place = lax.axis_index("ctx")
        entering += through_ref[...] * far_ref[...].astype(jnp.float32)
        entering = jnp.where(place == 3, entering, 0.0)
        entering += jnp.where(place == 1, first_ref[...].astype(jnp.float32), 0.0)
        entering += jnp.where(place == 2, middle_ref[...].astype(jnp.float32), 0.0)
    for slab in range(width // LANES):
        lanes = slice(slab * LANES, (slab + 1) * LANES)
        state = jnp.concatenate([entering[:, lanes]] * per_slab, axis=0)
        spread = jnp.where(diagonal, state, 0.0).astype(jnp.bfloat16)
        out_ref[:, lanes] = (part_ref[:, lanes] + dot(carry_ref[:, lanes], spread)).astype(
            out_ref.dtype
        )


def call(kernel, outs, *args, spaces=None, scratch=(), micros=0.3):
    spaces = spaces or [pltpu.VMEM] * len(args)
    return pl.pallas_call(
        kernel,
        out_shape=[jax.ShapeDtypeStruct(shape, dtype) for shape, dtype in outs],
        in_specs=[pl.BlockSpec(memory_space=space) for space in spaces],
        out_specs=[pl.BlockSpec(memory_space=pltpu.VMEM)] * len(outs),
        scratch_shapes=list(scratch),
        cost_estimate=pl.CostEstimate(
            flops=int(micros * 1e9), bytes_accessed=0, transcendentals=0
        ),
        compiler_params=pltpu.CompilerParams(vmem_limit_bytes=VMEM_BYTES),
    )(*args)


def shifted(array, axis, distance):
    size = lax.axis_size(axis)
    return lax.ppermute(array, axis, [(i, i + distance) for i in range(size - distance)])


def exchanged(array, axis, bit):
    return lax.ppermute(array, axis, [(i, i ^ bit) for i in range(lax.axis_size(axis))])


def cycled(array, cycle, crossing=()):
    fsdp_size, ctx_size = lax.axis_size("fsdp"), lax.axis_size("ctx")
    after = dict(zip(cycle, cycle[1:] + cycle[:1]))
    moves = []
    for core in range(fsdp_size):
        for place in range(ctx_size):
            other = (core ^ (place in crossing), after[place]) if place in after else (core ^ 1, place)
            moves.append((core * ctx_size + place, other[0] * ctx_size + other[1]))
    return lax.ppermute(array, ("fsdp", "ctx"), moves)


def entering_states(state, through):
    size = lax.axis_size("ctx")
    total, factor, distance = state.astype(jnp.float32), through, 1
    while distance < size:
        total = total + factor * shifted(total, "ctx", distance)
        factor = factor * shifted(factor, "ctx", distance)
        distance *= 2
    return shifted(total, "ctx", 1)


def body(
    query_stream,
    key_stream,
    value_stream,
    document_starts,
    medium_taps,
    modal_rate,
    modal_residue,
    skip_gain,
):
    tokens, width = query_stream.shape[1:]
    groups = width // GROUP_CH
    fsdp_size, dp_size = lax.axis_size("fsdp"), lax.axis_size("dp")
    ctx_size = lax.axis_size("ctx")
    modes = modal_rate.shape[1] * dp_size
    assert fsdp_size == 2 and tokens == medium_taps.shape[1] * fsdp_size
    assert modes == GROUP_CH and modal_rate.shape[1] <= 8
    taps = medium_taps.T
    half = jnp.bfloat16
    rows = modal_rate.shape[0]
    inputs = [
        key_stream[0],
        value_stream[0],
        modal_rate.T,
        modal_residue.T,
        query_stream[0],
        taps,
        document_starts,
        skip_gain.reshape(1, width),
    ]
    product, modal, spread, select, rates, query, own_taps, starts, gain = call(
        prepare_kernel,
        [
            ((tokens, width), half),
            ((16, rows), half),
            ((LANES, width), half),
            ((2 * modes, 16 * dp_size), half),
            ((16 * dp_size, width), jnp.float32),
        ]
        + [(a.shape, a.dtype) for a in inputs[4:]],
        *[pltpu.with_memory_space_constraint(a, pltpu.HBM) for a in inputs],
        spaces=[pltpu.HBM] * len(inputs),
        scratch=[pltpu.VMEM(a.shape, a.dtype) for a in inputs[:4]]
        + [pltpu.SemaphoreType.DMA((len(inputs),))],
    )
    halo = lax.ppermute(product, "ctx", [(i, (i + 1) % ctx_size) for i in range(ctx_size)])
    other_taps = exchanged(taps, "fsdp", 1)
    modal = [modal] + [exchanged(modal, "dp", bit) for bit in reversed(range(1, dp_size))]
    square = ((groups, tokens, tokens), half)
    previous, current, same, documents, clear = call(
        medium_kernel,
        [
            square,
            square,
            ((tokens, tokens), half),
            ((tokens, tokens), jnp.float32),
            ((2, tokens), jnp.float32),
        ],
        own_taps,
        other_taps,
        starts,
        scratch=[pltpu.VMEM((LANES, tokens), jnp.float32)],
    )
    medium, gated_own = call(
        own_kernel,
        [((tokens, width), jnp.float32), ((tokens, width), half)],
        product,
        query,
        current,
    )
    states = ((modes, width), jnp.float32)
    four = ctx_size == 4
    (state_own,) = call(
        first_kernel,
        [((modes, width), half)],
        *modal,
        spread,
        rates,
        documents,
        gated_own,
        scratch=[pltpu.VMEM((tokens, width), half)],
    )
    end, channels, through, far_through = call(
        functools.partial(modal_kernel, four),
        [((tokens, width), half), ((2 * modes, width), jnp.float32), states, states],
        *modal,
        select,
        spread,
        rates,
        documents,
        clear,
        state_own,
    )
    first = cycled(state_own, [0, 1], (1,)) if four else state_own
    (response,) = call(
        response_kernel, [((groups, tokens), jnp.float32)], channels, state_own
    )
    gated, state = call(
        gate_kernel,
        [((tokens, width), half), ((modes, width), half)],
        halo,
        query,
        previous,
        medium,
        end,
        response,
    )
    if four:
        both = state.astype(jnp.float32) + through * first.astype(jnp.float32)
        both = both.astype(half)
        near = cycled(state, [2, 3], ())
        middle = cycled(both, [1, 2], (2, ))
        far = cycled(both, [1, 3, 2], (2, ))
    else:
        near = middle = far = entering_states(state, through)
    part, carry = call(
        local_kernel,
        [((tokens, width), jnp.float32), ((tokens, width), half)],
        gated,
        response,
        same,
        documents,
        channels,
        gain,
    )
    (out,) = call(
        functools.partial(finish_kernel, four),
        [((tokens, width), half)],
        part,
        carry,
        first,
        far,
        middle,
        near,
        far_through,
    )
    return out[None]


def solution(mesh):
    return jax.shard_map(
        body,
        mesh=mesh,
        in_specs=(
            P(None, "ctx", ("fsdp", "dp")),
            P(None, "ctx", ("fsdp", "dp")),
            P(None, "ctx", ("fsdp", "dp")),
            P(),
            P(None, "fsdp"),
            P("fsdp", "dp"),
            P("fsdp", "dp"),
            P(("fsdp", "dp")),
        ),
        out_specs=P(None, "ctx", ("fsdp", "dp")),
        check_vma=False,
    )
```

```python
import functools

import jax
import jax.numpy as jnp
from jax import lax
from jax.experimental import pallas as pl
from jax.experimental.pallas import tpu as pltpu
from jax.sharding import PartitionSpec as P

GROUP_CH = 16
LANES = 128
VMEM_BYTES = 32 * 1024 * 1024


def iota(shape, dim):
    return lax.broadcasted_iota(jnp.int32, shape, dim)


def dot(a, b, contract=((1,), (0,))):
    return lax.dot_general(a, b, (contract, ((), ())), preferred_element_type=jnp.float32)


def prepare_kernel(
    key_hbm,
    value_hbm,
    rate_hbm,
    residue_hbm,
    query_hbm,
    taps_hbm,
    starts_hbm,
    gain_hbm,
    product_ref,
    modal_ref,
    spread_ref,
    select_ref,
    rates_ref,
    query_ref,
    taps_ref,
    starts_ref,
    gain_ref,
    key_ref,
    value_ref,
    rate_ref,
    residue_ref,
    arrived,
):
    pairs = (
        (key_hbm, key_ref),
        (value_hbm, value_ref),
        (rate_hbm, rate_ref),
        (residue_hbm, residue_ref),
        (query_hbm, query_ref),
        (taps_hbm, taps_ref),
        (starts_hbm, starts_ref),
        (gain_hbm, gain_ref),
    )
    copies = [
        pltpu.make_async_copy(source, target, arrived.at[i])
        for i, (source, target) in enumerate(pairs)
    ]
    for copy in copies:
        copy.start()
    dp_place = lax.axis_index("dp")
    modes, width = select_ref.shape[0] // 2, spread_ref.shape[1]
    per_part = rate_ref.shape[0]
    lines = select_ref.shape[1]
    pieces = lines // 16
    line, mode = iota((2 * modes, lines), 1), iota((2 * modes, lines), 0)
    within = line % 16
    held = jnp.where(mode < modes, within, within - 8)
    owner = jnp.bitwise_xor(dp_place, (pieces - line // 16) % pieces)
    wanted = owner * per_part + held == jnp.where(mode < modes, mode, mode - modes)
    select_ref[...] = ((held >= 0) & (held < per_part) & wanted).astype(jnp.bfloat16)
    line, mode = iota((lines, width), 0), iota((lines, width), 1) % modes
    within = line % 16
    owner = jnp.bitwise_xor(dp_place, (pieces - line // 16) % pieces)
    rates_ref[...] = ((within < per_part) & (owner * per_part + within == mode)).astype(
        jnp.float32
    )
    first = dp_place * (width // modes) % LANES
    spread_ref[...] = (
        iota((LANES, width), 0) == first + iota((LANES, width), 1) // modes
    ).astype(jnp.bfloat16)
    for copy in copies[:4]:
        copy.wait()
    product_ref[...] = (
        key_ref[...].astype(jnp.float32) * value_ref[...].astype(jnp.float32)
    ).astype(jnp.bfloat16)
    rate = rate_ref[...].astype(jnp.float32)
    residue = residue_ref[...].astype(jnp.float32)
    gap = jnp.zeros((8 - rate.shape[0], rate.shape[1]), jnp.float32)
    modal_ref[...] = jnp.concatenate([rate, gap, residue, gap], axis=0).astype(jnp.bfloat16)
    for copy in copies[4:]:
        copy.wait()


def block_starts(starts_ref, ctx_place, block):
    prior_place = jnp.maximum(ctx_place - 1, 0)
    return [
        starts_ref[:, pl.ds(pl.multiple_of(place * block, block), block)].astype(jnp.float32)
        for place in (ctx_place, prior_place)
    ]


def document_masks(own, prior, block):
    row, col = iota((block, block), 0), iota((block, block), 1)
    both = jnp.concatenate(
        [jnp.broadcast_to(own, (8, block)), jnp.broadcast_to(prior, (8, block))], axis=0
    ).astype(jnp.bfloat16)
    upto = (row <= col).astype(jnp.bfloat16)
    doc_row = dot(both, upto)[0:1]
    after_row = dot(both, (row > col).astype(jnp.bfloat16))[8:9]
    doc_col = dot(
        upto, jnp.broadcast_to(own, (block, block)).astype(jnp.bfloat16), ((0,), (1,))
    )
    current = (row >= col) & (doc_col == doc_row)
    previous = (col > row) & (doc_col == 0.0) & (after_row == 0.0)
    return doc_col, current, previous


def circulant(row, block):
    return pltpu.roll(
        jnp.broadcast_to(row, (block // 2, block)), 0, 1, stride=1, stride_axis=0
    ).astype(jnp.bfloat16)


def folded(mask, block):
    half = block // 2
    lower = pltpu.roll(mask[half:], half, 1)
    return [mask[:half].astype(jnp.bfloat16), lower.astype(jnp.bfloat16)]


def medium_kernel(
    taps_ref,
    other_taps_ref,
    starts_ref,
    previous_ref,
    current_ref,
    same_ref,
    doc_ref,
    clear_ref,
    rows_ref,
):
    fsdp_place, ctx_place, dp_place = (lax.axis_index(axis) for axis in ("fsdp", "ctx", "dp"))
    groups, block = previous_ref.shape[0], previous_ref.shape[1]
    half = taps_ref.shape[0]
    first = (fsdp_place * lax.axis_size("dp") + dp_place) * groups
    base = pl.multiple_of(first // LANES * LANES, LANES)
    tap, lane = iota((half, block), 0), iota((half, block), 1)
    lag_of_lane = (block - lane) % block
    own_place = (tap + fsdp_place * half == lag_of_lane).astype(jnp.bfloat16)
    other_place = (tap + (1 - fsdp_place) * half == lag_of_lane).astype(jnp.bfloat16)
    rows_ref[...] = dot(taps_ref[:, pl.ds(base, LANES)], own_place, ((0,), (0,))) + dot(
        other_taps_ref[:, pl.ds(base, LANES)], other_place, ((0,), (0,))
    )
    own, prior = block_starts(starts_ref, ctx_place, block)
    doc_col, current, previous = document_masks(own, prior, block)
    current = folded(current.astype(jnp.float32), block)
    previous = folded((previous & (ctx_place > 0)).astype(jnp.float32), block)
    halves = [slice(0, block // 2), slice(block // 2, block)]
    doc_ref[...] = doc_col
    for line, begun in enumerate((own, prior)):
        none = jnp.sum(begun, axis=1, keepdims=True) == 0.0
        clear_ref[line : line + 1, :] = jnp.where(none, jnp.ones((1, block), jnp.float32), 0.0)
    for part, rows in enumerate(halves):
        same_ref[rows, :] = current[part]
    for group in range(groups):
        turned = circulant(rows_ref[pl.ds(first - base + group, 1), :], block)
        for part, rows in enumerate(halves):
            previous_ref[group, rows, :] = turned * previous[part]
            current_ref[group, rows, :] = turned * current[part]


def slabs_of(width):
    return [slice(at, at + LANES) for at in range(0, width, LANES)]


def gated_by(query, medium):
    return (
        query.astype(jnp.float32) * medium.astype(jnp.bfloat16).astype(jnp.float32)
    ).astype(jnp.bfloat16)


def end_states(end_ref, gated_ref, state_ref):
    modes, width = state_ref.shape
    per_slab = LANES // GROUP_CH
    diagonal = iota((LANES, LANES), 0) // modes == iota((LANES, LANES), 1) // GROUP_CH
    for lanes in slabs_of(width):
        spread = jnp.where(
            diagonal, dot(end_ref[:, lanes], gated_ref[:, lanes], ((0,), (0,))), 0.0
        )
        state_ref[:, lanes] = jnp.sum(spread.reshape(per_slab, modes, LANES), axis=0).astype(
            state_ref.dtype
        )


def own_kernel(product_ref, query_ref, current_ref, medium_ref, gated_ref):
    for slab, lanes in enumerate(slabs_of(product_ref.shape[1])):
        medium = grouped(stored_halves(current_ref, slab), product_ref[:, lanes])
        medium_ref[:, lanes] = medium
        gated_ref[:, lanes] = gated_by(query_ref[:, lanes], medium)


def on_line(modes, width):
    return iota((modes, width), 0) == iota((modes, width), 1) % modes


def modal_parts(modal_refs, spread_ref, groups):
    first = lax.axis_index("dp") * groups
    base = pl.multiple_of(first // LANES * LANES, LANES)
    pieces = jnp.concatenate([ref[:, pl.ds(base, LANES)] for ref in modal_refs], axis=0)
    return dot(pieces, spread_ref[...])


def end_weights(lines, rates_ref, doc_ref, end_ref):
    block, width = end_ref.shape
    rate_line = jnp.sum(lines * rates_ref[...], axis=0, keepdims=True)
    left = (block - 1 - iota((block, LANES), 0)).astype(jnp.float32)
    keeps = doc_ref[...] == doc_ref[block - 1 : block, :]
    for lanes in slabs_of(width):
        weight = jnp.exp(-rate_line[:, lanes] * left)
        end_ref[:, lanes] = jnp.where(keeps, weight, 0.0).astype(jnp.bfloat16)


def first_kernel(*refs):
    *modal_refs, spread_ref, rates_ref, doc_ref, gated_ref, state_ref, end_ref = refs
    modes, width = state_ref.shape

    @pl.when(lax.axis_index("ctx") == 0)
    def _():
        lines = modal_parts(modal_refs, spread_ref, width // modes)
        end_weights(lines, rates_ref, doc_ref, end_ref)
        end_states(end_ref, gated_ref, state_ref)

    @pl.when(lax.axis_index("ctx") != 0)
    def _():
        state_ref[...] = jnp.zeros_like(state_ref)


def modal_kernel(four, *refs):
    *refs, end_ref, channels_ref, through_ref, far_ref = refs
    *modal_refs, select_ref, spread_ref, rates_ref, doc_ref, clear_ref, _ = refs
    modes, width = channels_ref.shape[0] // 2, channels_ref.shape[1]
    lines = modal_parts(modal_refs, spread_ref, width // modes)
    end_weights(lines, rates_ref, doc_ref, end_ref)
    by_channel = dot(select_ref[...], lines.astype(jnp.bfloat16))
    channels_ref[...] = by_channel
    wanted = (lax.axis_index("ctx") == 1).astype(jnp.float32) if four else 1.0
    for lanes in slabs_of(width):
        decay = jnp.exp(-by_channel[:modes, lanes] * end_ref.shape[0])
        through_ref[:, lanes] = decay * (clear_ref[0:1, :] * wanted)
        far_ref[:, lanes] = decay * clear_ref[1:2, :]


def modal_lines(channels_ref, modes, width):
    rate = channels_ref[:modes]
    scaled = channels_ref[modes:] * jnp.sqrt((1.0 - jnp.exp(-2.0 * rate)) / modes)
    chosen = on_line(modes, width)
    return [
        jnp.sum(jnp.where(chosen, part, 0.0), axis=0, keepdims=True) for part in (rate, scaled)
    ]


def response_kernel(channels_ref, _, rows_ref):
    groups, block = rows_ref.shape
    modes, width = channels_ref.shape[0] // 2, channels_ref.shape[1]
    rate_line, scaled_line = modal_lines(channels_ref, modes, width)
    lag = ((block - iota((block, LANES), 0)) % block).astype(jnp.float32)
    per_slab = LANES // modes
    gather = (iota((LANES, LANES), 0) // modes == iota((LANES, LANES), 1)).astype(jnp.bfloat16)
    for slab, lanes in enumerate(slabs_of(width)):
        terms = scaled_line[:, lanes] * jnp.exp(-rate_line[:, lanes] * lag)
        high = terms.astype(jnp.bfloat16)
        low = (terms - high.astype(jnp.float32)).astype(jnp.bfloat16)
        sums = jnp.transpose(dot(high, gather) + dot(low, gather))
        rows_ref[slab * per_slab : (slab + 1) * per_slab, :] = sums[:per_slab]


def grouped(halves, values):
    rows = values.shape[0]
    half = rows // 2
    lane = iota((half, LANES), 1) // GROUP_CH
    results = []
    for part, chosen in enumerate(halves):
        turned = values if part == 0 else jnp.concatenate([values[half:], values[:half]], axis=0)
        product = dot(chosen, turned)
        result = product[:half]
        for k in range(1, chosen.shape[0] // half):
            result = jnp.where(lane == k, product[k * half : (k + 1) * half], result)
        results.append(result)
    return jnp.concatenate(results, axis=0)


def stored_halves(matrices_ref, slab):
    per_slab = LANES // GROUP_CH
    groups = slice(slab * per_slab, (slab + 1) * per_slab)
    half = matrices_ref.shape[1] // 2
    return [
        matrices_ref[groups, part * half : (part + 1) * half].reshape(per_slab * half, 2 * half)
        for part in range(2)
    ]


def gate_kernel(
    halo_ref, query_ref, previous_ref, medium_ref, end_ref, _, gated_ref, state_ref
):
    for slab, lanes in enumerate(slabs_of(halo_ref.shape[1])):
        medium = medium_ref[:, lanes] + grouped(
            stored_halves(previous_ref, slab), halo_ref[:, lanes]
        )
        gated_ref[:, lanes] = gated_by(query_ref[:, lanes], medium)
    end_states(end_ref, gated_ref, state_ref)


def local_kernel(
    gated_ref, rows_ref, same_ref, doc_ref, channels_ref, gain_ref, part_ref, carry_ref
):
    block, width = part_ref.shape
    modes = channels_ref.shape[0] // 2
    per_slab = LANES // GROUP_CH
    half = block // 2
    same = [same_ref[:half, :], same_ref[half:, :]]
    rate_line, scaled_line = modal_lines(channels_ref, modes, width)
    since = (iota((block, LANES), 0) + 1).astype(jnp.float32)
    continues = doc_ref[...] == 0.0
    for slab, lanes in enumerate(slabs_of(width)):
        turned = [
            circulant(rows_ref[group : group + 1, :], block)
            for group in range(slab * per_slab, (slab + 1) * per_slab)
        ]
        halves = [jnp.concatenate([line * mask for line in turned], axis=0) for mask in same]
        gated = gated_ref[:, lanes]
        part_ref[:, lanes] = grouped(halves, gated) + gain_ref[:, lanes] * gated.astype(jnp.float32)
        weight = scaled_line[:, lanes] * jnp.exp(-rate_line[:, lanes] * since)
        carry_ref[:, lanes] = jnp.where(continues, weight, 0.0).astype(jnp.bfloat16)


def finish_kernel(
    four, part_ref, carry_ref, first_ref, far_ref, middle_ref, near_ref, through_ref, out_hbm, out_ref, leaving
):
    width = part_ref.shape[1]
    modes = near_ref.shape[0]
    per_slab = LANES // GROUP_CH
    diagonal = iota((LANES, LANES), 0) // modes == iota((LANES, LANES), 1) // GROUP_CH
    entering = near_ref[...].astype(jnp.float32)
    if four:
        place = lax.axis_index("ctx")
        entering += through_ref[...] * far_ref[...].astype(jnp.float32)
        entering = jnp.where(place == 3, entering, 0.0)
        entering += jnp.where(place == 1, first_ref[...].astype(jnp.float32), 0.0)
        entering += jnp.where(place == 2, middle_ref[...].astype(jnp.float32), 0.0)
    copies = []
    for slab, lanes in enumerate(slabs_of(width)):
        state = jnp.concatenate([entering[:, lanes]] * per_slab, axis=0)
        spread = jnp.where(diagonal, state, 0.0).astype(jnp.bfloat16)
        out_ref[:, lanes] = (part_ref[:, lanes] + dot(carry_ref[:, lanes], spread)).astype(
            out_ref.dtype
        )
        if slab % 2 == 1:
            pair = pl.ds((slab - 1) * LANES, 2 * LANES)
            copies.append(
                pltpu.make_async_copy(
                    out_ref.at[:, pair], out_hbm.at[:, pair], leaving.at[slab // 2]
                )
            )
            copies[-1].start()
    for copy in copies:
        copy.wait()


def call(kernel, outs, *args, spaces=None, scratch=(), micros=0.3, result=pltpu.VMEM):
    spaces = spaces or [pltpu.VMEM] * len(args)
    return pl.pallas_call(
        kernel,
        out_shape=[jax.ShapeDtypeStruct(shape, dtype) for shape, dtype in outs],
        in_specs=[pl.BlockSpec(memory_space=space) for space in spaces],
        out_specs=[pl.BlockSpec(memory_space=result)] * len(outs),
        scratch_shapes=list(scratch),
        cost_estimate=pl.CostEstimate(
            flops=int(micros * 1e9), bytes_accessed=0, transcendentals=0
        ),
        compiler_params=pltpu.CompilerParams(vmem_limit_bytes=VMEM_BYTES),
    )(*args)


def shifted(array, axis, distance):
    size = lax.axis_size(axis)
    return lax.ppermute(array, axis, [(i, i + distance) for i in range(size - distance)])


def exchanged(array, axis, bit):
    return lax.ppermute(array, axis, [(i, i ^ bit) for i in range(lax.axis_size(axis))])


def cycled(array, cycle, crossing=()):
    fsdp_size, ctx_size = lax.axis_size("fsdp"), lax.axis_size("ctx")
    after = dict(zip(cycle, cycle[1:] + cycle[:1]))
    moves = []
    for core in range(fsdp_size):
        for place in range(ctx_size):
            other = (core ^ (place in crossing), after[place]) if place in after else (core ^ 1, place)
            moves.append((core * ctx_size + place, other[0] * ctx_size + other[1]))
    return lax.ppermute(array, ("fsdp", "ctx"), moves)


def entering_states(state, through):
    size = lax.axis_size("ctx")
    total, factor, distance = state.astype(jnp.float32), through, 1
    while distance < size:
        total = total + factor * shifted(total, "ctx", distance)
        factor = factor * shifted(factor, "ctx", distance)
        distance *= 2
    return shifted(total, "ctx", 1)


def body(
    query_stream,
    key_stream,
    value_stream,
    document_starts,
    medium_taps,
    modal_rate,
    modal_residue,
    skip_gain,
):
    tokens, width = query_stream.shape[1:]
    groups = width // GROUP_CH
    fsdp_size, dp_size = lax.axis_size("fsdp"), lax.axis_size("dp")
    ctx_size = lax.axis_size("ctx")
    modes = modal_rate.shape[1] * dp_size
    assert fsdp_size == 2 and tokens == medium_taps.shape[1] * fsdp_size
    assert modes == GROUP_CH and modal_rate.shape[1] <= 8
    taps = medium_taps.T
    half = jnp.bfloat16
    rows = modal_rate.shape[0]
    inputs = [
        key_stream[0],
        value_stream[0],
        modal_rate.T,
        modal_residue.T,
        query_stream[0],
        taps,
        document_starts,
        skip_gain.reshape(1, width),
    ]
    product, modal, spread, select, rates, query, own_taps, starts, gain = call(
        prepare_kernel,
        [
            ((tokens, width), half),
            ((16, rows), half),
            ((LANES, width), half),
            ((2 * modes, 16 * dp_size), half),
            ((16 * dp_size, width), jnp.float32),
        ]
        + [(a.shape, a.dtype) for a in inputs[4:]],
        *[pltpu.with_memory_space_constraint(a, pltpu.HBM) for a in inputs],
        spaces=[pltpu.HBM] * len(inputs),
        scratch=[pltpu.VMEM(a.shape, a.dtype) for a in inputs[:4]]
        + [pltpu.SemaphoreType.DMA((len(inputs),))],
    )
    halo = lax.ppermute(product, "ctx", [(i, (i + 1) % ctx_size) for i in range(ctx_size)])
    other_taps = exchanged(taps, "fsdp", 1)
    modal = [modal] + [exchanged(modal, "dp", bit) for bit in reversed(range(1, dp_size))]
    square = ((groups, tokens, tokens), half)
    previous, current, same, documents, clear = call(
        medium_kernel,
        [
            square,
            square,
            ((tokens, tokens), half),
            ((tokens, tokens), jnp.float32),
            ((2, tokens), jnp.float32),
        ],
        own_taps,
        other_taps,
        starts,
        scratch=[pltpu.VMEM((LANES, tokens), jnp.float32)],
    )
    medium, gated_own = call(
        own_kernel,
        [((tokens, width), jnp.float32), ((tokens, width), half)],
        product,
        query,
        current,
    )
    states = ((modes, width), jnp.float32)
    four = ctx_size == 4
    (state_own,) = call(
        first_kernel,
        [((modes, width), half)],
        *modal,
        spread,
        rates,
        documents,
        gated_own,
        scratch=[pltpu.VMEM((tokens, width), half)],
    )
    end, channels, through, far_through = call(
        functools.partial(modal_kernel, four),
        [((tokens, width), half), ((2 * modes, width), jnp.float32), states, states],
        *modal,
        select,
        spread,
        rates,
        documents,
        clear,
        state_own,
    )
    first = cycled(state_own, [0, 1], (1,)) if four else state_own
    (response,) = call(
        response_kernel, [((groups, tokens), jnp.float32)], channels, state_own
    )
    gated, state = call(
        gate_kernel,
        [((tokens, width), half), ((modes, width), half)],
        halo,
        query,
        previous,
        medium,
        end,
        response,
    )
    if four:
        both = state.astype(jnp.float32) + through * first.astype(jnp.float32)
        both = both.astype(half)
        near = cycled(state, [2, 3], ())
        middle = cycled(both, [1, 2], (2, ))
        far = cycled(both, [1, 3, 2], (2, ))
    else:
        near = middle = far = entering_states(state, through)
    part, carry = call(
        local_kernel,
        [((tokens, width), jnp.float32), ((tokens, width), half)],
        gated,
        response,
        same,
        documents,
        channels,
        gain,
    )
    (out,) = call(
        functools.partial(finish_kernel, four),
        [((tokens, width), half)],
        part,
        carry,
        first,
        far,
        middle,
        near,
        far_through,
        scratch=[
            pltpu.VMEM((tokens, width), half),
            pltpu.SemaphoreType.DMA((width // LANES // 2,)),
        ],
        result=pltpu.HBM,
    )
    return out[None]


def solution(mesh):
    return jax.shard_map(
        body,
        mesh=mesh,
        in_specs=(
            P(None, "ctx", ("fsdp", "dp")),
            P(None, "ctx", ("fsdp", "dp")),
            P(None, "ctx", ("fsdp", "dp")),
            P(),
            P(None, "fsdp"),
            P("fsdp", "dp"),
            P("fsdp", "dp"),
            P(("fsdp", "dp")),
        ),
        out_specs=P(None, "ctx", ("fsdp", "dp")),
        check_vma=False,
    )
```

```python
import functools

import jax
import jax.numpy as jnp
from jax import lax
from jax.experimental import pallas as pl
from jax.experimental.pallas import tpu as pltpu
from jax.sharding import PartitionSpec as P

GROUP_CH = 16
LANES = 128
VMEM_BYTES = 32 * 1024 * 1024


def iota(shape, dim):
    return lax.broadcasted_iota(jnp.int32, shape, dim)


def dot(a, b, contract=((1,), (0,))):
    return lax.dot_general(a, b, (contract, ((), ())), preferred_element_type=jnp.float32)


def prepare_kernel(
    key_hbm,
    value_hbm,
    rate_hbm,
    residue_hbm,
    query_hbm,
    taps_hbm,
    starts_hbm,
    gain_hbm,
    product_ref,
    modal_ref,
    spread_ref,
    select_ref,
    rates_ref,
    query_ref,
    taps_ref,
    starts_ref,
    gain_ref,
    key_ref,
    value_ref,
    rate_ref,
    residue_ref,
    arrived,
):
    pairs = (
        (key_hbm, key_ref),
        (value_hbm, value_ref),
        (rate_hbm, rate_ref),
        (residue_hbm, residue_ref),
        (query_hbm, query_ref),
        (taps_hbm, taps_ref),
        (starts_hbm, starts_ref),
        (gain_hbm, gain_ref),
    )
    copies = [
        pltpu.make_async_copy(source, target, arrived.at[i])
        for i, (source, target) in enumerate(pairs)
    ]
    for copy in copies:
        copy.start()
    dp_place = lax.axis_index("dp")
    modes, width = select_ref.shape[0] // 2, spread_ref.shape[1]
    per_part = rate_ref.shape[0]
    lines = select_ref.shape[1]
    pieces = lines // 16
    line, mode = iota((2 * modes, lines), 1), iota((2 * modes, lines), 0)
    within = line % 16
    held = jnp.where(mode < modes, within, within - 8)
    owner = jnp.bitwise_xor(dp_place, (pieces - line // 16) % pieces)
    wanted = owner * per_part + held == jnp.where(mode < modes, mode, mode - modes)
    select_ref[...] = ((held >= 0) & (held < per_part) & wanted).astype(jnp.bfloat16)
    line, mode = iota((lines, width), 0), iota((lines, width), 1) % modes
    within = line % 16
    owner = jnp.bitwise_xor(dp_place, (pieces - line // 16) % pieces)
    rates_ref[...] = ((within < per_part) & (owner * per_part + within == mode)).astype(
        jnp.float32
    )
    first = dp_place * (width // modes) % LANES
    spread_ref[...] = (
        iota((LANES, width), 0) == first + iota((LANES, width), 1) // modes
    ).astype(jnp.bfloat16)
    for copy in copies[:4]:
        copy.wait()
    product_ref[...] = (
        key_ref[...].astype(jnp.float32) * value_ref[...].astype(jnp.float32)
    ).astype(jnp.bfloat16)
    rate = rate_ref[...].astype(jnp.float32)
    residue = residue_ref[...].astype(jnp.float32)
    gap = jnp.zeros((8 - rate.shape[0], rate.shape[1]), jnp.float32)
    modal_ref[...] = jnp.concatenate([rate, gap, residue, gap], axis=0).astype(jnp.bfloat16)
    for copy in copies[4:]:
        copy.wait()


def block_starts(starts_ref, ctx_place, block):
    prior_place = jnp.maximum(ctx_place - 1, 0)
    return [
        starts_ref[:, pl.ds(pl.multiple_of(place * block, block), block)].astype(jnp.float32)
        for place in (ctx_place, prior_place)
    ]


def document_masks(own, prior, block):
    row, col = iota((block, block), 0), iota((block, block), 1)
    both = jnp.concatenate(
        [jnp.broadcast_to(own, (8, block)), jnp.broadcast_to(prior, (8, block))], axis=0
    ).astype(jnp.bfloat16)
    upto = (row <= col).astype(jnp.bfloat16)
    doc_row = dot(both, upto)[0:1]
    after_row = dot(both, (row > col).astype(jnp.bfloat16))[8:9]
    doc_col = dot(
        upto, jnp.broadcast_to(own, (block, block)).astype(jnp.bfloat16), ((0,), (1,))
    )
    current = (row >= col) & (doc_col == doc_row)
    previous = (col > row) & (doc_col == 0.0) & (after_row == 0.0)
    return doc_col, current, previous


def circulant(row, block):
    return pltpu.roll(
        jnp.broadcast_to(row, (block // 2, block)), 0, 1, stride=1, stride_axis=0
    ).astype(jnp.bfloat16)


def folded(mask, block):
    half = block // 2
    lower = pltpu.roll(mask[half:], half, 1)
    return [mask[:half].astype(jnp.bfloat16), lower.astype(jnp.bfloat16)]


def medium_kernel(
    taps_ref,
    other_taps_ref,
    starts_ref,
    previous_ref,
    current_ref,
    same_ref,
    doc_ref,
    clear_ref,
    rows_ref,
):
    fsdp_place, ctx_place, dp_place = (lax.axis_index(axis) for axis in ("fsdp", "ctx", "dp"))
    groups, block = previous_ref.shape[0], previous_ref.shape[1]
    half = taps_ref.shape[0]
    first = (fsdp_place * lax.axis_size("dp") + dp_place) * groups
    base = pl.multiple_of(first // LANES * LANES, LANES)
    tap, lane = iota((half, block), 0), iota((half, block), 1)
    lag_of_lane = (block - lane) % block
    own_place = (tap + fsdp_place * half == lag_of_lane).astype(jnp.bfloat16)
    other_place = (tap + (1 - fsdp_place) * half == lag_of_lane).astype(jnp.bfloat16)
    rows_ref[...] = dot(taps_ref[:, pl.ds(base, LANES)], own_place, ((0,), (0,))) + dot(
        other_taps_ref[:, pl.ds(base, LANES)], other_place, ((0,), (0,))
    )
    own, prior = block_starts(starts_ref, ctx_place, block)
    doc_col, current, previous = document_masks(own, prior, block)
    current = folded(current.astype(jnp.float32), block)
    previous = folded((previous & (ctx_place > 0)).astype(jnp.float32), block)
    halves = [slice(0, block // 2), slice(block // 2, block)]
    doc_ref[...] = doc_col
    for line, begun in enumerate((own, prior)):
        none = jnp.sum(begun, axis=1, keepdims=True) == 0.0
        clear_ref[line : line + 1, :] = jnp.where(none, jnp.ones((1, block), jnp.float32), 0.0)
    for part, rows in enumerate(halves):
        same_ref[rows, :] = current[part]
    for group in range(groups):
        turned = circulant(rows_ref[pl.ds(first - base + group, 1), :], block)
        for part, rows in enumerate(halves):
            previous_ref[group, rows, :] = turned * previous[part]
            current_ref[group, rows, :] = turned * current[part]


def slabs_of(width):
    return [slice(at, at + LANES) for at in range(0, width, LANES)]


def gated_by(query, medium):
    return (
        query.astype(jnp.float32) * medium.astype(jnp.bfloat16).astype(jnp.float32)
    ).astype(jnp.bfloat16)


def end_states(end_ref, gated_ref, state_ref):
    modes, width = state_ref.shape
    per_slab = LANES // GROUP_CH
    diagonal = iota((LANES, LANES), 0) // modes == iota((LANES, LANES), 1) // GROUP_CH
    for lanes in slabs_of(width):
        spread = jnp.where(
            diagonal, dot(end_ref[:, lanes], gated_ref[:, lanes], ((0,), (0,))), 0.0
        )
        state_ref[:, lanes] = jnp.sum(spread.reshape(per_slab, modes, LANES), axis=0).astype(
            state_ref.dtype
        )


def own_kernel(product_ref, query_ref, current_ref, medium_ref, gated_ref):
    for slab, lanes in enumerate(slabs_of(product_ref.shape[1])):
        medium = grouped(stored_halves(current_ref, slab), product_ref[:, lanes])
        medium_ref[:, lanes] = medium
        gated_ref[:, lanes] = gated_by(query_ref[:, lanes], medium)


def on_line(modes, width):
    return iota((modes, width), 0) == iota((modes, width), 1) % modes


def modal_parts(modal_refs, spread_ref, groups):
    first = lax.axis_index("dp") * groups
    base = pl.multiple_of(first // LANES * LANES, LANES)
    pieces = jnp.concatenate([ref[:, pl.ds(base, LANES)] for ref in modal_refs], axis=0)
    return dot(pieces, spread_ref[...])


def end_weights(lines, rates_ref, doc_ref, end_ref):
    block, width = end_ref.shape
    rate_line = jnp.sum(lines * rates_ref[...], axis=0, keepdims=True)
    left = (block - 1 - iota((block, LANES), 0)).astype(jnp.float32)
    keeps = doc_ref[...] == doc_ref[block - 1 : block, :]
    for lanes in slabs_of(width):
        weight = jnp.exp(-rate_line[:, lanes] * left)
        end_ref[:, lanes] = jnp.where(keeps, weight, 0.0).astype(jnp.bfloat16)


def first_kernel(*refs):
    *modal_refs, spread_ref, rates_ref, doc_ref, gated_ref, state_ref, end_ref = refs
    modes, width = state_ref.shape

    @pl.when(lax.axis_index("ctx") == 0)
    def _():
        lines = modal_parts(modal_refs, spread_ref, width // modes)
        end_weights(lines, rates_ref, doc_ref, end_ref)
        end_states(end_ref, gated_ref, state_ref)

    @pl.when(lax.axis_index("ctx") != 0)
    def _():
        state_ref[...] = jnp.zeros_like(state_ref)


def modal_kernel(four, *refs):
    *refs, end_ref, channels_ref, through_ref, far_ref = refs
    *modal_refs, select_ref, spread_ref, rates_ref, doc_ref, clear_ref, _ = refs
    modes, width = channels_ref.shape[0] // 2, channels_ref.shape[1]
    lines = modal_parts(modal_refs, spread_ref, width // modes)
    end_weights(lines, rates_ref, doc_ref, end_ref)
    by_channel = dot(select_ref[...], lines.astype(jnp.bfloat16))
    channels_ref[...] = by_channel
    wanted = (lax.axis_index("ctx") == 1).astype(jnp.float32) if four else 1.0
    for lanes in slabs_of(width):
        decay = jnp.exp(-by_channel[:modes, lanes] * end_ref.shape[0])
        through_ref[:, lanes] = decay * (clear_ref[0:1, :] * wanted)
        far_ref[:, lanes] = decay * clear_ref[1:2, :]


def modal_lines(channels_ref, modes, width):
    rate = channels_ref[:modes]
    scaled = channels_ref[modes:] * jnp.sqrt((1.0 - jnp.exp(-2.0 * rate)) / modes)
    chosen = on_line(modes, width)
    return [
        jnp.sum(jnp.where(chosen, part, 0.0), axis=0, keepdims=True) for part in (rate, scaled)
    ]


def response_kernel(channels_ref, _, rows_ref):
    groups, block = rows_ref.shape
    modes, width = channels_ref.shape[0] // 2, channels_ref.shape[1]
    rate_line, scaled_line = modal_lines(channels_ref, modes, width)
    lag = ((block - iota((block, LANES), 0)) % block).astype(jnp.float32)
    per_slab = LANES // modes
    gather = (iota((LANES, LANES), 0) // modes == iota((LANES, LANES), 1)).astype(jnp.bfloat16)
    for slab, lanes in enumerate(slabs_of(width)):
        terms = scaled_line[:, lanes] * jnp.exp(-rate_line[:, lanes] * lag)
        high = terms.astype(jnp.bfloat16)
        low = (terms - high.astype(jnp.float32)).astype(jnp.bfloat16)
        sums = jnp.transpose(dot(high, gather) + dot(low, gather))
        rows_ref[slab * per_slab : (slab + 1) * per_slab, :] = sums[:per_slab]


def grouped(halves, values):
    rows = values.shape[0]
    half = rows // 2
    lane = iota((half, LANES), 1) // GROUP_CH
    results = []
    for part, chosen in enumerate(halves):
        turned = values if part == 0 else jnp.concatenate([values[half:], values[:half]], axis=0)
        product = dot(chosen, turned)
        result = product[:half]
        for k in range(1, chosen.shape[0] // half):
            result = jnp.where(lane == k, product[k * half : (k + 1) * half], result)
        results.append(result)
    return jnp.concatenate(results, axis=0)


def stored_halves(matrices_ref, slab):
    per_slab = LANES // GROUP_CH
    groups = slice(slab * per_slab, (slab + 1) * per_slab)
    half = matrices_ref.shape[1] // 2
    return [
        matrices_ref[groups, part * half : (part + 1) * half].reshape(per_slab * half, 2 * half)
        for part in range(2)
    ]


def gate_kernel(
    halo_ref, query_ref, previous_ref, medium_ref, end_ref, _, gated_ref, state_ref
):
    for slab, lanes in enumerate(slabs_of(halo_ref.shape[1])):
        medium = medium_ref[:, lanes] + grouped(
            stored_halves(previous_ref, slab), halo_ref[:, lanes]
        )
        gated_ref[:, lanes] = gated_by(query_ref[:, lanes], medium)
    end_states(end_ref, gated_ref, state_ref)


def local_kernel(
    gated_ref, rows_ref, same_ref, doc_ref, channels_ref, gain_ref, part_ref, carry_ref
):
    block, width = part_ref.shape
    modes = channels_ref.shape[0] // 2
    per_slab = LANES // GROUP_CH
    half = block // 2
    same = [same_ref[:half, :], same_ref[half:, :]]
    rate_line, scaled_line = modal_lines(channels_ref, modes, width)
    since = (iota((block, LANES), 0) + 1).astype(jnp.float32)
    continues = doc_ref[...] == 0.0
    for slab, lanes in enumerate(slabs_of(width)):
        turned = [
            circulant(rows_ref[group : group + 1, :], block)
            for group in range(slab * per_slab, (slab + 1) * per_slab)
        ]
        halves = [jnp.concatenate([line * mask for line in turned], axis=0) for mask in same]
        gated = gated_ref[:, lanes]
        part_ref[:, lanes] = grouped(halves, gated) + gain_ref[:, lanes] * gated.astype(jnp.float32)
        weight = scaled_line[:, lanes] * jnp.exp(-rate_line[:, lanes] * since)
        carry_ref[:, lanes] = jnp.where(continues, weight, 0.0).astype(jnp.bfloat16)


def finish_kernel(
    four, part_ref, carry_ref, first_ref, far_ref, middle_ref, near_ref, through_ref, out_ref
):
    width = part_ref.shape[1]
    modes = near_ref.shape[0]
    per_slab = LANES // GROUP_CH
    diagonal = iota((LANES, LANES), 0) // modes == iota((LANES, LANES), 1) // GROUP_CH
    entering = near_ref[...].astype(jnp.float32)
    if four:
        place = lax.axis_index("ctx")
        entering += through_ref[...] * far_ref[...].astype(jnp.float32)
        entering = jnp.where(place == 3, entering, 0.0)
        entering += jnp.where(place == 1, first_ref[...].astype(jnp.float32), 0.0)
        entering += jnp.where(place == 2, middle_ref[...].astype(jnp.float32), 0.0)
    for slab in range(width // LANES):
        lanes = slice(slab * LANES, (slab + 1) * LANES)
        state = jnp.concatenate([entering[:, lanes]] * per_slab, axis=0)
        spread = jnp.where(diagonal, state, 0.0).astype(jnp.bfloat16)
        out_ref[:, lanes] = (part_ref[:, lanes] + dot(carry_ref[:, lanes], spread)).astype(
            out_ref.dtype
        )


def call(kernel, outs, *args, spaces=None, scratch=(), micros=0.3):
    spaces = spaces or [pltpu.VMEM] * len(args)
    return pl.pallas_call(
        kernel,
        out_shape=[jax.ShapeDtypeStruct(shape, dtype) for shape, dtype in outs],
        in_specs=[pl.BlockSpec(memory_space=space) for space in spaces],
        out_specs=[pl.BlockSpec(memory_space=pltpu.VMEM)] * len(outs),
        scratch_shapes=list(scratch),
        cost_estimate=pl.CostEstimate(
            flops=int(micros * 1e9), bytes_accessed=0, transcendentals=0
        ),
        compiler_params=pltpu.CompilerParams(vmem_limit_bytes=VMEM_BYTES),
    )(*args)


def shifted(array, axis, distance):
    size = lax.axis_size(axis)
    return lax.ppermute(array, axis, [(i, i + distance) for i in range(size - distance)])


def exchanged(array, axis, bit):
    return lax.ppermute(array, axis, [(i, i ^ bit) for i in range(lax.axis_size(axis))])


def cycled(array, cycle, crossing=()):
    fsdp_size, ctx_size = lax.axis_size("fsdp"), lax.axis_size("ctx")
    after = dict(zip(cycle, cycle[1:] + cycle[:1]))
    moves = []
    for core in range(fsdp_size):
        for place in range(ctx_size):
            other = (core ^ (place in crossing), after[place]) if place in after else (core ^ 1, place)
            moves.append((core * ctx_size + place, other[0] * ctx_size + other[1]))
    return lax.ppermute(array, ("fsdp", "ctx"), moves)


def entering_states(state, through):
    size = lax.axis_size("ctx")
    total, factor, distance = state.astype(jnp.float32), through, 1
    while distance < size:
        total = total + factor * shifted(total, "ctx", distance)
        factor = factor * shifted(factor, "ctx", distance)
        distance *= 2
    return shifted(total, "ctx", 1)


def body(
    query_stream,
    key_stream,
    value_stream,
    document_starts,
    medium_taps,
    modal_rate,
    modal_residue,
    skip_gain,
):
    tokens, width = query_stream.shape[1:]
    groups = width // GROUP_CH
    fsdp_size, dp_size = lax.axis_size("fsdp"), lax.axis_size("dp")
    ctx_size = lax.axis_size("ctx")
    modes = modal_rate.shape[1] * dp_size
    assert fsdp_size == 2 and tokens == medium_taps.shape[1] * fsdp_size
    assert modes == GROUP_CH and modal_rate.shape[1] <= 8
    taps = medium_taps.T
    half = jnp.bfloat16
    rows = modal_rate.shape[0]
    inputs = [
        key_stream[0],
        value_stream[0],
        modal_rate.T,
        modal_residue.T,
        query_stream[0],
        taps,
        document_starts,
        skip_gain.reshape(1, width),
    ]
    product, modal, spread, select, rates, query, own_taps, starts, gain = call(
        prepare_kernel,
        [
            ((tokens, width), half),
            ((16, rows), half),
            ((LANES, width), half),
            ((2 * modes, 16 * dp_size), half),
            ((16 * dp_size, width), jnp.float32),
        ]
        + [(a.shape, a.dtype) for a in inputs[4:]],
        *[pltpu.with_memory_space_constraint(a, pltpu.HBM) for a in inputs],
        spaces=[pltpu.HBM] * len(inputs),
        scratch=[pltpu.VMEM(a.shape, a.dtype) for a in inputs[:4]]
        + [pltpu.SemaphoreType.DMA((len(inputs),))],
    )
    halo = lax.ppermute(product, "ctx", [(i, (i + 1) % ctx_size) for i in range(ctx_size)])
    other_taps = exchanged(taps, "fsdp", 1)
    modal = [modal] + [exchanged(modal, "dp", bit) for bit in reversed(range(1, dp_size))]
    square = ((groups, tokens, tokens), half)
    previous, current, same, documents, clear = call(
        medium_kernel,
        [
            square,
            square,
            ((tokens, tokens), half),
            ((tokens, tokens), jnp.float32),
            ((2, tokens), jnp.float32),
        ],
        own_taps,
        other_taps,
        starts,
        scratch=[pltpu.VMEM((LANES, tokens), jnp.float32)],
    )
    medium, gated_own = call(
        own_kernel,
        [((tokens, width), jnp.float32), ((tokens, width), half)],
        product,
        query,
        current,
    )
    states = ((modes, width), jnp.float32)
    four = ctx_size == 4
    (state_own,) = call(
        first_kernel,
        [((modes, width), half)],
        *modal,
        spread,
        rates,
        documents,
        gated_own,
        scratch=[pltpu.VMEM((tokens, width), half)],
    )
    end, channels, through, far_through = call(
        functools.partial(modal_kernel, four),
        [((tokens, width), half), ((2 * modes, width), jnp.float32), states, states],
        *modal,
        select,
        spread,
        rates,
        documents,
        clear,
        state_own,
    )
    first = cycled(state_own, [0, 1], (1,)) if four else state_own
    (response,) = call(
        response_kernel, [((groups, tokens), jnp.float32)], channels, state_own
    )
    gated, state = call(
        gate_kernel,
        [((tokens, width), half), ((modes, width), half)],
        halo,
        query,
        previous,
        medium,
        end,
        response,
    )
    if four:
        both = state.astype(jnp.float32) + through * first.astype(jnp.float32)
        both = both.astype(half)
        near = cycled(state, [2, 3], ())
        middle = cycled(both, [1, 2], (2, ))
        far = cycled(both, [1, 3, 2], (2, 3))
    else:
        near = middle = far = entering_states(state, through)
    part, carry = call(
        local_kernel,
        [((tokens, width), jnp.float32), ((tokens, width), half)],
        gated,
        response,
        same,
        documents,
        channels,
        gain,
    )
    (out,) = call(
        functools.partial(finish_kernel, four),
        [((tokens, width), half)],
        part,
        carry,
        first,
        far,
        middle,
        near,
        far_through,
    )
    return out[None]


def solution(mesh):
    return jax.shard_map(
        body,
        mesh=mesh,
        in_specs=(
            P(None, "ctx", ("fsdp", "dp")),
            P(None, "ctx", ("fsdp", "dp")),
            P(None, "ctx", ("fsdp", "dp")),
            P(),
            P(None, "fsdp"),
            P("fsdp", "dp"),
            P("fsdp", "dp"),
            P(("fsdp", "dp")),
        ),
        out_specs=P(None, "ctx", ("fsdp", "dp")),
        check_vma=False,
    )
```
